32 devices in a mesh: dp: 16 (over z, y, core), tensor: 2 (over x).
Axes of the slice: x: 2, y: 2, z: 4, core: 2. Of those that a mesh axis runs over, the one named last changes fastest.
Arguments:
- tokens: bfloat16 [8192, 1024], P(('dp', 'tensor')), may hold values from -6 to 6
- cotangent: bfloat16 [8192, 1024], P(('dp', 'tensor')), may hold values from -6 to 6
- segment_ids: int32 [8192], P('dp'), may hold values from 0 to 63, never falling along the last dimension, each value on 1 to 512 neighbouring positions
- w_query: bfloat16 [2, 1024, 1024], P(None, 'dp', 'tensor'), may hold values from -0.1875 to 0.1875
- w_key: bfloat16 [2, 1024, 1024], P(None, 'dp', 'tensor'), may hold values from -0.1875 to 0.1875
- w_value: bfloat16 [2, 1024, 1024], P(None, 'dp', 'tensor'), may hold values from -0.1875 to 0.1875
- w_out: bfloat16 [2, 1024, 1024], P(None, ('tensor', 'dp')), may hold values from -0.75 to 0.75
- w_up: bfloat16 [2, 1024, 4096], P(None, 'dp', 'tensor'), may hold values from -0.1875 to 0.1875
- w_down: bfloat16 [2, 4096, 1024], P(None, ('tensor', 'dp')), may hold values from -0.09375 to 0.09375
- qv_bias: bfloat16 [2, 2, 1024], P(None, None, ('tensor', 'dp')), may hold values from -3 to 3
- up_bias: bfloat16 [2, 4096], P(None, ('tensor', 'dp')), may hold values from -3 to 3
- norm_gain: float32 [2, 2, 1024], P(None, None, ('dp', 'tensor')), may hold values from 0.5 to 1.5
- shift_bias: float32 [2, 4, 1024], P(None, None, ('dp', 'tensor')), may hold values from -2 to 2
Outputs:
- output: float32 [8192, 1024], P(('dp', 'tensor'))
- input_grad: float32 [8192, 1024], P(('dp', 'tensor'))
- grad_query: float32 [2, 1024, 1024], P(None, 'dp', 'tensor')
- grad_key: float32 [2, 1024, 1024], P(None, 'dp', 'tensor')
- grad_value: float32 [2, 1024, 1024], P(None, 'dp', 'tensor')
- grad_out: float32 [2, 1024, 1024], P(None, ('tensor', 'dp'))
- grad_up: float32 [2, 1024, 4096], P(None, 'dp', 'tensor')
- grad_down: float32 [2, 4096, 1024], P(None, ('tensor', 'dp'))
- grad_qv_bias: float32 [2, 2, 1024], P(None, None, ('tensor', 'dp'))
- grad_up_bias: float32 [2, 4096], P(None, ('tensor', 'dp'))
- grad_gain: float32 [2, 2, 1024], P(None, None, ('dp', 'tensor'))
- grad_shift: float32 [2, 4, 1024], P(None, None, ('dp', 'tensor'))
The draws below stay inside these ranges and needn't reach their ends.
Inputs may be any that keep to these rules, and one draw needn't show every extreme that they name: segment_ids never fall along the tokens; every number from 0 up is some token's document, and one document has exactly 512 tokens.
All inputs are finite; a program needn't handle non-finite values.
Results may differ from the reference program's by a relative error of at most 0.034.
Values may be sent and summed in bfloat16 or wider, within the bound.
A program may use at most 192 MiB of HBM per device.

```python
import math
import jax
import jax.numpy as jnp
import numpy as np
from jax import lax

D = 1024
HEADS = 16
HEAD = 64
FF = 4096
LAYERS = 2
SEQ_LEN = 512
TOKENS = 8192


def levels(stream_key, extent, pieces, low, top_value):
    loudness, own = 1.0, jax.random.fold_in(stream_key, 6)
    for axis_at, parts in pieces:
        steps = jnp.exp(jax.random.uniform(jax.random.fold_in(own, axis_at), (parts,), jnp.float32, low / len(pieces), top_value / len(pieces)))
        loudness = loudness * jnp.repeat(steps, extent[axis_at] // parts).reshape([-1 if axis == axis_at else 1 for axis in range(len(extent))])
    return loudness


def length_profile(number_of, total, most, skew):
    loads = [(1 << 20) // math.isqrt(grade ** skew) + 1 for grade in range(2, number_of + 1)]
    spare, given = total - most - (number_of - 1), [1] * (number_of - 1)
    while spare > 0:
        movable = [i for i in range(number_of - 1) if given[i] < most]
        mass, remaining = sum([loads[i] for i in movable]), spare
        for i in movable:
            more = min(most - given[i], max(1, remaining * loads[i] // mass), spare)
            given[i] = given[i] + more
            spare = spare - more
    return np.array([most] + given)


def ragged(own_key, number_of, total, limit, lean):
    if number_of == 2:
        one = jax.random.randint(own_key, (), max(1, total - limit), min(limit, total - 1) + 1)
        return jnp.stack([one, total - one])
    tallies = jnp.asarray(length_profile(number_of, total, limit, lean), jnp.int32)
    pairs = (number_of - 1) // 2
    donor, taker = tallies[1:1 + 2 * pairs:2], tallies[2:2 + 2 * pairs:2]
    margin = jnp.minimum(donor - 1, limit - taker)
    passed = jax.random.randint(jax.random.fold_in(own_key, 1), (pairs,), 0, 1 << 20) % (margin + 1)
    tallies = tallies.at[1:1 + 2 * pairs:2].set(donor - passed).at[2:2 + 2 * pairs:2].set(taker + passed)
    return tallies[jax.random.permutation(jax.random.fold_in(own_key, 2), number_of)]


def noise(rng, shape, width, reach, cuts=(), held_as=jnp.bfloat16):
    array = width * jax.random.normal(rng, shape, jnp.float32)
    if cuts:
        array = array * levels(rng, shape, cuts, -0.22, 0.18)
    return jnp.clip(array, -reach, reach).astype(held_as)


def setup_inputs(seed: int = 0) -> dict:
    seeds = jax.random.split(jax.random.key(seed), 14)
    tokens = noise(seeds[0], (TOKENS, D), 1.0, 6.0, ((0, 32),))
    cotangent = noise(seeds[1], (TOKENS, D), 1.0, 6.0, ((0, 32),))
    segment_ids = jnp.searchsorted(jnp.cumsum(ragged(seeds[2], 4 * TOKENS // SEQ_LEN, TOKENS, SEQ_LEN, 2)), jnp.arange(TOKENS), side="right").astype(jnp.int32)
    w_query = noise(seeds[3], (LAYERS, D, D), D ** -0.5, 0.1875, ((1, 16), (2, 2)))
    w_key = noise(seeds[4], (LAYERS, D, D), D ** -0.5, 0.1875, ((1, 16), (2, 2)))
    w_value = noise(seeds[5], (LAYERS, D, D), D ** -0.5, 0.1875, ((1, 16), (2, 2)))
    w_out = noise(seeds[6], (LAYERS, D, D), (D // 16) ** -0.5, 0.75, ((1, 32),))
    w_up = noise(seeds[7], (LAYERS, D, FF), D ** -0.5, 0.1875, ((1, 16), (2, 2)))
    w_down = noise(seeds[8], (LAYERS, FF, D), FF ** -0.5, 0.09375, ((1, 32),))
    qv_bias = noise(seeds[9], (LAYERS, 2, D), 0.5, 3.0, ((2, 32),))
    up_bias = noise(seeds[10], (LAYERS, FF), 0.5, 3.0, ((1, 32),))
    norm_gain = jnp.clip(1.0 + 0.1 * jax.random.normal(seeds[11], (LAYERS, 2, D), jnp.float32), 0.5, 1.5)
    shift_bias = noise(seeds[12], (LAYERS, 4, D), 0.3, 2.0, ((2, 32),), jnp.float32)
    return dict(tokens=tokens, cotangent=cotangent, segment_ids=segment_ids, w_query=w_query, w_key=w_key, w_value=w_value, w_out=w_out, w_up=w_up, w_down=w_down, qv_bias=qv_bias, up_bias=up_bias, norm_gain=norm_gain, shift_bias=shift_bias)


HI = lax.Precision.HIGHEST
EPS = 1e-06
NEG = -1e+30

@jax.custom_vjp
def low(v):
    return lax.optimization_barrier(v.astype(jnp.bfloat16)).astype(jnp.float32)

@jax.custom_vjp
def low_back(v):
    return v

def low_keep(v):
    return (low(v), None)

def low_pass(kept, grad):
    return (grad,)

def back_keep(v):
    return (v, None)

def back_low(kept, grad):
    return (low(grad),)
low.defvjp(low_keep, low_pass)
low_back.defvjp(back_keep, back_low)

def layer_norm(z, gain, shift):
    mean = lax.optimization_barrier(jnp.mean(z, axis=-1, keepdims=True))
    cent = z - mean
    var = lax.optimization_barrier(jnp.mean(cent * cent, axis=-1, keepdims=True))
    return cent * lax.rsqrt(var + EPS) * gain + shift

def matmul(left, right):
    return jnp.dot(left, right, precision=HI)

def reference(tokens, cotangent, segment_ids, w_query, w_key, w_value, w_out, w_up, w_down, qv_bias, up_bias, norm_gain, shift_bias):
    seqs = TOKENS // SEQ_LEN
    bunch = math.gcd(seqs, max(1, 4096 // SEQ_LEN))
    scale = HEAD ** (-0.5)
    segs = segment_ids.reshape(seqs // bunch, bunch, SEQ_LEN)

    def block(args):
        qb, kb, vb, sb = args
        same = sb[:, :, None] == sb[:, None, :]
        scores = jnp.einsum('gqhd,gkhd->ghqk', qb, kb, precision=HI) * scale
        scores = low_back(jnp.where(same[:, None], scores, NEG))
        probs = low(jax.nn.softmax(scores, axis=-1))
        return jnp.einsum('ghqk,gkhd->gqhd', probs, vb, precision=HI)

    def attend(query, key, value):
        shape = (seqs // bunch, bunch, SEQ_LEN, HEADS, HEAD)
        result = lax.map(jax.checkpoint(block), (query.reshape(shape), key.reshape(shape), value.reshape(shape), segs))
        return result.reshape(TOKENS, D)

    def forward(stream, wq, wk, wv, wo, wu, wd, qvb, ub, gains, shifts):
        for layer in range(LAYERS):
            xb = low(stream)
            query = low(low_back(matmul(xb, wq[layer]) + qvb[layer, 0]))
            key = low(low_back(matmul(xb, wk[layer])))
            value = low(low_back(matmul(xb, wv[layer]) + qvb[layer, 1]))
            attended = low(low_back(attend(query, key, value)))
            mixed = stream + low_back(matmul(attended, wo[layer])) + shifts[layer, 0]
            normed = layer_norm(mixed, gains[layer, 0], shifts[layer, 1])
            pre = low_back(matmul(low(normed), wu[layer]) + ub[layer])
            hidden = low(jax.nn.gelu(pre, approximate=False))
            second = normed + low_back(matmul(hidden, wd[layer])) + shifts[layer, 2]
            stream = layer_norm(second, gains[layer, 1], shifts[layer, 3])
        return stream
    params = (w_query, w_key, w_value, w_out, w_up, w_down, qv_bias, up_bias, norm_gain, shift_bias)
    params = tuple((p.astype(jnp.float32) for p in params))
    output, pull = jax.vjp(forward, tokens.astype(jnp.float32), *params)
    grads = pull(cotangent.astype(jnp.float32))
    return (output, grads[0], grads[1], grads[2], grads[3], grads[4], grads[5], grads[6], grads[7], grads[8], grads[9], grads[10])
```

```python
import functools
import math

import jax
import jax.numpy as jnp
from jax import lax
from jax.experimental import pallas as pl
from jax.experimental.pallas import tpu as pltpu
from jax.sharding import PartitionSpec as P

HEAD = 64
LEN = 512


EPS = 1e-06
NEG = -1e30


def layer_norm(z, gain, shift):
    mean = jnp.mean(z, axis=-1, keepdims=True)
    cent = z - mean
    var = jnp.mean(cent * cent, axis=-1, keepdims=True)
    return cent * lax.rsqrt(var + EPS) * gain + shift


def gelu_exact(pre):
    return jax.nn.gelu(pre, approximate=False)


def inner(left, right):
    return lax.dot_general(
        left, right, (((0,), (0,)), ((), ())), preferred_element_type=jnp.float32
    )


def times_back(left, right):
    return lax.dot_general(
        left, right, (((1,), (1,)), ((), ())), preferred_element_type=jnp.float32
    )


def gather_rows(rows):
    return lax.all_gather(rows, "tensor", axis=0, tiled=True)


def gather_grads(rows):
    return lax.all_gather(rows, "tensor", axis=0, tiled=True)


def sum_rows(term, rows):
    return lax.psum_scatter(
        term(jnp.int32(0), lax.axis_size("tensor") * rows).astype(jnp.bfloat16),
        "tensor",
        scatter_dimension=0,
        tiled=True,
    ).astype(jnp.float32)


def sum_grads(term, rows):
    return lax.psum_scatter(
        term(jnp.int32(0), lax.axis_size("tensor") * rows).astype(jnp.bfloat16),
        "tensor",
        scatter_dimension=0,
        tiled=True,
    ).astype(jnp.float32)


def allowed(segment):
    return segment[:, None] == segment[None, :]


def attend_one(args):
    query, key, value, segment = args
    scale = HEAD ** (-0.5)
    scores = jnp.einsum("qhd,khd->hqk", query, key, preferred_element_type=jnp.float32) * scale
    scores = jnp.where(allowed(segment)[None], scores, NEG)
    top = jnp.max(scores, axis=-1, keepdims=True)
    total = top + jnp.log(jnp.sum(jnp.exp(scores - top), axis=-1, keepdims=True))
    probs = jnp.exp(scores - total).astype(jnp.bfloat16)
    result = jnp.einsum("hqk,khd->qhd", probs, value, preferred_element_type=jnp.float32)
    return (result.astype(jnp.bfloat16), total[..., 0])


def attend_back(args):
    query, key, value, segment, total, d_att = args
    scale = HEAD ** (-0.5)
    scores = jnp.einsum("qhd,khd->hqk", query, key, preferred_element_type=jnp.float32) * scale
    scores = jnp.where(allowed(segment)[None], scores, NEG)
    probs = jnp.exp(scores - total[..., None])
    d_probs = jnp.einsum("qhd,khd->hqk", d_att, value, preferred_element_type=jnp.float32)
    row_dot = jnp.sum(d_probs * probs, axis=-1, keepdims=True)
    d_scores = (probs * (d_probs - row_dot)).astype(jnp.bfloat16)
    d_query = (
        jnp.einsum("hqk,khd->qhd", d_scores, key, preferred_element_type=jnp.float32) * scale
    ).astype(jnp.bfloat16)
    d_key = (
        jnp.einsum("hqk,qhd->khd", d_scores, query, preferred_element_type=jnp.float32) * scale
    ).astype(jnp.bfloat16)
    d_value = jnp.einsum(
        "hqk,qhd->khd", probs.astype(jnp.bfloat16), d_att, preferred_element_type=jnp.float32
    ).astype(jnp.bfloat16)
    return (d_query, d_key, d_value)


def forward_layer(stream, mats, vecs, segs, seq):
    w_q, w_k, w_v, w_o, w_u, w_d, qvb, upb = mats
    gains, shifts = vecs
    seqs = segs.shape[0]
    rows = stream.shape[0]
    x_rows = gather_rows(stream.astype(jnp.bfloat16))
    query = (
        jnp.dot(x_rows, w_q, preferred_element_type=jnp.float32) + qvb[0].astype(jnp.float32)
    ).astype(jnp.bfloat16)
    key = jnp.dot(x_rows, w_k, preferred_element_type=jnp.float32).astype(jnp.bfloat16)
    value = (
        jnp.dot(x_rows, w_v, preferred_element_type=jnp.float32) + qvb[1].astype(jnp.float32)
    ).astype(jnp.bfloat16)
    width = query.shape[1]
    local_heads = width // HEAD

    def split(matrix):
        return matrix.reshape(seqs, seq, local_heads, HEAD)

    attended, totals = lax.map(attend_one, (split(query), split(key), split(value), segs))
    attended = attended.reshape(seqs * seq, width)

    def out_term(start, count):
        return jnp.dot(attended, w_o, preferred_element_type=jnp.float32)

    out_sum = sum_rows(out_term, rows)
    mixed = stream + out_sum + shifts[0]
    normed = layer_norm(mixed, gains[0], shifts[1])
    n_rows = gather_rows(normed.astype(jnp.bfloat16))
    pre = jnp.dot(n_rows, w_u, preferred_element_type=jnp.float32) + upb.astype(jnp.float32)
    hidden = gelu_exact(pre).astype(jnp.bfloat16)

    def down_term(start, count):
        return jnp.dot(hidden, w_d, preferred_element_type=jnp.float32)

    down_sum = sum_rows(down_term, rows)
    second = normed + down_sum + shifts[2]
    result = layer_norm(second, gains[1], shifts[3])
    kept = (x_rows, query, key, value, attended, totals, mixed, n_rows, pre, hidden, second)
    return (result, kept)


def backward_layer_any(grad, mats, vecs, kept, segs, seq):
    w_q, w_k, w_v, w_o, w_u, w_d, qvb, upb = mats
    gains, shifts = vecs
    x_rows, query, key, value, attended, totals, mixed, n_rows, pre, hidden, second = kept
    seqs = segs.shape[0]
    rows = grad.shape[0]
    width = query.shape[1]
    local_heads = width // HEAD

    def split(matrix):
        return matrix.reshape(seqs, seq, local_heads, HEAD)

    _, pull_second = jax.vjp(layer_norm, second, gains[1], shifts[3])
    d_second, d_gain_two, d_shift_two = pull_second(grad)
    d_down_bias = jnp.sum(d_second, axis=0)
    d_f = gather_grads(d_second.astype(jnp.bfloat16))
    grad_down = inner(hidden, d_f)
    d_hidden = times_back(d_f, w_d)
    _, pull_gelu = jax.vjp(gelu_exact, pre)
    d_pre = pull_gelu(d_hidden)[0].astype(jnp.bfloat16)
    grad_up = inner(n_rows, d_pre)
    d_up_bias = jnp.sum(d_pre.astype(jnp.float32), axis=0)

    def up_term(start, count):
        return times_back(d_pre, w_u)

    d_normed = d_second + sum_grads(up_term, rows)
    _, pull_first = jax.vjp(layer_norm, mixed, gains[0], shifts[1])
    d_mixed, d_gain_one, d_shift_one = pull_first(d_normed)
    d_out_bias = jnp.sum(d_mixed, axis=0)
    d_a = gather_grads(d_mixed.astype(jnp.bfloat16))
    grad_out = inner(attended, d_a)
    d_att = times_back(d_a, w_o).astype(jnp.bfloat16)
    d_query, d_key, d_value = lax.map(
        attend_back, (split(query), split(key), split(value), segs, totals, split(d_att))
    )
    d_query = d_query.reshape(seqs * seq, width)
    d_key = d_key.reshape(seqs * seq, width)
    d_value = d_value.reshape(seqs * seq, width)
    grad_q = inner(x_rows, d_query)
    grad_k = inner(x_rows, d_key)
    grad_v = inner(x_rows, d_value)
    d_qv = jnp.stack(
        [jnp.sum(d_query.astype(jnp.float32), axis=0), jnp.sum(d_value.astype(jnp.float32), axis=0)]
    )

    def in_term(start, count):
        part = times_back(d_query, w_q)
        part = part + times_back(d_key, w_k)
        return part + times_back(d_value, w_v)

    d_stream = d_mixed + sum_grads(in_term, rows)
    mat_grads = (grad_q, grad_k, grad_v, grad_out, grad_up, grad_down, d_qv, d_up_bias)
    vec_grads = (
        jnp.stack([d_gain_one, d_gain_two]),
        jnp.stack([d_out_bias, d_shift_one, d_down_bias, d_shift_two]),
    )
    return (d_stream, mat_grads, vec_grads)


def backward_layer(grad, mats, vecs, kept, segs, seq):
    w_q, w_k, w_v, w_o, w_u, w_d, qvb, upb = mats
    gains, shifts = vecs
    x_rows, query, key, value, attended, totals, mixed, n_rows, pre, hidden, second = kept
    seqs = segs.shape[0]
    rows = grad.shape[0]
    width = query.shape[1]
    local_heads = width // HEAD

    def split(matrix):
        return matrix.reshape(seqs, seq, local_heads, HEAD)

    _, pull_second = jax.vjp(layer_norm, second, gains[1], shifts[3])
    d_second, d_gain_two, d_shift_two = pull_second(grad)
    d_down_bias = jnp.sum(d_second, axis=0)
    d_f = gather_grads(d_second.astype(jnp.bfloat16))
    grad_down = inner(hidden, d_f)
    d_hidden = times_back(d_f, w_d)
    d_pre = (d_hidden * pre.astype(jnp.float32)).astype(jnp.bfloat16)
    grad_up = inner(n_rows, d_pre)
    d_up_bias = jnp.sum(d_pre.astype(jnp.float32), axis=0)

    def up_term(start, count):
        return times_back(d_pre, w_u)

    d_normed = d_second + sum_grads(up_term, rows)
    _, pull_first = jax.vjp(layer_norm, mixed, gains[0], shifts[1])
    d_mixed, d_gain_one, d_shift_one = pull_first(d_normed)
    d_out_bias = jnp.sum(d_mixed, axis=0)
    d_a = gather_grads(d_mixed.astype(jnp.bfloat16))
    grad_out = inner(attended, d_a)
    d_att = times_back(d_a, w_o).astype(jnp.bfloat16)
    d_query, d_key, d_value = lax.map(
        attend_back, (split(query), split(key), split(value), segs, totals, split(d_att))
    )
    d_query = d_query.reshape(seqs * seq, width)
    d_key = d_key.reshape(seqs * seq, width)
    d_value = d_value.reshape(seqs * seq, width)
    grad_q = inner(x_rows, d_query)
    grad_k = inner(x_rows, d_key)
    grad_v = inner(x_rows, d_value)
    d_qv = jnp.stack(
        [jnp.sum(d_query.astype(jnp.float32), axis=0), jnp.sum(d_value.astype(jnp.float32), axis=0)]
    )

    def in_term(start, count):
        part = times_back(d_query, w_q)
        part = part + times_back(d_key, w_k)
        return part + times_back(d_value, w_v)

    d_stream = d_mixed + sum_grads(in_term, rows)
    mat_grads = (grad_q, grad_k, grad_v, grad_out, grad_up, grad_down, d_qv, d_up_bias)
    vec_grads = (
        jnp.stack([d_gain_one, d_gain_two]),
        jnp.stack([d_out_bias, d_shift_one, d_down_bias, d_shift_two]),
    )
    return (d_stream, mat_grads, vec_grads)


MESH = pl.DeviceIdType.MESH
BF = jnp.bfloat16
F32 = jnp.float32
CH = 12


def nt(left, right):
    return lax.dot_general(left, right, (((1,), (1,)), ((), ())), preferred_element_type=F32)


def nn(left, right):
    return lax.dot_general(left, right, (((1,), (0,)), ((), ())), preferred_element_type=F32)


def tn(left, right):
    return lax.dot_general(left, right, (((0,), (0,)), ((), ())), preferred_element_type=F32)


def remote(src, dst, send_sem, recv_sem, device):
    return pltpu.make_async_remote_copy(
        src_ref=src, dst_ref=dst, send_sem=send_sem, recv_sem=recv_sem, device_id=device, device_id_type=MESH
    )


class Place:
    def __init__(self, depth):
        self.depth = depth
        self.dp = lax.axis_index("dp")
        self.x = lax.axis_index("tensor")
        self.z = self.dp // 4
        self.y = (self.dp // 2) % 2
        self.c = self.dp % 2

    def at(self, z, y, c):
        return {"dp": z * 4 + y * 2 + c, "tensor": self.x}

    def far(self, step):
        return self.at((self.z + step) % self.depth, self.y, self.c)

    def before(self, step):
        return (self.z + self.depth - step) % self.depth

    @property
    def side(self):
        return self.at(self.z, 1 - self.y, self.c)

    @property
    def twin(self):
        return self.at(self.z, self.y, 1 - self.c)

    @property
    def peer(self):
        return {"dp": self.dp, "tensor": 1 - self.x}

    def greet(self):
        barrier = pltpu.get_barrier_semaphore()
        partners = [self.far(i) for i in range(1, self.depth)] + [self.side, self.twin, self.peer]
        for device in partners:
            pl.semaphore_signal(barrier, inc=1, device_id=device, device_id_type=MESH)
        pl.semaphore_wait(barrier, len(partners))


class Gather:
    def __init__(self, place, wp, wg, send, recv, total):
        self.p, self.wp, self.wg, self.send, self.recv, self.total = place, wp, wg, send, recv, total
        self.view = wg.reshape(wg.shape[0], place.depth, 2, 2, *wg.shape[2:])
        self.time = 0
        self.have = 0

    def far(self, k, i):
        p = self.p
        return remote(self.wp.at[k], self.wg.at[k, p.dp], self.send.at[k, i - 1], self.recv.at[k, i - 1], p.far(i))

    def far_in(self, k, i):
        p = self.p
        ref = self.wg.at[k, p.before(i) * 4 + p.y * 2 + p.c]
        return remote(ref, ref, self.send.at[k, i - 1], self.recv.at[k, i - 1], p.far(i))

    def side(self, k, y):
        p, d = self.p, self.p.depth - 1
        ref = self.view.at[k, :, y, p.c]
        return remote(ref, ref, self.send.at[k, d], self.recv.at[k, d], p.side)

    def twin(self, k, c):
        p, d = self.p, self.p.depth
        ref = self.view.at[k, :, :, c]
        return remote(ref, ref, self.send.at[k, d], self.recv.at[k, d], p.twin)

    def begin(self, ahead):
        self.ahead = ahead
        for k in range(ahead):
            for i in range(1, self.p.depth):
                self.far(k, i).start()

    def tick(self):
        t, n = self.time, self.total
        if t >= n + 3:
            return
        if t + self.ahead < n:
            for i in range(1, self.p.depth):
                self.far(t + self.ahead, i).start()
        if t < n:
            for i in range(1, self.p.depth):
                self.far_in(t, i).wait_recv()
            self.side(t, self.p.y).start()
        if 1 <= t <= n:
            self.side(t - 1, 1 - self.p.y).wait_recv()
            self.twin(t - 1, self.p.c).start()
        if t >= 2 and t - 2 < n:
            self.twin(t - 2, 1 - self.p.c).wait_recv()
            self.have = t - 1
        self.time += 1

    def until(self, count):
        while self.have < count:
            self.tick()

    def finish(self):
        self.until(self.total)
        for k in range(self.total):
            for i in range(1, self.p.depth):
                self.far(k, i).wait_send()
            self.side(k, self.p.y).wait_send()
            self.twin(k, self.p.c).wait_send()


def norm_rows(z, gain, shift):
    mean = jnp.mean(z, axis=-1, keepdims=True)
    cent = z - mean
    var = jnp.mean(cent * cent, axis=-1, keepdims=True)
    return cent * lax.rsqrt(var + EPS) * gain + shift


def fwd_kernel(depth, layers, wp, vp, tok, segc, segr,
               wg, vec_o, out_o, xg_o, qkv_o, att_o, lse_o, mix_o, ng_o, hid_o, gp_o, sec_o,
               vg, vec, stream, normed, bias, work, prob, xg, qkv, att, lse, mix, ng, hid, gp, sec, sbuf, rbuf,
               wqkv, wo, wu, wd,
               w_send, w_recv, v_send, v_recv, x_send, x_recv, l_sem, o_sem, own_sem):
    p = Place(depth)
    x = p.x
    rows = tok.shape[0]
    group = 2 * rows
    mine = pl.ds(pl.multiple_of(x * rows, rows), rows)
    theirs = pl.ds(pl.multiple_of((1 - x) * rows, rows), rows)
    n_chunks = layers * CH
    gat = Gather(p, wp, wg, w_send, w_recv, n_chunks)
    own = pltpu.make_async_copy(wp, wg.at[:, p.dp], own_sem)
    own.start()
    vg[x, p.z, p.y, p.c] = vp[...]
    xg[0, mine, :] = tok[...]
    p.greet()

    def give_rows(ref, index):
        return remote(ref, ref, x_send.at[index], x_recv.at[index], p.peer)

    v_far = [remote(vg.at[x, p.z, p.y, p.c], vg.at[x, p.z, p.y, p.c], v_send.at[i - 1], v_recv.at[i - 1], p.far(i))
             for i in range(1, depth)]
    for copy in v_far:
        copy.start()
    give_rows(xg.at[0, mine, :], 0).start()
    gat.begin(3)

    stream[...] = tok[...].astype(F32)
    def bias_rows(i, _):
        r = pl.ds(pl.multiple_of(i * 64, 64), 64)
        bias[r, :] = jnp.where(segc[r, :] == segr[...], 0.0, NEG)
        return _
    lax.fori_loop(0, group // 64, bias_rows, 0)

    for copy in v_far:
        copy.wait_recv()
    v_side = remote(vg.at[x, :, p.y, p.c], vg.at[x, :, p.y, p.c], v_send.at[depth - 1], v_recv.at[depth - 1], p.side)
    v_side.start()
    v_side.wait_recv()
    v_twin = remote(vg.at[x, :, :, p.c], vg.at[x, :, :, p.c], v_send.at[depth], v_recv.at[depth], p.twin)
    v_twin.start()
    own.wait()
    v_twin.wait_recv()
    v_peer = remote(vg.at[x], vg.at[x], v_send.at[depth + 1], v_recv.at[depth + 1], p.peer)
    v_peer.start()
    gat.tick()
    v_peer.wait_recv()
    heads_w = qkv.shape[-1]
    for z in range(depth):
        for y in range(2):
            b = (z * 2 + y) * 128
            vec[0:16, b:b + 128] = (vg[0, z, y, 0, 0:16] + vg[0, z, y, 1, 0:16]
                                    + vg[1, z, y, 0, 0:16] + vg[1, z, y, 1, 0:16])
    for z in range(depth):
        for_half = vg[x, z, 0, 0, 16:24] + vg[x, z, 0, 1, 16:24] + vg[x, z, 1, 0, 16:24] + vg[x, z, 1, 1, 16:24]
        vec[16:24, z * 128:(z + 1) * 128] = for_half
        for y in range(2):
            for c in range(2):
                b = (z * 4 + y * 2 + c) * 128
                vec[24:32, b:b + 128] = vg[x, z, y, c, 24:32]
    outs = []

    def keep(src, dst):
        copy = pltpu.make_async_copy(src, dst, o_sem.at[len(outs)])
        copy.start()
        outs.append(copy)

    keep(vec, vec_o)
    loads = {}

    def load(name, src, dst):
        copy = pltpu.make_async_copy(src, dst, l_sem.at[len(loads)])
        copy.start()
        loads[name] = copy

    def gain(l, i):
        r = l * 2 + i
        return vec[r:r + 1, 0:1024]

    def shift(l, i):
        r = 4 + l * 4 + i
        return vec[r:r + 1, 0:1024]

    def project(l, r):
        for m in range(3):
            w = wqkv[m].reshape(-1, heads_w)
            res = nn(xg[l, r, :], w)
            if m != 1:
                b = 16 + l * 2 + (m // 2)
                res = res + vec[b:b + 1, 0:heads_w]
            qkv[l, m, r, :] = res.astype(BF)

    half_lane = lax.broadcasted_iota(jnp.int32, (1, 128), 1) < HEAD
    first_half = jnp.where(half_lane, 1.0, 0.0).astype(BF)
    second_half = jnp.where(half_lane, 0.0, 1.0).astype(BF)
    scale = HEAD ** -0.5

    def attend(l):
        def pair(hp, carry):
            lanes = pl.ds(pl.multiple_of(hp * 128, 128), 128)
            k128 = qkv[l, 1, :, lanes]
            v_t = qkv[l, 2, :, lanes].T
            for qb in range(group // 256):
                q_rows = slice(qb * 256, (qb + 1) * 256)
                q128 = qkv[l, 0, q_rows, lanes]
                both = []
                for half in range(2):
                    k_half = k128 * ((second_half if half else first_half) * scale)
                    work[half] = nt(k_half, q128)
                    top = jnp.full((8, 256), NEG, F32)
                    for i in range(group // 64):
                        r = slice(i * 64, (i + 1) * 64)
                        s = work[half, r, :] + bias[r, q_rows]
                        work[half, r, :] = s
                        top = jnp.maximum(top, jnp.max(s.reshape(8, 8, 256), axis=0))
                    top = jnp.max(top, axis=0, keepdims=True)
                    tot = jnp.zeros((8, 256), F32)
                    for i in range(group // 64):
                        r = slice(i * 64, (i + 1) * 64)
                        e = jnp.exp(work[half, r, :] - top)
                        tot = tot + jnp.sum(e.reshape(8, 8, 256), axis=0)
                        prob[half, r, :] = e.astype(BF)
                    tot = jnp.sum(tot, axis=0, keepdims=True)
                    lse[l, pl.ds(hp * 2 + half, 1), q_rows] = top + jnp.log(tot)
                    res = nn(v_t[half * HEAD:(half + 1) * HEAD], prob[half])
                    both.append(res / tot)
                att[l, q_rows, lanes] = jnp.concatenate(both, axis=0).T.astype(BF)
            return carry
        lax.fori_loop(0, heads_w // 128, pair, 0)

    def out_term(l, r):
        return nn(att[l, r, :], wo[...].reshape(heads_w, -1))

    inv_sqrt2 = 2.0 ** -0.5
    inv_sqrt_2pi = (2.0 * math.pi) ** -0.5

    def up(l, j):
        b = 24 + l
        for cb in range(2):
            cols = slice(j * 512 + cb * 256, j * 512 + (cb + 1) * 256)
            w = wu[j, :, :, cb * 256:(cb + 1) * 256].reshape(-1, 256)
            work[cb] = nn(ng[l], w) + vec[b:b + 1, cols]

            def some(i, carry):
                r = pl.ds(pl.multiple_of(i * 32, 32), 32)
                pre = work[cb, r, :]
                part = 0.5 + 0.5 * lax.erf(pre * inv_sqrt2)
                hid[l, r, cols] = (pre * part).astype(BF)
                gp[l, r, cols] = (part + pre * jnp.exp(-0.5 * pre * pre) * inv_sqrt_2pi).astype(BF)
                return carry
            lax.fori_loop(0, group // 32, some, 0)

    def down_term(l, r, h):
        cols = slice(h * 256, (h + 1) * 256)
        w = wd[:, :, :, cols].reshape(-1, 256)
        return nn(hid[l, r, :], w)

    for l in range(layers):
        c0 = l * CH
        gat.until(c0 + 3)
        for m in range(3):
            load(("a", l, m), wg.at[c0 + m], wqkv.at[m])
        gat.tick()
        for m in range(3):
            loads["a", l, m].wait()
        project(l, mine)
        give_rows(xg.at[l, theirs, :], l * 4).wait_recv()
        keep(xg.at[l], xg_o.at[l])
        project(l, theirs)
        keep(qkv.at[l], qkv_o.at[l])
        gat.tick()
        attend(l)
        keep(lse.at[l], lse_o.at[l])
        keep(att.at[l], att_o.at[l])
        gat.until(c0 + 4)
        for hh in range(2):
            load(("o", l, hh), wg.at[c0 + 3, :, hh * 32:(hh + 1) * 32, :], wo.at[:, :, hh * 512:(hh + 1) * 512])
        gat.tick()
        for hh in range(2):
            loads["o", l, hh].wait()
        if l > 0:
            remote(sbuf, rbuf.at[0], x_send.at[l * 4 - 1], x_recv.at[l * 4 - 1], p.peer).wait_send()
        sbuf[...] = out_term(l, theirs).astype(BF)
        send = remote(sbuf, rbuf.at[l * 2], x_send.at[l * 4 + 1], x_recv.at[l * 4 + 1], p.peer)
        send.start()
        mix[l] = stream[...] + out_term(l, mine) + shift(l, 0)
        gat.tick()
        gat.tick()
        send.wait_recv()
        for i in range(rows // 32):
            r = slice(i * 32, (i + 1) * 32)
            mixed = mix[l, r, :] + rbuf[l * 2, r, :].astype(F32)
            mix[l, r, :] = mixed
            res = norm_rows(mixed, gain(l, 0), shift(l, 1))
            normed[r, :] = res
            ng[l, pl.ds(pl.multiple_of(x * rows + i * 32, 32), 32), :] = res.astype(BF)
        keep(mix.at[l], mix_o.at[l])
        give_rows(ng.at[l, mine, :], l * 4 + 2).start()
        for j in range(4):
            gat.until(c0 + 5 + j)
            load(("u", l, j), wg.at[c0 + 4 + j], wu.at[j])
            if j == 2:
                give_rows(ng.at[l, theirs, :], l * 4 + 2).wait_recv()
            if j >= 2:
                loads["u", l, j - 2].wait()
                up(l, j - 2)
        for j in (2, 3):
            loads["u", l, j].wait()
            up(l, j)
            gat.tick()
        keep(ng.at[l], ng_o.at[l])
        keep(hid.at[l], hid_o.at[l])
        keep(gp.at[l], gp_o.at[l])
        send.wait_send()
        for h in range(4):
            gat.until(c0 + 9 + h)
            for q in range(2):
                load(("d", l, h, q), wg.at[c0 + 8 + h, :, :, q * 256:(q + 1) * 256],
                     wd.at[:, q, :, h * 256:(h + 1) * 256])
            if h >= 1:
                for q in range(2):
                    loads["d", l, h - 1, q].wait()
                sbuf[:, (h - 1) * 256:h * 256] = down_term(l, theirs, h - 1).astype(BF)
        for q in range(2):
            loads["d", l, 3, q].wait()
        sbuf[:, 768:1024] = down_term(l, theirs, 3).astype(BF)
        send = remote(sbuf, rbuf.at[l * 2 + 1], x_send.at[l * 4 + 3], x_recv.at[l * 4 + 3], p.peer)
        send.start()
        gat.tick()
        for h in range(4):
            cols = slice(h * 256, (h + 1) * 256)
            sec[l, :, cols] = normed[:, cols] + down_term(l, mine, h) + shift(l, 2)[:, cols]
        gat.tick()
        gat.tick()
        send.wait_recv()
        for i in range(rows // 32):
            r = slice(i * 32, (i + 1) * 32)
            second = sec[l, r, :] + rbuf[l * 2 + 1, r, :].astype(F32)
            sec[l, r, :] = second
            res = norm_rows(second, gain(l, 1), shift(l, 3))
            stream[r, :] = res
            if l + 1 < layers:
                xg[l + 1, pl.ds(pl.multiple_of(x * rows + i * 32, 32), 32), :] = res.astype(BF)
        keep(sec.at[l], sec_o.at[l])
        if l + 1 < layers:
            give_rows(xg.at[l + 1, mine, :], l * 4 + 4).start()
    keep(stream, out_o)
    send.wait_send()
    gat.finish()
    for copy in v_far + [v_side, v_twin, v_peer]:
        copy.wait_send()
    for l in range(layers):
        give_rows(xg.at[l, mine, :], l * 4).wait_send()
        give_rows(ng.at[l, mine, :], l * 4 + 2).wait_send()
    for copy in outs:
        copy.wait()


def forward_call(depth, layers, rows, wp, vp, tok, segc, segr):
    group, hw, fh = 2 * rows, 512, 2048
    vm = pltpu.VMEM
    saved = [((layers, group, 1024), BF), ((layers, 3, group, hw), BF), ((layers, group, hw), BF),
             ((layers, 8, group), F32), ((layers, rows, 1024), F32), ((layers, group, 1024), BF),
             ((layers, group, fh), BF), ((layers, group, fh), BF), ((layers, rows, 1024), F32)]
    dp = depth * 4
    n = layers * CH
    out_shape = [jax.ShapeDtypeStruct((n, dp, 64, 512), BF), jax.ShapeDtypeStruct((32, 2048), F32),
                 jax.ShapeDtypeStruct((rows, 1024), F32)] + [jax.ShapeDtypeStruct(s, t) for s, t in saved]
    scratch = [vm((2, depth, 2, 2, 32, 128), F32), vm((32, 2048), F32), vm((rows, 1024), F32), vm((rows, 1024), F32),
               vm((group, group), F32), vm((2, group, 256), F32), vm((2, group, 256), BF)]
    scratch += [vm(s, t) for s, t in saved]
    scratch += [vm((rows, 1024), BF), vm((2 * layers, rows, 1024), BF),
                vm((3, dp, 64, 512), BF), vm((dp, 32, 1024), BF), vm((4, dp, 64, 512), BF), vm((dp, 2, 64, 1024), BF)]
    dma = pltpu.SemaphoreType.DMA
    scratch += [dma((n, depth + 1)), dma((n, depth + 1)), dma((depth + 2,)), dma((depth + 2,)),
                dma((4 * layers,)), dma((4 * layers,)), dma((17 * layers,)), dma((16 * layers,)), dma]
    full = pl.BlockSpec(memory_space=pltpu.VMEM)
    hbm = pl.BlockSpec(memory_space=pl.ANY)
    return pl.pallas_call(
        functools.partial(fwd_kernel, depth, layers),
        out_shape=out_shape,
        in_specs=[hbm, full, full, full, full],
        out_specs=[hbm] * len(out_shape),
        scratch_shapes=scratch,
        compiler_params=pltpu.CompilerParams(collective_id=1, has_side_effects=True, vmem_limit_bytes=62 * 2**20),
        cost_estimate=pl.CostEstimate(flops=14 * 10**9, bytes_accessed=60 * 10**6, transcendentals=0),
    )(wp, vp, tok, segc, segr)

def pack(w_query, w_key, w_value, w_out, w_up, w_down):
    layers = w_query.shape[0]
    o = w_out.reshape(layers, 1, 32, 2, 512).transpose(0, 1, 3, 2, 4).reshape(layers, 1, 64, 512)
    u = w_up.reshape(layers, 64, 4, 512).transpose(0, 2, 1, 3)
    d = w_down.reshape(layers, 2, 64, 4, 256).transpose(0, 3, 2, 1, 4).reshape(layers, 4, 64, 512)
    parts = [w_query[:, None], w_key[:, None], w_value[:, None], o, u, d]
    return jnp.concatenate(parts, axis=1).reshape(layers * CH, 64, 512)


def pack_vectors(qv_bias, up_bias, norm_gain, shift_bias):
    layers = qv_bias.shape[0]
    dp, x = lax.axis_index("dp"), lax.axis_index("tensor")

    def spread(rows32, slot):
        tiled = jnp.tile(rows32, (1, 4))
        lane = lax.broadcasted_iota(jnp.int32, tiled.shape, 1) // 32
        return jnp.where(lane == slot, tiled, 0.0)

    full = jnp.concatenate([norm_gain.reshape(layers * 2, 32), shift_bias.reshape(layers * 4, 32)])
    full = spread(full, (dp * 2 + x) % 4)
    half = spread(qv_bias.astype(F32).reshape(layers * 2, 32), dp % 4)
    out = jnp.zeros((32, 128), F32)
    out = out.at[0:layers * 6].set(full)
    out = out.at[16:16 + layers * 2].set(half)
    return out.at[24:24 + layers].set(up_bias.astype(F32))


def on_device(
    tokens,
    cotangent,
    segment_ids,
    w_query,
    w_key,
    w_value,
    w_out,
    w_up,
    w_down,
    qv_bias,
    up_bias,
    norm_gain,
    shift_bias,
):
    layers = w_query.shape[0]
    rows = tokens.shape[0]
    dp = lax.axis_size("dp")
    wp = pack(w_query, w_key, w_value, w_out, w_up, w_down)
    vp = pack_vectors(qv_bias, up_bias, norm_gain, shift_bias)
    (wg, vec, out, xg, qkv, att, lse, mix, ng, hid, gp, sec) = forward_call(
        dp // 4, layers, rows, wp, vp, tokens, segment_ids[:, None], segment_ids[None, :]
    )
    grad = cotangent.astype(F32)
    mat_shards = [None] * layers
    vec_shards = [None] * layers
    segs = segment_ids[None]
    for l in reversed(range(layers)):
        c = l * CH
        w_q, w_k, w_v = (wg[c + i].reshape(1024, 512) for i in range(3))
        w_o = wg[c + 3].reshape(dp, 2, 32, 512).transpose(0, 2, 1, 3).reshape(512, 1024)
        w_u = wg[c + 4:c + 8].reshape(4, 1024, 512).transpose(1, 0, 2).reshape(1024, 2048)
        w_d = wg[c + 8:c + 12].reshape(4, dp, 64, 2, 256).transpose(1, 3, 2, 0, 4).reshape(2048, 1024)
        mats = (w_q, w_k, w_v, w_o, w_u, w_d, None, None)
        vecs = (vec[l * 2:l * 2 + 2, :1024], vec[4 + l * 4:8 + l * 4, :1024])
        kept = (xg[l], qkv[l, 0], qkv[l, 1], qkv[l, 2], att[l], lse[l][None], mix[l], ng[l], gp[l], hid[l], sec[l])
        grad, mat_grads, vec_grads = backward_layer(grad, mats, vecs, kept, segs, segs.shape[1])
        dims = (0, 0, 0, 0, 0, 0, 1, 0)
        mat_shards[l] = tuple(
            lax.psum_scatter(g.astype(BF), "dp", scatter_dimension=d, tiled=True).astype(F32)
            for g, d in zip(mat_grads, dims)
        )
        vec_shards[l] = tuple(
            lax.psum_scatter(g, ("dp", "tensor"), scatter_dimension=1, tiled=True) for g in vec_grads
        )

    def stacked(index, source):
        return jnp.stack([entry[index] for entry in source])

    return (out, grad) + tuple(stacked(i, mat_shards) for i in range(8)) + tuple(stacked(i, vec_shards) for i in range(2))


def on_any_mesh(
    tokens,
    cotangent,
    segment_ids,
    w_query,
    w_key,
    w_value,
    w_out,
    w_up,
    w_down,
    qv_bias,
    up_bias,
    norm_gain,
    shift_bias,
):
    layers = w_query.shape[0]
    group = segment_ids.shape[0]
    seq = min(LEN, group)
    segs = segment_ids.reshape(group // seq, seq)
    stream = tokens.astype(jnp.float32)
    kept_all = []
    mats_all = []
    vecs_all = []
    for layer in range(layers):
        mats = (
            lax.all_gather(w_query[layer], "dp", axis=0, tiled=True),
            lax.all_gather(w_key[layer], "dp", axis=0, tiled=True),
            lax.all_gather(w_value[layer], "dp", axis=0, tiled=True),
            lax.all_gather(w_out[layer], "dp", axis=0, tiled=True),
            lax.all_gather(w_up[layer], "dp", axis=0, tiled=True),
            lax.all_gather(w_down[layer], "dp", axis=0, tiled=True),
            lax.all_gather(qv_bias[layer], "dp", axis=1, tiled=True),
            lax.all_gather(up_bias[layer], "dp", axis=0, tiled=True),
        )
        vecs = (
            lax.all_gather(norm_gain[layer], ("dp", "tensor"), axis=1, tiled=True),
            lax.all_gather(shift_bias[layer], ("dp", "tensor"), axis=1, tiled=True),
        )
        stream, kept = forward_layer(stream, mats, vecs, segs, seq)
        kept_all.append(kept)
        mats_all.append(mats)
        vecs_all.append(vecs)
    grad = cotangent.astype(jnp.float32)
    mat_shards = [None] * layers
    vec_shards = [None] * layers
    for layer in reversed(range(layers)):
        mats = (
            lax.all_gather(w_query[layer], "dp", axis=0, tiled=True),
            lax.all_gather(w_key[layer], "dp", axis=0, tiled=True),
            lax.all_gather(w_value[layer], "dp", axis=0, tiled=True),
            lax.all_gather(w_out[layer], "dp", axis=0, tiled=True),
            lax.all_gather(w_up[layer], "dp", axis=0, tiled=True),
            lax.all_gather(w_down[layer], "dp", axis=0, tiled=True),
            lax.all_gather(qv_bias[layer], "dp", axis=1, tiled=True),
            lax.all_gather(up_bias[layer], "dp", axis=0, tiled=True),
        )
        grad, mat_grads, vec_grads = backward_layer_any(
            grad, mats, vecs_all[layer], kept_all[layer], segs, seq
        )
        g_q, g_k, g_v, g_o, g_u, g_d, g_qv, g_ub = mat_grads
        mat_shards[layer] = (
            lax.psum_scatter(
                g_q.astype(jnp.bfloat16), "dp", scatter_dimension=0, tiled=True
            ).astype(jnp.float32),
            lax.psum_scatter(
                g_k.astype(jnp.bfloat16), "dp", scatter_dimension=0, tiled=True
            ).astype(jnp.float32),
            lax.psum_scatter(
                g_v.astype(jnp.bfloat16), "dp", scatter_dimension=0, tiled=True
            ).astype(jnp.float32),
            lax.psum_scatter(
                g_o.astype(jnp.bfloat16), "dp", scatter_dimension=0, tiled=True
            ).astype(jnp.float32),
            lax.psum_scatter(
                g_u.astype(jnp.bfloat16), "dp", scatter_dimension=0, tiled=True
            ).astype(jnp.float32),
            lax.psum_scatter(
                g_d.astype(jnp.bfloat16), "dp", scatter_dimension=0, tiled=True
            ).astype(jnp.float32),
            lax.psum_scatter(
                g_qv.astype(jnp.bfloat16), "dp", scatter_dimension=1, tiled=True
            ).astype(jnp.float32),
            lax.psum_scatter(
                g_ub.astype(jnp.bfloat16), "dp", scatter_dimension=0, tiled=True
            ).astype(jnp.float32),
        )
        g_gain, g_shift = vec_grads
        vec_shards[layer] = (
            lax.psum_scatter(g_gain, ("dp", "tensor"), scatter_dimension=1, tiled=True),
            lax.psum_scatter(g_shift, ("dp", "tensor"), scatter_dimension=1, tiled=True),
        )

    def stacked(index, source):
        return jnp.stack([entry[index] for entry in source])

    return (
        stream,
        grad,
        stacked(0, mat_shards),
        stacked(1, mat_shards),
        stacked(2, mat_shards),
        stacked(3, mat_shards),
        stacked(4, mat_shards),
        stacked(5, mat_shards),
        stacked(6, mat_shards),
        stacked(7, mat_shards),
        stacked(0, vec_shards),
        stacked(1, vec_shards),
    )


def solution(mesh):
    in_specs = (
        P(("dp", "tensor"), None),
        P(("dp", "tensor"), None),
        P("dp"),
        P(None, "dp", "tensor"),
        P(None, "dp", "tensor"),
        P(None, "dp", "tensor"),
        P(None, ("tensor", "dp"), None),
        P(None, "dp", "tensor"),
        P(None, ("tensor", "dp"), None),
        P(None, None, ("tensor", "dp")),
        P(None, ("tensor", "dp")),
        P(None, None, ("dp", "tensor")),
        P(None, None, ("dp", "tensor")),
    )
    out_specs = (
        P(("dp", "tensor"), None),
        P(("dp", "tensor"), None),
        P(None, "dp", "tensor"),
        P(None, "dp", "tensor"),
        P(None, "dp", "tensor"),
        P(None, ("tensor", "dp"), None),
        P(None, "dp", "tensor"),
        P(None, ("tensor", "dp"), None),
        P(None, None, ("tensor", "dp")),
        P(None, ("tensor", "dp")),
        P(None, None, ("dp", "tensor")),
        P(None, None, ("dp", "tensor")),
    )
    small = mesh.shape["tensor"] == 2 and mesh.shape["dp"] == 16
    return jax.shard_map(
        on_device if small else on_any_mesh, mesh=mesh, in_specs=in_specs, out_specs=out_specs, check_vma=False
    )
```

```python
import functools
import math

import jax
import jax.numpy as jnp
from jax import lax
from jax.experimental import pallas as pl
from jax.experimental.pallas import tpu as pltpu
from jax.sharding import PartitionSpec as P

HEAD = 64
LEN = 512


EPS = 1e-06
NEG = -1e30


def layer_norm(z, gain, shift):
    mean = jnp.mean(z, axis=-1, keepdims=True)
    cent = z - mean
    var = jnp.mean(cent * cent, axis=-1, keepdims=True)
    return cent * lax.rsqrt(var + EPS) * gain + shift


def gelu_exact(pre):
    return jax.nn.gelu(pre, approximate=False)


def inner(left, right):
    return lax.dot_general(
        left, right, (((0,), (0,)), ((), ())), preferred_element_type=jnp.float32
    )


def times_back(left, right):
    return lax.dot_general(
        left, right, (((1,), (1,)), ((), ())), preferred_element_type=jnp.float32
    )


def gather_rows(rows):
    return lax.all_gather(rows, "tensor", axis=0, tiled=True)


def gather_grads(rows):
    return lax.all_gather(rows, "tensor", axis=0, tiled=True)


def sum_rows(term, rows):
    return lax.psum_scatter(
        term(jnp.int32(0), lax.axis_size("tensor") * rows).astype(jnp.bfloat16),
        "tensor",
        scatter_dimension=0,
        tiled=True,
    ).astype(jnp.float32)


def sum_grads(term, rows):
    return lax.psum_scatter(
        term(jnp.int32(0), lax.axis_size("tensor") * rows).astype(jnp.bfloat16),
        "tensor",
        scatter_dimension=0,
        tiled=True,
    ).astype(jnp.float32)


def allowed(segment):
    return segment[:, None] == segment[None, :]


def attend_one(args):
    query, key, value, segment = args
    scale = HEAD ** (-0.5)
    scores = jnp.einsum("qhd,khd->hqk", query, key, preferred_element_type=jnp.float32) * scale
    scores = jnp.where(allowed(segment)[None], scores, NEG)
    top = jnp.max(scores, axis=-1, keepdims=True)
    total = top + jnp.log(jnp.sum(jnp.exp(scores - top), axis=-1, keepdims=True))
    probs = jnp.exp(scores - total).astype(jnp.bfloat16)
    result = jnp.einsum("hqk,khd->qhd", probs, value, preferred_element_type=jnp.float32)
    return (result.astype(jnp.bfloat16), total[..., 0])


def attend_back(args):
    query, key, value, segment, total, d_att = args
    scale = HEAD ** (-0.5)
    scores = jnp.einsum("qhd,khd->hqk", query, key, preferred_element_type=jnp.float32) * scale
    scores = jnp.where(allowed(segment)[None], scores, NEG)
    probs = jnp.exp(scores - total[..., None])
    d_probs = jnp.einsum("qhd,khd->hqk", d_att, value, preferred_element_type=jnp.float32)
    row_dot = jnp.sum(d_probs * probs, axis=-1, keepdims=True)
    d_scores = (probs * (d_probs - row_dot)).astype(jnp.bfloat16)
    d_query = (
        jnp.einsum("hqk,khd->qhd", d_scores, key, preferred_element_type=jnp.float32) * scale
    ).astype(jnp.bfloat16)
    d_key = (
        jnp.einsum("hqk,qhd->khd", d_scores, query, preferred_element_type=jnp.float32) * scale
    ).astype(jnp.bfloat16)
    d_value = jnp.einsum(
        "hqk,qhd->khd", probs.astype(jnp.bfloat16), d_att, preferred_element_type=jnp.float32
    ).astype(jnp.bfloat16)
    return (d_query, d_key, d_value)


def forward_layer(stream, mats, vecs, segs, seq):
    w_q, w_k, w_v, w_o, w_u, w_d, qvb, upb = mats
    gains, shifts = vecs
    seqs = segs.shape[0]
    rows = stream.shape[0]
    x_rows = gather_rows(stream.astype(jnp.bfloat16))
    query = (
        jnp.dot(x_rows, w_q, preferred_element_type=jnp.float32) + qvb[0].astype(jnp.float32)
    ).astype(jnp.bfloat16)
    key = jnp.dot(x_rows, w_k, preferred_element_type=jnp.float32).astype(jnp.bfloat16)
    value = (
        jnp.dot(x_rows, w_v, preferred_element_type=jnp.float32) + qvb[1].astype(jnp.float32)
    ).astype(jnp.bfloat16)
    width = query.shape[1]
    local_heads = width // HEAD

    def split(matrix):
        return matrix.reshape(seqs, seq, local_heads, HEAD)

    attended, totals = lax.map(attend_one, (split(query), split(key), split(value), segs))
    attended = attended.reshape(seqs * seq, width)

    def out_term(start, count):
        return jnp.dot(attended, w_o, preferred_element_type=jnp.float32)

    out_sum = sum_rows(out_term, rows)
    mixed = stream + out_sum + shifts[0]
    normed = layer_norm(mixed, gains[0], shifts[1])
    n_rows = gather_rows(normed.astype(jnp.bfloat16))
    pre = jnp.dot(n_rows, w_u, preferred_element_type=jnp.float32) + upb.astype(jnp.float32)
    hidden = gelu_exact(pre).astype(jnp.bfloat16)

    def down_term(start, count):
        return jnp.dot(hidden, w_d, preferred_element_type=jnp.float32)

    down_sum = sum_rows(down_term, rows)
    second = normed + down_sum + shifts[2]
    result = layer_norm(second, gains[1], shifts[3])
    kept = (x_rows, query, key, value, attended, totals, mixed, n_rows, pre, hidden, second)
    return (result, kept)


def backward_layer(grad, mats, vecs, kept, segs, seq):
    w_q, w_k, w_v, w_o, w_u, w_d, qvb, upb = mats
    gains, shifts = vecs
    x_rows, query, key, value, attended, totals, mixed, n_rows, pre, hidden, second = kept
    seqs = segs.shape[0]
    rows = grad.shape[0]
    width = query.shape[1]
    local_heads = width // HEAD

    def split(matrix):
        return matrix.reshape(seqs, seq, local_heads, HEAD)

    _, pull_second = jax.vjp(layer_norm, second, gains[1], shifts[3])
    d_second, d_gain_two, d_shift_two = pull_second(grad)
    d_down_bias = jnp.sum(d_second, axis=0)
    d_f = gather_grads(d_second.astype(jnp.bfloat16))
    grad_down = inner(hidden, d_f)
    d_hidden = times_back(d_f, w_d)
    _, pull_gelu = jax.vjp(gelu_exact, pre)
    d_pre = pull_gelu(d_hidden)[0].astype(jnp.bfloat16)
    grad_up = inner(n_rows, d_pre)
    d_up_bias = jnp.sum(d_pre.astype(jnp.float32), axis=0)

    def up_term(start, count):
        return times_back(d_pre, w_u)

    d_normed = d_second + sum_grads(up_term, rows)
    _, pull_first = jax.vjp(layer_norm, mixed, gains[0], shifts[1])
    d_mixed, d_gain_one, d_shift_one = pull_first(d_normed)
    d_out_bias = jnp.sum(d_mixed, axis=0)
    d_a = gather_grads(d_mixed.astype(jnp.bfloat16))
    grad_out = inner(attended, d_a)
    d_att = times_back(d_a, w_o).astype(jnp.bfloat16)
    d_query, d_key, d_value = lax.map(
        attend_back, (split(query), split(key), split(value), segs, totals, split(d_att))
    )
    d_query = d_query.reshape(seqs * seq, width)
    d_key = d_key.reshape(seqs * seq, width)
    d_value = d_value.reshape(seqs * seq, width)
    grad_q = inner(x_rows, d_query)
    grad_k = inner(x_rows, d_key)
    grad_v = inner(x_rows, d_value)
    d_qv = jnp.stack(
        [jnp.sum(d_query.astype(jnp.float32), axis=0), jnp.sum(d_value.astype(jnp.float32), axis=0)]
    )

    def in_term(start, count):
        part = times_back(d_query, w_q)
        part = part + times_back(d_key, w_k)
        return part + times_back(d_value, w_v)

    d_stream = d_mixed + sum_grads(in_term, rows)
    mat_grads = (grad_q, grad_k, grad_v, grad_out, grad_up, grad_down, d_qv, d_up_bias)
    vec_grads = (
        jnp.stack([d_gain_one, d_gain_two]),
        jnp.stack([d_out_bias, d_shift_one, d_down_bias, d_shift_two]),
    )
    return (d_stream, mat_grads, vec_grads)


MESH = pl.DeviceIdType.MESH
BF = jnp.bfloat16
F32 = jnp.float32
CH = 12


def nt(left, right):
    return lax.dot_general(left, right, (((1,), (1,)), ((), ())), preferred_element_type=F32)


def nn(left, right):
    return lax.dot_general(left, right, (((1,), (0,)), ((), ())), preferred_element_type=F32)


def tn(left, right):
    return lax.dot_general(left, right, (((0,), (0,)), ((), ())), preferred_element_type=F32)


def remote(src, dst, send_sem, recv_sem, device):
    return pltpu.make_async_remote_copy(
        src_ref=src, dst_ref=dst, send_sem=send_sem, recv_sem=recv_sem, device_id=device, device_id_type=MESH
    )


class Place:
    def __init__(self, depth):
        self.depth = depth
        self.dp = lax.axis_index("dp")
        self.x = lax.axis_index("tensor")
        self.z = self.dp // 4
        self.y = (self.dp // 2) % 2
        self.c = self.dp % 2

    def at(self, z, y, c):
        return {"dp": z * 4 + y * 2 + c, "tensor": self.x}

    def far(self, step):
        return self.at((self.z + step) % self.depth, self.y, self.c)

    def before(self, step):
        return (self.z + self.depth - step) % self.depth

    @property
    def side(self):
        return self.at(self.z, 1 - self.y, self.c)

    @property
    def twin(self):
        return self.at(self.z, self.y, 1 - self.c)

    @property
    def peer(self):
        return {"dp": self.dp, "tensor": 1 - self.x}

    def greet(self):
        barrier = pltpu.get_barrier_semaphore()
        partners = [self.far(i) for i in range(1, self.depth)] + [self.side, self.twin, self.peer]
        for device in partners:
            pl.semaphore_signal(barrier, inc=1, device_id=device, device_id_type=MESH)
        pl.semaphore_wait(barrier, len(partners))


class Gather:
    def __init__(self, place, wp, wg, send, recv, total):
        self.p, self.wp, self.wg, self.send, self.recv, self.total = place, wp, wg, send, recv, total
        self.view = wg.reshape(wg.shape[0], place.depth, 2, 2, *wg.shape[2:])
        self.time = 0
        self.have = 0

    def far(self, k, i):
        p = self.p
        return remote(self.wp.at[k], self.wg.at[k, p.dp], self.send.at[k, i - 1], self.recv.at[k, i - 1], p.far(i))

    def far_in(self, k, i):
        p = self.p
        ref = self.wg.at[k, p.before(i) * 4 + p.y * 2 + p.c]
        return remote(ref, ref, self.send.at[k, i - 1], self.recv.at[k, i - 1], p.far(i))

    def side(self, k, y):
        p, d = self.p, self.p.depth - 1
        ref = self.view.at[k, :, y, p.c]
        return remote(ref, ref, self.send.at[k, d], self.recv.at[k, d], p.side)

    def twin(self, k, c):
        p, d = self.p, self.p.depth
        ref = self.view.at[k, :, :, c]
        return remote(ref, ref, self.send.at[k, d], self.recv.at[k, d], p.twin)

    def begin(self, ahead):
        self.ahead = ahead
        for k in range(ahead):
            for i in range(1, self.p.depth):
                self.far(k, i).start()

    def tick(self):
        t, n = self.time, self.total
        if t >= n + 3:
            return
        if t + self.ahead < n:
            for i in range(1, self.p.depth):
                self.far(t + self.ahead, i).start()
        if t < n:
            for i in range(1, self.p.depth):
                self.far_in(t, i).wait_recv()
            self.side(t, self.p.y).start()
        if 1 <= t <= n:
            self.side(t - 1, 1 - self.p.y).wait_recv()
            self.twin(t - 1, self.p.c).start()
        if t >= 2 and t - 2 < n:
            self.twin(t - 2, 1 - self.p.c).wait_recv()
            self.have = t - 1
        self.time += 1

    def until(self, count):
        while self.have < count:
            self.tick()

    def finish(self):
        self.until(self.total)
        for k in range(self.total):
            for i in range(1, self.p.depth):
                self.far(k, i).wait_send()
            self.side(k, self.p.y).wait_send()
            self.twin(k, self.p.c).wait_send()


def norm_rows(z, gain, shift):
    mean = jnp.mean(z, axis=-1, keepdims=True)
    cent = z - mean
    var = jnp.mean(cent * cent, axis=-1, keepdims=True)
    return cent * lax.rsqrt(var + EPS) * gain + shift


def fwd_kernel(depth, layers, wp, vp, tok, segc, segr,
               wg, vec_o, out_o, xt_o, qkv_o, attt_o, lse_o, mix_o, nt_o, ht_o, gp_o, sec_o,
               vg, vec, stream, normed, bias, work, prob, xt, qkv, attt, lse, mix, ngt, hidt, gp, sec,
               xg, ng, hid, att, sbuf, rbuf,
               wqkv, wo, wu, wd,
               w_send, w_recv, v_send, v_recv, x_send, x_recv, l_sem, o_sem, own_sem):
    p = Place(depth)
    x = p.x
    rows = tok.shape[0]
    group = 2 * rows
    mine = pl.ds(pl.multiple_of(x * rows, rows), rows)
    theirs = pl.ds(pl.multiple_of((1 - x) * rows, rows), rows)
    n_chunks = layers * CH
    gat = Gather(p, wp, wg, w_send, w_recv, n_chunks)
    own = pltpu.make_async_copy(wp, wg.at[:, p.dp], own_sem)
    own.start()
    vg[x, p.z, p.y, p.c] = vp[...]
    xg[0, mine, :] = tok[...]
    p.greet()

    def give_rows(ref, index):
        return remote(ref, ref, x_send.at[index], x_recv.at[index], p.peer)

    v_far = [remote(vg.at[x, p.z, p.y, p.c], vg.at[x, p.z, p.y, p.c], v_send.at[i - 1], v_recv.at[i - 1], p.far(i))
             for i in range(1, depth)]
    for copy in v_far:
        copy.start()
    give_rows(xg.at[0, mine, :], 0).start()
    gat.begin(3)

    stream[...] = tok[...].astype(F32)
    def bias_rows(i, _):
        r = pl.ds(pl.multiple_of(i * 64, 64), 64)
        bias[r, :] = jnp.where(segc[r, :] == segr[...], 0.0, NEG)
        return _
    lax.fori_loop(0, group // 64, bias_rows, 0)

    for copy in v_far:
        copy.wait_recv()
    v_side = remote(vg.at[x, :, p.y, p.c], vg.at[x, :, p.y, p.c], v_send.at[depth - 1], v_recv.at[depth - 1], p.side)
    v_side.start()
    v_side.wait_recv()
    v_twin = remote(vg.at[x, :, :, p.c], vg.at[x, :, :, p.c], v_send.at[depth], v_recv.at[depth], p.twin)
    v_twin.start()
    own.wait()
    v_twin.wait_recv()
    v_peer = remote(vg.at[x], vg.at[x], v_send.at[depth + 1], v_recv.at[depth + 1], p.peer)
    v_peer.start()
    gat.tick()
    v_peer.wait_recv()
    heads_w = qkv.shape[-1]
    for z in range(depth):
        for y in range(2):
            b = (z * 2 + y) * 128
            vec[0:16, b:b + 128] = (vg[0, z, y, 0, 0:16] + vg[0, z, y, 1, 0:16]
                                    + vg[1, z, y, 0, 0:16] + vg[1, z, y, 1, 0:16])
    for z in range(depth):
        for_half = vg[x, z, 0, 0, 16:24] + vg[x, z, 0, 1, 16:24] + vg[x, z, 1, 0, 16:24] + vg[x, z, 1, 1, 16:24]
        vec[16:24, z * 128:(z + 1) * 128] = for_half
        for y in range(2):
            for c in range(2):
                b = (z * 4 + y * 2 + c) * 128
                vec[24:32, b:b + 128] = vg[x, z, y, c, 24:32]
    outs = []

    def keep(src, dst):
        copy = pltpu.make_async_copy(src, dst, o_sem.at[len(outs)])
        copy.start()
        outs.append(copy)

    keep(vec, vec_o)
    loads = {}

    def load(name, src, dst):
        copy = pltpu.make_async_copy(src, dst, l_sem.at[len(loads)])
        copy.start()
        loads[name] = copy

    def gain(l, i):
        r = l * 2 + i
        return vec[r:r + 1, 0:1024]

    def shift(l, i):
        r = 4 + l * 4 + i
        return vec[r:r + 1, 0:1024]

    def project(l, r):
        for m in range(3):
            w = wqkv[m].reshape(-1, heads_w)
            res = nn(xg[l, r, :], w)
            if m != 1:
                b = 16 + l * 2 + (m // 2)
                res = res + vec[b:b + 1, 0:heads_w]
            qkv[l, m, r, :] = res.astype(BF)

    half_lane = lax.broadcasted_iota(jnp.int32, (1, 128), 1) < HEAD
    first_half = jnp.where(half_lane, 1.0, 0.0).astype(BF)
    second_half = jnp.where(half_lane, 0.0, 1.0).astype(BF)
    scale = HEAD ** -0.5

    def attend(l):
        def pair(hp, carry):
            lanes = pl.ds(pl.multiple_of(hp * 128, 128), 128)
            k128 = qkv[l, 1, :, lanes]
            v_t = qkv[l, 2, :, lanes].T
            for qb in range(group // 256):
                q_rows = slice(qb * 256, (qb + 1) * 256)
                q128 = qkv[l, 0, q_rows, lanes]
                both = []
                for half in range(2):
                    k_half = k128 * ((second_half if half else first_half) * scale)
                    work[half] = nt(k_half, q128)
                    top = jnp.full((8, 256), NEG, F32)
                    for i in range(group // 64):
                        r = slice(i * 64, (i + 1) * 64)
                        s = work[half, r, :] + bias[r, q_rows]
                        work[half, r, :] = s
                        top = jnp.maximum(top, jnp.max(s.reshape(8, 8, 256), axis=0))
                    top = jnp.max(top, axis=0, keepdims=True)
                    tot = jnp.zeros((8, 256), F32)
                    for i in range(group // 64):
                        r = slice(i * 64, (i + 1) * 64)
                        e = jnp.exp(work[half, r, :] - top)
                        tot = tot + jnp.sum(e.reshape(8, 8, 256), axis=0)
                        prob[half, r, :] = e.astype(BF)
                    tot = jnp.sum(tot, axis=0, keepdims=True)
                    lse[l, pl.ds(hp * 2 + half, 1), q_rows] = top + jnp.log(tot)
                    res = nn(v_t[half * HEAD:(half + 1) * HEAD], prob[half])
                    both.append(res / tot)
                o_t = jnp.concatenate(both, axis=0)
                attt[l, lanes, q_rows] = o_t.astype(BF)
                att[q_rows, lanes] = o_t.T.astype(BF)
            return carry
        lax.fori_loop(0, heads_w // 128, pair, 0)

    def out_term(l, r):
        return nn(att[r, :], wo[...].reshape(heads_w, -1))

    def flip(src, dst):
        def block(i, carry):
            c = pl.ds(pl.multiple_of(i * 256, 256), 256)
            dst[c, :] = src[:, c].T
            return carry
        lax.fori_loop(0, src.shape[1] // 256, block, 0)

    inv_sqrt2 = 2.0 ** -0.5
    inv_sqrt_2pi = (2.0 * math.pi) ** -0.5

    def up(l, j):
        b = 24 + l
        for cb in range(2):
            cols = slice(j * 512 + cb * 256, j * 512 + (cb + 1) * 256)
            w = wu[j, :, :, cb * 256:(cb + 1) * 256].reshape(-1, 256)
            work[cb] = nn(ng[l], w) + vec[b:b + 1, cols]

            def some(i, carry):
                r = pl.ds(pl.multiple_of(i * 32, 32), 32)
                pre = work[cb, r, :]
                part = 0.5 + 0.5 * lax.erf(pre * inv_sqrt2)
                hid[r, cols] = (pre * part).astype(BF)
                gp[l, r, cols] = (part + pre * jnp.exp(-0.5 * pre * pre) * inv_sqrt_2pi).astype(BF)
                return carry
            lax.fori_loop(0, group // 32, some, 0)

    def down_term(l, r, h):
        cols = slice(h * 256, (h + 1) * 256)
        w = wd[:, :, :, cols].reshape(-1, 256)
        return nn(hid[r, :], w)

    for l in range(layers):
        c0 = l * CH
        gat.until(c0 + 3)
        for m in range(3):
            load(("a", l, m), wg.at[c0 + m], wqkv.at[m])
        gat.tick()
        for m in range(3):
            loads["a", l, m].wait()
        project(l, mine)
        give_rows(xg.at[l, theirs, :], l * 4).wait_recv()
        project(l, theirs)
        keep(qkv.at[l], qkv_o.at[l])
        gat.tick()
        attend(l)
        keep(lse.at[l], lse_o.at[l])
        keep(attt.at[l], attt_o.at[l])
        gat.until(c0 + 4)
        for hh in range(2):
            load(("o", l, hh), wg.at[c0 + 3, :, hh * 32:(hh + 1) * 32, :], wo.at[:, :, hh * 512:(hh + 1) * 512])
        gat.tick()
        for hh in range(2):
            loads["o", l, hh].wait()
        if l > 0:
            remote(sbuf, rbuf.at[0], x_send.at[l * 4 - 1], x_recv.at[l * 4 - 1], p.peer).wait_send()
        sbuf[...] = out_term(l, theirs).astype(BF)
        send = remote(sbuf, rbuf.at[l * 2], x_send.at[l * 4 + 1], x_recv.at[l * 4 + 1], p.peer)
        send.start()
        mix[l] = stream[...] + out_term(l, mine) + shift(l, 0)
        gat.tick()
        flip(xg.at[l], xt.at[l])
        keep(xt.at[l], xt_o.at[l])
        gat.tick()
        send.wait_recv()
        for i in range(rows // 32):
            r = slice(i * 32, (i + 1) * 32)
            mixed = mix[l, r, :] + rbuf[l * 2, r, :].astype(F32)
            mix[l, r, :] = mixed
            res = norm_rows(mixed, gain(l, 0), shift(l, 1))
            normed[r, :] = res
            ng[l, pl.ds(pl.multiple_of(x * rows + i * 32, 32), 32), :] = res.astype(BF)
        keep(mix.at[l], mix_o.at[l])
        give_rows(ng.at[l, mine, :], l * 4 + 2).start()
        for j in range(4):
            gat.until(c0 + 5 + j)
            load(("u", l, j), wg.at[c0 + 4 + j], wu.at[j])
            if j == 2:
                give_rows(ng.at[l, theirs, :], l * 4 + 2).wait_recv()
            if j >= 2:
                loads["u", l, j - 2].wait()
                up(l, j - 2)
        for j in (2, 3):
            loads["u", l, j].wait()
            up(l, j)
            gat.tick()
        keep(gp.at[l], gp_o.at[l])
        send.wait_send()
        for h in range(4):
            gat.until(c0 + 9 + h)
            for q in range(2):
                load(("d", l, h, q), wg.at[c0 + 8 + h, :, :, q * 256:(q + 1) * 256],
                     wd.at[:, q, :, h * 256:(h + 1) * 256])
            if h >= 1:
                for q in range(2):
                    loads["d", l, h - 1, q].wait()
                sbuf[:, (h - 1) * 256:h * 256] = down_term(l, theirs, h - 1).astype(BF)
        for q in range(2):
            loads["d", l, 3, q].wait()
        sbuf[:, 768:1024] = down_term(l, theirs, 3).astype(BF)
        send = remote(sbuf, rbuf.at[l * 2 + 1], x_send.at[l * 4 + 3], x_recv.at[l * 4 + 3], p.peer)
        send.start()
        gat.tick()
        for h in range(4):
            cols = slice(h * 256, (h + 1) * 256)
            sec[l, :, cols] = normed[:, cols] + down_term(l, mine, h) + shift(l, 2)[:, cols]
        gat.tick()
        flip(ng.at[l], ngt.at[l])
        flip(hid, hidt.at[l])
        keep(ngt.at[l], nt_o.at[l])
        keep(hidt.at[l], ht_o.at[l])
        gat.tick()
        send.wait_recv()
        for i in range(rows // 32):
            r = slice(i * 32, (i + 1) * 32)
            second = sec[l, r, :] + rbuf[l * 2 + 1, r, :].astype(F32)
            sec[l, r, :] = second
            res = norm_rows(second, gain(l, 1), shift(l, 3))
            stream[r, :] = res
            if l + 1 < layers:
                xg[l + 1, pl.ds(pl.multiple_of(x * rows + i * 32, 32), 32), :] = res.astype(BF)
        keep(sec.at[l], sec_o.at[l])
        if l + 1 < layers:
            give_rows(xg.at[l + 1, mine, :], l * 4 + 4).start()
    keep(stream, out_o)
    send.wait_send()
    gat.finish()
    for copy in v_far + [v_side, v_twin, v_peer]:
        copy.wait_send()
    for l in range(layers):
        give_rows(xg.at[l, mine, :], l * 4).wait_send()
        give_rows(ng.at[l, mine, :], l * 4 + 2).wait_send()
    for copy in outs:
        copy.wait()


def forward_call(depth, layers, rows, wp, vp, tok, segc, segr):
    group, hw, fh = 2 * rows, 512, 2048
    vm = pltpu.VMEM
    saved = [((layers, 1024, group), BF), ((layers, 3, group, hw), BF), ((layers, hw, group), BF),
             ((layers, 8, group), F32), ((layers, rows, 1024), F32), ((layers, 1024, group), BF),
             ((layers, fh, group), BF), ((layers, group, fh), BF), ((layers, rows, 1024), F32)]
    dp = depth * 4
    n = layers * CH
    out_shape = [jax.ShapeDtypeStruct((n, dp, 64, 512), BF), jax.ShapeDtypeStruct((32, 2048), F32),
                 jax.ShapeDtypeStruct((rows, 1024), F32)] + [jax.ShapeDtypeStruct(s, t) for s, t in saved]
    scratch = [vm((2, depth, 2, 2, 32, 128), F32), vm((32, 2048), F32), vm((rows, 1024), F32), vm((rows, 1024), F32),
               vm((group, group), F32), vm((2, group, 256), F32), vm((2, group, 256), BF)]
    scratch += [vm(s, t) for s, t in saved]
    scratch += [vm((layers, group, 1024), BF), vm((layers, group, 1024), BF), vm((group, fh), BF), vm((group, hw), BF)]
    scratch += [vm((rows, 1024), BF), vm((2 * layers, rows, 1024), BF),
                vm((3, dp, 64, 512), BF), vm((dp, 32, 1024), BF), vm((4, dp, 64, 512), BF), vm((dp, 2, 64, 1024), BF)]
    dma = pltpu.SemaphoreType.DMA
    scratch += [dma((n, depth + 1)), dma((n, depth + 1)), dma((depth + 2,)), dma((depth + 2,)),
                dma((4 * layers,)), dma((4 * layers,)), dma((17 * layers,)), dma((16 * layers,)), dma]
    full = pl.BlockSpec(memory_space=pltpu.VMEM)
    hbm = pl.BlockSpec(memory_space=pl.ANY)
    return pl.pallas_call(
        functools.partial(fwd_kernel, depth, layers),
        out_shape=out_shape,
        in_specs=[hbm, full, full, full, full],
        out_specs=[hbm] * len(out_shape),
        scratch_shapes=scratch,
        compiler_params=pltpu.CompilerParams(collective_id=1, has_side_effects=True, vmem_limit_bytes=62 * 2**20),
        cost_estimate=pl.CostEstimate(flops=14 * 10**9, bytes_accessed=60 * 10**6, transcendentals=0),
    )(wp, vp, tok, segc, segr)


class Scatter:
    def __init__(self, place, order, grads, r1, r2, r3, stage, put, send, recv, out_sem):
        self.p, self.order, self.grads, self.r1, self.r2, self.r3 = place, order, grads, r1, r2, r3
        self.stage, self.put, self.send, self.recv, self.out_sem = stage, put, send, recv, out_sem
        self.view = grads.reshape(grads.shape[0], place.depth, 2, 2, *grads.shape[2:])
        self.time = 0
        self.ready = 0
        self.total = len(order)
        self.slots = r1.shape[0]
        self.outs = {}

    def core(self, n):
        p, s, d = self.p, n % self.slots, self.p.depth - 1
        return remote(self.view.at[self.order[n] % CH, :, :, 1 - p.c], self.r1.at[s],
                      self.send.at[n, d + 1], self.recv.at[n, d + 1], p.twin)

    def side(self, n):
        p, s, d = self.p, n % self.slots, self.p.depth - 1
        return remote(self.r1.at[s, :, 1 - p.y], self.r2.at[s], self.send.at[n, d], self.recv.at[n, d], p.side)

    def far(self, n, i):
        p, s = self.p, n % self.slots
        return remote(self.r2.at[s, (p.z + i) % p.depth], self.r3.at[s, i - 1],
                      self.send.at[n, i - 1], self.recv.at[n, i - 1], p.far(i))

    def step_far(self, n):
        p, s = self.p, n % self.slots
        for i in range(1, p.depth):
            self.far(n, i).wait()
        self.side(n).wait_send()
        if n >= 2:
            for copy in self.outs[n - 2]:
                copy.wait()
        total = self.r2[s, p.z].astype(F32)
        for i in range(p.depth - 1):
            total = total + self.r3[s, i].astype(F32)
        self.stage[n % 2] = total
        self.outs[n] = self.put(self.order[n], self.stage.at[n % 2], self.out_sem.at[n % 2])
        for copy in self.outs[n]:
            copy.start()

    def step_side(self, n):
        p, s = self.p, n % self.slots
        self.side(n).wait_recv()
        self.r2[s] = self.r2[s] + self.r1[s, :, p.y]
        for i in range(1, p.depth):
            self.far(n, i).start()

    def step_core(self, n):
        p, s = self.p, n % self.slots
        self.core(n).wait()
        self.r1[s] = self.r1[s] + self.view[self.order[n] % CH, :, :, p.c]
        self.side(n).start()

    def tick(self):
        t, n = self.time, self.total
        if t >= n + 3 or (t < n and t >= self.ready):
            return
        if 3 <= t:
            self.step_far(t - 3)
        if 2 <= t < n + 2:
            self.step_side(t - 2)
        if 1 <= t < n + 1:
            self.step_core(t - 1)
        if t < n:
            self.core(t).start()
        self.time += 1

    def free(self, n):
        while self.time < n - CH + 2:
            self.tick()

    def finish(self):
        while self.time < self.total + 3:
            self.tick()
        for n in (self.total - 2, self.total - 1):
            for copy in self.outs[n]:
                copy.wait()


def bwd_kernel(depth, layers, vec, cot, segc, segr, wg, xt_i, qkv_i, attt_i, lse_i, mix_i, nt_i, ht_i, gp_i, sec_i,
               grad_o, vsum_o, gq_o, gk_o, gv_o, go_o, gu_o, gd_o,
               grads, r1, r2, r3, stage, wqkv, wo, wu, wd,
               xt, qkv, attt, lse, mix, ngt, hidt, gp, sec,
               dpre, fg, ag, rbuf, sbuf, g, dz, dqkv, datt, work, prob, bias, vacc, vx, vc, vy, vz,
               g_send, g_recv, x_send, x_recv, v_send, v_recv, l_sem, o_sem, e_sem):
    p = Place(depth)
    x = p.x
    rows = cot.shape[0]
    group = 2 * rows
    heads_w = datt.shape[-1]
    mine = pl.ds(pl.multiple_of(x * rows, rows), rows)
    theirs = pl.ds(pl.multiple_of((1 - x) * rows, rows), rows)
    loads = {}

    def load(name, src, dst):
        copy = pltpu.make_async_copy(src, dst, l_sem.at[len(loads)])
        copy.start()
        loads[name] = copy

    def need(*names):
        for name in names:
            loads[name].wait()

    def load_down(l):
        for h in range(4):
            for q in range(2):
                load(("d", l, h, q), wg.at[l * CH + 8 + h, :, :, q * 256:(q + 1) * 256],
                     wd.at[:, q, :, h * 256:(h + 1) * 256])

    def need_down(l):
        need(*[("d", l, h, q) for h in range(4) for q in range(2)])

    def load_out(l):
        for hh in range(2):
            load(("o", l, hh), wg.at[l * CH + 3, :, hh * 32:(hh + 1) * 32, :], wo.at[:, :, hh * 512:(hh + 1) * 512])

    top = layers - 1
    load(("sec", top), sec_i.at[top], sec)
    load_down(top)
    load(("gp", top), gp_i.at[top], gp)
    load(("wu", top), wg.at[pl.ds(top * CH + 4, 4)], wu)
    load(("hidt", top), ht_i.at[top], hidt)
    load(("ngt", top), nt_i.at[top], ngt)
    load(("mix", top), mix_i.at[top], mix)
    load_out(top)
    load(("attt", top), attt_i.at[top], attt)
    load(("qkv", top), qkv_i.at[top], qkv)
    load(("lse", top), lse_i.at[top], lse)
    load(("wqkv", top), wg.at[pl.ds(top * CH, 3)], wqkv)
    load(("xt", top), xt_i.at[top], xt)

    order = []
    for l in reversed(range(layers)):
        order += [l * CH + k for k in (8, 9, 10, 11, 4, 5, 6, 7, 3, 0, 1, 2)]

    def put(k, src, sem):
        l, k = k // CH, k % CH
        if k < 3:
            pairs = [(src, (gq_o, gk_o, gv_o)[k].at[l])]
        elif k == 3:
            pairs = [(src.at[hh * 32:(hh + 1) * 32], go_o.at[l, :, hh * 512:(hh + 1) * 512]) for hh in range(2)]
        elif k < 8:
            pairs = [(src, gu_o.at[l, :, (k - 4) * 512:(k - 3) * 512])]
        else:
            h = k - 8
            pairs = [(src.at[:, q * 256:(q + 1) * 256], gd_o.at[l, q * 64:(q + 1) * 64, h * 256:(h + 1) * 256])
                     for q in range(2)]
        return [pltpu.make_async_copy(a, b, sem.at[i]) for i, (a, b) in enumerate(pairs)]

    rs = Scatter(p, order, grads, r1, r2, r3, stage, put, g_send, g_recv, o_sem)
    p.greet()
    g[...] = cot[...].astype(F32)
    vacc[...] = jnp.zeros_like(vacc)
    def bias_rows(i, carry):
        r = pl.ds(pl.multiple_of(i * 64, 64), 64)
        bias[r, :] = jnp.where(segc[r, :] == segr[...], 0.0, NEG)
        return carry
    lax.fori_loop(0, group // 64, bias_rows, 0)

    def give_rows(ref, index):
        return remote(ref, ref, x_send.at[index], x_recv.at[index], p.peer)

    ones = jnp.ones((8, group), BF)
    half_lane = lax.broadcasted_iota(jnp.int32, (1, 128), 1) < HEAD
    first_half = jnp.where(half_lane, 1.0, 0.0).astype(BF)
    second_half = jnp.where(half_lane, 0.0, 1.0).astype(BF)
    scale = HEAD ** -0.5

    def norm_back(z_ref, extra, gain_row, shift_row, out_row, dest):
        gain = vec[gain_row:gain_row + 1, 0:1024]

        def some(i, carry):
            sg, ss, so = carry
            r = pl.ds(pl.multiple_of(i * 32, 32), 32)
            zz = z_ref[r, :]
            mean = jnp.mean(zz, axis=-1, keepdims=True)
            cent = zz - mean
            var = jnp.mean(cent * cent, axis=-1, keepdims=True)
            inv = lax.rsqrt(var + EPS)
            hat = cent * inv
            up = g[r, :] if extra is None else dz[r, :] + extra[r, :].astype(F32)
            gg = up * gain
            m1 = jnp.mean(gg, axis=-1, keepdims=True)
            m2 = jnp.mean(gg * hat, axis=-1, keepdims=True)
            d = inv * (gg - m1 - hat * m2)
            dz[r, :] = d
            dest[pl.ds(pl.multiple_of(x * rows + i * 32, 32), 32), :] = d.astype(BF)
            fold = lambda v: jnp.sum(v.reshape(4, 8, 1024), axis=0)
            return sg + fold(up * hat), ss + fold(up), so + fold(d)
        zero = jnp.zeros((8, 1024), F32)
        sg, ss, so = lax.fori_loop(0, rows // 32, some, (zero, zero, zero))
        vacc[gain_row:gain_row + 1, :] = jnp.sum(sg, axis=0, keepdims=True)
        vacc[shift_row:shift_row + 1, :] = jnp.sum(ss, axis=0, keepdims=True)
        vacc[out_row:out_row + 1, :] = jnp.sum(so, axis=0, keepdims=True)

    def hidden_back(l, r):
        def block(nb, carry):
            cols = pl.ds(pl.multiple_of(nb * 256, 256), 256)
            w = wd[pl.ds(nb * 2, 2)].reshape(256, -1)
            dpre[r, cols] = (nt(fg[l, r, :], w) * gp[r, cols].astype(F32)).astype(BF)
            return carry
        lax.fori_loop(0, 8, block, 0)

    def up_back(r, nb):
        w = [wu[j, nb * 4:(nb + 1) * 4].reshape(256, 512) for j in range(4)]
        return sum(nt(dpre[r, j * 512:(j + 1) * 512], w[j]) for j in range(4))

    def in_back(r, nb):
        w = [wqkv[m, nb * 4:(nb + 1) * 4].reshape(256, 512) for m in range(3)]
        return sum(nt(dqkv[m, r, :], w[m]) for m in range(3))

    def grad_down():
        def block(mb, carry):
            res = nn(hidt[pl.ds(pl.multiple_of(mb * 256, 256), 256), :], fg[l]).astype(BF).reshape(2, 2, 64, 1024)
            for h in range(4):
                for q in range(2):
                    grads[8 + h, pl.ds(mb * 2, 2), :, q * 256:(q + 1) * 256] = res[:, q, :, h * 256:(h + 1) * 256]
            return carry
        lax.fori_loop(0, 8, block, 0)

    def grad_cols(slot, lhs, rhs, mb):
        r = slice(mb * 256, (mb + 1) * 256)
        grads[slot, mb * 4:(mb + 1) * 4] = nn(lhs[r, :], rhs).astype(BF).reshape(4, 64, 512)

    def grad_out():
        for mb in range(2):
            res = nn(attt[mb * 256:(mb + 1) * 256, :], ag[l]).astype(BF).reshape(8, 32, 1024)
            for hh in range(2):
                grads[3, mb * 8:(mb + 1) * 8, hh * 32:(hh + 1) * 32, :] = res[:, :, hh * 512:(hh + 1) * 512]

    def attend_back(first, last):
        def pair(hp, carry):
            lanes = pl.ds(pl.multiple_of(hp * 128, 128), 128)
            q128, k128, v128 = qkv[0, :, lanes], qkv[1, :, lanes], qkv[2, :, lanes]
            o128 = datt[:, lanes]
            k_t = k128.T * scale
            d_k = d_v = None
            d_q = []
            for half in range(2):
                m = second_half if half else first_half
                work[0] = nt(k128 * (m * scale), q128)
                work[1] = nt(v128 * m, o128)
                l_row = lse[pl.ds(hp * 2 + half, 1), :]

                def some(i, dots):
                    r = pl.ds(pl.multiple_of(i * 32, 32), 32)
                    e = jnp.exp(work[0, r, :] + bias[r, :] - l_row)
                    work[0, r, :] = e
                    prob[0, r, :] = e.astype(BF)
                    return dots + jnp.sum((e * work[1, r, :]).reshape(4, 8, group), axis=0)
                dots = lax.fori_loop(0, group // 32, some, jnp.zeros((8, group), F32))
                r_row = jnp.sum(dots, axis=0, keepdims=True)

                def more(i, c):
                    r = pl.ds(pl.multiple_of(i * 32, 32), 32)
                    prob[1, r, :] = (work[0, r, :] * (work[1, r, :] - r_row)).astype(BF)
                    return c
                lax.fori_loop(0, group // 32, more, 0)
                dv_half = nn(prob[0], o128 * m)
                dk_half = nn(prob[1], q128 * m)
                d_v = dv_half if half == 0 else d_v + dv_half
                d_k = dk_half if half == 0 else d_k + dk_half
                d_q.append(nn(k_t[half * HEAD:(half + 1) * HEAD], prob[1]))
            dqkv[0, :, lanes] = jnp.concatenate(d_q, axis=0).T.astype(BF)
            dqkv[1, :, lanes] = (d_k * scale).astype(BF)
            dqkv[2, :, lanes] = d_v.astype(BF)
            return carry
        lax.fori_loop(first, last, pair, 0)

    for l in reversed(range(layers)):
        base = (layers - 1 - l) * 4
        need(("sec", l))
        norm_back(sec, None, l * 2 + 1, 4 + l * 4 + 3, 4 + l * 4 + 2, fg.at[l])
        give_rows(fg.at[l, mine, :], base).start()
        if l > 0:
            load(("sec", l - 1), sec_i.at[l - 1], sec)
        need_down(l)
        need(("gp", l))
        hidden_back(l, mine)
        rs.tick()
        rs.tick()
        give_rows(fg.at[l, theirs, :], base).wait_recv()
        hidden_back(l, theirs)
        if l > 0:
            load_down(l - 1)
            load(("gp", l - 1), gp_i.at[l - 1], gp)
        need(("wu", l))
        if l < top:
            give_rows(sbuf, base - 1).wait_send()
        for nb in range(4):
            sbuf[:, nb * 256:(nb + 1) * 256] = up_back(theirs, nb).astype(BF)
        send = remote(sbuf, rbuf.at[l * 2], x_send.at[base + 1], x_recv.at[base + 1], p.peer)
        send.start()
        need(("hidt", l))
        rs.free(rs.ready + 3)
        grad_down()
        if l > 0:
            load(("hidt", l - 1), ht_i.at[l - 1], hidt)
        rs.ready += 4
        rs.tick()
        for nb in range(4):
            cols = slice(nb * 256, (nb + 1) * 256)
            dz[:, cols] = dz[:, cols] + up_back(mine, nb)
        if l > 0:
            load(("wu", l - 1), wg.at[pl.ds((l - 1) * CH + 4, 4)], wu)
        need(("ngt", l))
        rs.free(rs.ready + 3)
        for j in range(4):
            for mb in range(4):
                grad_cols(4 + j, ngt, dpre[:, j * 512:(j + 1) * 512], mb)
            res = nn(ones, dpre[:, j * 512:(j + 1) * 512])
            row, col = 16 + l * 2 + j // 2, (j % 2) * 512
            vacc[row:row + 1, col:col + 512] = res[0:1]
        if l > 0:
            load(("ngt", l - 1), nt_i.at[l - 1], ngt)
        rs.ready += 4
        rs.tick()
        need(("mix", l))
        send.wait()
        norm_back(mix, rbuf.at[l * 2], l * 2, 4 + l * 4 + 1, 4 + l * 4, ag.at[l])
        give_rows(ag.at[l, mine, :], base + 2).start()
        if l > 0:
            load(("mix", l - 1), mix_i.at[l - 1], mix)
        need(("o", l, 0), ("o", l, 1))
        w_o = wo[...].reshape(heads_w, -1)
        datt[mine, :] = nt(ag[l, mine, :], w_o).astype(BF)
        rs.tick()
        rs.tick()
        give_rows(ag.at[l, theirs, :], base + 2).wait_recv()
        datt[theirs, :] = nt(ag[l, theirs, :], w_o).astype(BF)
        if l > 0:
            load_out(l - 1)
        need(("attt", l))
        rs.free(rs.ready)
        grad_out()
        rs.ready += 1
        if l > 0:
            load(("attt", l - 1), attt_i.at[l - 1], attt)
        need(("qkv", l), ("lse", l))
        attend_back(0, 2)
        rs.tick()
        attend_back(2, 4)
        rs.tick()
        if l > 0:
            load(("qkv", l - 1), qkv_i.at[l - 1], qkv)
            load(("lse", l - 1), lse_i.at[l - 1], lse)
        need(("wqkv", l))
        for nb in range(4):
            sbuf[:, nb * 256:(nb + 1) * 256] = in_back(theirs, nb).astype(BF)
        send = remote(sbuf, rbuf.at[l * 2 + 1], x_send.at[base + 3], x_recv.at[base + 3], p.peer)
        send.start()
        need(("xt", l))
        rs.free(rs.ready + 2)
        for m in range(3):
            for mb in range(4):
                grad_cols(m, xt, dqkv[m], mb)
            if m != 1:
                vacc[20 + l:21 + l, (m // 2) * 512:(m // 2) * 512 + 512] = nn(ones, dqkv[m])[0:1]
        rs.ready += 3
        rs.tick()
        for nb in range(4):
            cols = slice(nb * 256, (nb + 1) * 256)
            g[:, cols] = dz[:, cols] + in_back(mine, nb)
        if l > 0:
            load(("wqkv", l - 1), wg.at[pl.ds((l - 1) * CH, 3)], wqkv)
            load(("xt", l - 1), xt_i.at[l - 1], xt)
        rs.tick()
        send.wait_recv()
        g[...] = g[...] + rbuf[l * 2 + 1].astype(F32)
    end = pltpu.make_async_copy(g, grad_o, e_sem.at[0])
    end.start()
    s_x = remote(vacc.at[0:16], vx, v_send.at[0], v_recv.at[0], p.peer)
    s_x.start()
    rs.tick()
    s_x.wait()
    vacc[0:16] = vacc[0:16] + vx[...]
    s_c = remote(vacc, vc, v_send.at[1], v_recv.at[1], p.twin)
    s_c.start()
    s_c.wait()
    vacc[...] = vacc[...] + vc[...]
    s_y = remote(vacc, vy, v_send.at[2], v_recv.at[2], p.side)
    s_y.start()
    rs.tick()
    s_y.wait()
    vacc[...] = vacc[...] + vy[...]
    s_z = [remote(vacc, vz.at[i - 1], v_send.at[2 + i], v_recv.at[2 + i], p.far(i)) for i in range(1, depth)]
    for copy in s_z:
        copy.start()
    rs.tick()
    for copy in s_z:
        copy.wait()
    total = vacc[...]
    for i in range(depth - 1):
        total = total + vz[i]
    vc[...] = total
    last = pltpu.make_async_copy(vc, vsum_o, e_sem.at[1])
    last.start()
    rs.finish()
    send.wait_send()
    for l in range(layers):
        base = (layers - 1 - l) * 4
        give_rows(fg.at[l, mine, :], base).wait_send()
        give_rows(ag.at[l, mine, :], base + 2).wait_send()
    end.wait()
    last.wait()


def backward_call(depth, layers, rows, vec, cot, segc, segr, wg, saved):
    group, hw, fh = 2 * rows, 512, 2048
    vm = pltpu.VMEM
    dp = depth * 4
    n = layers * CH
    slots = 4
    shapes = [(rows, 1024), (24, 1024), (layers, 64, hw), (layers, 64, hw), (layers, 64, hw), (layers, 32, 1024),
              (layers, 64, fh), (layers, 128, 1024)]
    scratch = [vm((CH, dp, 64, 512), BF), vm((slots, depth, 2, 64, 512), BF), vm((slots, depth, 64, 512), BF),
               vm((slots, depth - 1, 64, 512), BF), vm((2, 64, 512), F32),
               vm((3, dp, 64, 512), BF), vm((dp, 32, 1024), BF), vm((4, dp, 64, 512), BF), vm((dp, 2, 64, 1024), BF)]
    scratch += [vm(s.shape[1:], s.dtype) for s in saved]
    scratch += [vm((group, fh), BF), vm((layers, group, 1024), BF), vm((layers, group, 1024), BF),
                vm((2 * layers, rows, 1024), BF), vm((rows, 1024), BF), vm((rows, 1024), F32), vm((rows, 1024), F32),
                vm((3, group, hw), BF), vm((group, hw), BF), vm((2, group, group), F32), vm((2, group, group), BF),
                vm((group, group), F32), vm((24, 1024), F32), vm((16, 1024), F32),
                vm((24, 1024), F32), vm((24, 1024), F32), vm((depth - 1, 24, 1024), F32)]
    dma = pltpu.SemaphoreType.DMA
    scratch += [dma((n, depth + 1)), dma((n, depth + 1)), dma((4 * layers,)), dma((4 * layers,)),
                dma((depth + 2,)), dma((depth + 2,)), dma((24 * layers,)), dma((2, 2)), dma((2,))]
    full = pl.BlockSpec(memory_space=pltpu.VMEM)
    hbm = pl.BlockSpec(memory_space=pl.ANY)
    return pl.pallas_call(
        functools.partial(bwd_kernel, depth, layers),
        out_shape=[jax.ShapeDtypeStruct(s, F32) for s in shapes],
        in_specs=[full] * 4 + [hbm] * (1 + len(saved)),
        out_specs=[hbm] * len(shapes),
        scratch_shapes=scratch,
        compiler_params=pltpu.CompilerParams(collective_id=2, has_side_effects=True, vmem_limit_bytes=63 * 2**20),
        cost_estimate=pl.CostEstimate(flops=28 * 10**9, bytes_accessed=60 * 10**6, transcendentals=0),
    )(vec, cot, segc, segr, wg, *saved)


def pack(w_query, w_key, w_value, w_out, w_up, w_down):
    layers = w_query.shape[0]
    o = w_out.reshape(layers, 1, 32, 2, 512).transpose(0, 1, 3, 2, 4).reshape(layers, 1, 64, 512)
    u = w_up.reshape(layers, 64, 4, 512).transpose(0, 2, 1, 3)
    d = w_down.reshape(layers, 2, 64, 4, 256).transpose(0, 3, 2, 1, 4).reshape(layers, 4, 64, 512)
    parts = [w_query[:, None], w_key[:, None], w_value[:, None], o, u, d]
    return jnp.concatenate(parts, axis=1).reshape(layers * CH, 64, 512)


def pack_vectors(qv_bias, up_bias, norm_gain, shift_bias):
    layers = qv_bias.shape[0]
    dp, x = lax.axis_index("dp"), lax.axis_index("tensor")

    def spread(rows32, slot):
        tiled = jnp.tile(rows32, (1, 4))
        lane = lax.broadcasted_iota(jnp.int32, tiled.shape, 1) // 32
        return jnp.where(lane == slot, tiled, 0.0)

    full = jnp.concatenate([norm_gain.reshape(layers * 2, 32), shift_bias.reshape(layers * 4, 32)])
    full = spread(full, (dp * 2 + x) % 4)
    half = spread(qv_bias.astype(F32).reshape(layers * 2, 32), dp % 4)
    out = jnp.zeros((32, 128), F32)
    out = out.at[0:layers * 6].set(full)
    out = out.at[16:16 + layers * 2].set(half)
    return out.at[24:24 + layers].set(up_bias.astype(F32))


def on_device(
    tokens,
    cotangent,
    segment_ids,
    w_query,
    w_key,
    w_value,
    w_out,
    w_up,
    w_down,
    qv_bias,
    up_bias,
    norm_gain,
    shift_bias,
):
    layers = w_query.shape[0]
    rows = tokens.shape[0]
    depth = lax.axis_size("dp") // 4
    wp = pack(w_query, w_key, w_value, w_out, w_up, w_down)
    vp = pack_vectors(qv_bias, up_bias, norm_gain, shift_bias)
    segc, segr = segment_ids[:, None], segment_ids[None, :]
    wg, vec, out, *saved = forward_call(depth, layers, rows, wp, vp, tokens, segc, segr)
    grad, vsum, g_q, g_k, g_v, g_o, g_u, g_d = backward_call(depth, layers, rows, vec, cotangent, segc, segr, wg, saved)
    dp, x = lax.axis_index("dp"), lax.axis_index("tensor")
    gains = lax.dynamic_slice_in_dim(vsum[0:layers * 6], (dp * 2 + x) * 32, 32, 1)
    g_qv = lax.dynamic_slice_in_dim(vsum[20:20 + layers].reshape(layers, 2, 512), dp * 32, 32, 2)
    g_ub = lax.dynamic_slice_in_dim(vsum[16:16 + 2 * layers].reshape(layers, 2048), dp * 128, 128, 1)
    return (
        out,
        grad,
        g_q,
        g_k,
        g_v,
        g_o,
        g_u,
        g_d,
        g_qv,
        g_ub,
        gains[0:layers * 2].reshape(layers, 2, 32),
        gains[layers * 2:].reshape(layers, 4, 32),
    )


def on_any_mesh(
    tokens,
    cotangent,
    segment_ids,
    w_query,
    w_key,
    w_value,
    w_out,
    w_up,
    w_down,
    qv_bias,
    up_bias,
    norm_gain,
    shift_bias,
):
    layers = w_query.shape[0]
    group = segment_ids.shape[0]
    seq = min(LEN, group)
    segs = segment_ids.reshape(group // seq, seq)
    stream = tokens.astype(jnp.float32)
    kept_all = []
    mats_all = []
    vecs_all = []
    for layer in range(layers):
        mats = (
            lax.all_gather(w_query[layer], "dp", axis=0, tiled=True),
            lax.all_gather(w_key[layer], "dp", axis=0, tiled=True),
            lax.all_gather(w_value[layer], "dp", axis=0, tiled=True),
            lax.all_gather(w_out[layer], "dp", axis=0, tiled=True),
            lax.all_gather(w_up[layer], "dp", axis=0, tiled=True),
            lax.all_gather(w_down[layer], "dp", axis=0, tiled=True),
            lax.all_gather(qv_bias[layer], "dp", axis=1, tiled=True),
            lax.all_gather(up_bias[layer], "dp", axis=0, tiled=True),
        )
        vecs = (
            lax.all_gather(norm_gain[layer], ("dp", "tensor"), axis=1, tiled=True),
            lax.all_gather(shift_bias[layer], ("dp", "tensor"), axis=1, tiled=True),
        )
        stream, kept = forward_layer(stream, mats, vecs, segs, seq)
        kept_all.append(kept)
        mats_all.append(mats)
        vecs_all.append(vecs)
    grad = cotangent.astype(jnp.float32)
    mat_shards = [None] * layers
    vec_shards = [None] * layers
    for layer in reversed(range(layers)):
        mats = (
            lax.all_gather(w_query[layer], "dp", axis=0, tiled=True),
            lax.all_gather(w_key[layer], "dp", axis=0, tiled=True),
            lax.all_gather(w_value[layer], "dp", axis=0, tiled=True),
            lax.all_gather(w_out[layer], "dp", axis=0, tiled=True),
            lax.all_gather(w_up[layer], "dp", axis=0, tiled=True),
            lax.all_gather(w_down[layer], "dp", axis=0, tiled=True),
            lax.all_gather(qv_bias[layer], "dp", axis=1, tiled=True),
            lax.all_gather(up_bias[layer], "dp", axis=0, tiled=True),
        )
        grad, mat_grads, vec_grads = backward_layer(
            grad, mats, vecs_all[layer], kept_all[layer], segs, seq
        )
        g_q, g_k, g_v, g_o, g_u, g_d, g_qv, g_ub = mat_grads
        mat_shards[layer] = (
            lax.psum_scatter(
                g_q.astype(jnp.bfloat16), "dp", scatter_dimension=0, tiled=True
            ).astype(jnp.float32),
            lax.psum_scatter(
                g_k.astype(jnp.bfloat16), "dp", scatter_dimension=0, tiled=True
            ).astype(jnp.float32),
            lax.psum_scatter(
                g_v.astype(jnp.bfloat16), "dp", scatter_dimension=0, tiled=True
            ).astype(jnp.float32),
            lax.psum_scatter(
                g_o.astype(jnp.bfloat16), "dp", scatter_dimension=0, tiled=True
            ).astype(jnp.float32),
            lax.psum_scatter(
                g_u.astype(jnp.bfloat16), "dp", scatter_dimension=0, tiled=True
            ).astype(jnp.float32),
            lax.psum_scatter(
                g_d.astype(jnp.bfloat16), "dp", scatter_dimension=0, tiled=True
            ).astype(jnp.float32),
            lax.psum_scatter(
                g_qv.astype(jnp.bfloat16), "dp", scatter_dimension=1, tiled=True
            ).astype(jnp.float32),
            lax.psum_scatter(
                g_ub.astype(jnp.bfloat16), "dp", scatter_dimension=0, tiled=True
            ).astype(jnp.float32),
        )
        g_gain, g_shift = vec_grads
        vec_shards[layer] = (
            lax.psum_scatter(g_gain, ("dp", "tensor"), scatter_dimension=1, tiled=True),
            lax.psum_scatter(g_shift, ("dp", "tensor"), scatter_dimension=1, tiled=True),
        )

    def stacked(index, source):
        return jnp.stack([entry[index] for entry in source])

    return (
        stream,
        grad,
        stacked(0, mat_shards),
        stacked(1, mat_shards),
        stacked(2, mat_shards),
        stacked(3, mat_shards),
        stacked(4, mat_shards),
        stacked(5, mat_shards),
        stacked(6, mat_shards),
        stacked(7, mat_shards),
        stacked(0, vec_shards),
        stacked(1, vec_shards),
    )


def solution(mesh):
    in_specs = (
        P(("dp", "tensor"), None),
        P(("dp", "tensor"), None),
        P("dp"),
        P(None, "dp", "tensor"),
        P(None, "dp", "tensor"),
        P(None, "dp", "tensor"),
        P(None, ("tensor", "dp"), None),
        P(None, "dp", "tensor"),
        P(None, ("tensor", "dp"), None),
        P(None, None, ("tensor", "dp")),
        P(None, ("tensor", "dp")),
        P(None, None, ("dp", "tensor")),
        P(None, None, ("dp", "tensor")),
    )
    out_specs = (
        P(("dp", "tensor"), None),
        P(("dp", "tensor"), None),
        P(None, "dp", "tensor"),
        P(None, "dp", "tensor"),
        P(None, "dp", "tensor"),
        P(None, ("tensor", "dp"), None),
        P(None, "dp", "tensor"),
        P(None, ("tensor", "dp"), None),
        P(None, None, ("tensor", "dp")),
        P(None, ("tensor", "dp")),
        P(None, None, ("dp", "tensor")),
        P(None, None, ("dp", "tensor")),
    )
    small = mesh.shape["tensor"] == 2 and mesh.shape["dp"] == 16
    return jax.shard_map(
        on_device if small else on_any_mesh, mesh=mesh, in_specs=in_specs, out_specs=out_specs, check_vma=False
    )
```

```python
import functools
import math

import jax
import jax.numpy as jnp
from jax import lax
from jax.experimental import pallas as pl
from jax.experimental.pallas import tpu as pltpu
from jax.sharding import PartitionSpec as P

HEAD = 64
LEN = 512


EPS = 1e-06
NEG = -1e30


def layer_norm(z, gain, shift):
    mean = jnp.mean(z, axis=-1, keepdims=True)
    cent = z - mean
    var = jnp.mean(cent * cent, axis=-1, keepdims=True)
    return cent * lax.rsqrt(var + EPS) * gain + shift


def gelu_exact(pre):
    return jax.nn.gelu(pre, approximate=False)


def inner(left, right):
    return lax.dot_general(
        left, right, (((0,), (0,)), ((), ())), preferred_element_type=jnp.float32
    )


def times_back(left, right):
    return lax.dot_general(
        left, right, (((1,), (1,)), ((), ())), preferred_element_type=jnp.float32
    )


def gather_rows(rows):
    return lax.all_gather(rows, "tensor", axis=0, tiled=True)


def gather_grads(rows):
    return lax.all_gather(rows, "tensor", axis=0, tiled=True)


def sum_rows(term, rows):
    return lax.psum_scatter(
        term(jnp.int32(0), lax.axis_size("tensor") * rows).astype(jnp.bfloat16),
        "tensor",
        scatter_dimension=0,
        tiled=True,
    ).astype(jnp.float32)


def sum_grads(term, rows):
    return lax.psum_scatter(
        term(jnp.int32(0), lax.axis_size("tensor") * rows).astype(jnp.bfloat16),
        "tensor",
        scatter_dimension=0,
        tiled=True,
    ).astype(jnp.float32)


def allowed(segment):
    return segment[:, None] == segment[None, :]


def attend_one(args):
    query, key, value, segment = args
    scale = HEAD ** (-0.5)
    scores = jnp.einsum("qhd,khd->hqk", query, key, preferred_element_type=jnp.float32) * scale
    scores = jnp.where(allowed(segment)[None], scores, NEG)
    top = jnp.max(scores, axis=-1, keepdims=True)
    total = top + jnp.log(jnp.sum(jnp.exp(scores - top), axis=-1, keepdims=True))
    probs = jnp.exp(scores - total).astype(jnp.bfloat16)
    result = jnp.einsum("hqk,khd->qhd", probs, value, preferred_element_type=jnp.float32)
    return (result.astype(jnp.bfloat16), total[..., 0])


def attend_back(args):
    query, key, value, segment, total, d_att = args
    scale = HEAD ** (-0.5)
    scores = jnp.einsum("qhd,khd->hqk", query, key, preferred_element_type=jnp.float32) * scale
    scores = jnp.where(allowed(segment)[None], scores, NEG)
    probs = jnp.exp(scores - total[..., None])
    d_probs = jnp.einsum("qhd,khd->hqk", d_att, value, preferred_element_type=jnp.float32)
    row_dot = jnp.sum(d_probs * probs, axis=-1, keepdims=True)
    d_scores = (probs * (d_probs - row_dot)).astype(jnp.bfloat16)
    d_query = (
        jnp.einsum("hqk,khd->qhd", d_scores, key, preferred_element_type=jnp.float32) * scale
    ).astype(jnp.bfloat16)
    d_key = (
        jnp.einsum("hqk,qhd->khd", d_scores, query, preferred_element_type=jnp.float32) * scale
    ).astype(jnp.bfloat16)
    d_value = jnp.einsum(
        "hqk,qhd->khd", probs.astype(jnp.bfloat16), d_att, preferred_element_type=jnp.float32
    ).astype(jnp.bfloat16)
    return (d_query, d_key, d_value)


def forward_layer(stream, mats, vecs, segs, seq):
    w_q, w_k, w_v, w_o, w_u, w_d, qvb, upb = mats
    gains, shifts = vecs
    seqs = segs.shape[0]
    rows = stream.shape[0]
    x_rows = gather_rows(stream.astype(jnp.bfloat16))
    query = (
        jnp.dot(x_rows, w_q, preferred_element_type=jnp.float32) + qvb[0].astype(jnp.float32)
    ).astype(jnp.bfloat16)
    key = jnp.dot(x_rows, w_k, preferred_element_type=jnp.float32).astype(jnp.bfloat16)
    value = (
        jnp.dot(x_rows, w_v, preferred_element_type=jnp.float32) + qvb[1].astype(jnp.float32)
    ).astype(jnp.bfloat16)
    width = query.shape[1]
    local_heads = width // HEAD

    def split(matrix):
        return matrix.reshape(seqs, seq, local_heads, HEAD)

    attended, totals = lax.map(attend_one, (split(query), split(key), split(value), segs))
    attended = attended.reshape(seqs * seq, width)

    def out_term(start, count):
        return jnp.dot(attended, w_o, preferred_element_type=jnp.float32)

    out_sum = sum_rows(out_term, rows)
    mixed = stream + out_sum + shifts[0]
    normed = layer_norm(mixed, gains[0], shifts[1])
    n_rows = gather_rows(normed.astype(jnp.bfloat16))
    pre = jnp.dot(n_rows, w_u, preferred_element_type=jnp.float32) + upb.astype(jnp.float32)
    hidden = gelu_exact(pre).astype(jnp.bfloat16)

    def down_term(start, count):
        return jnp.dot(hidden, w_d, preferred_element_type=jnp.float32)

    down_sum = sum_rows(down_term, rows)
    second = normed + down_sum + shifts[2]
    result = layer_norm(second, gains[1], shifts[3])
    kept = (x_rows, query, key, value, attended, totals, mixed, n_rows, pre, hidden, second)
    return (result, kept)


def backward_layer(grad, mats, vecs, kept, segs, seq):
    w_q, w_k, w_v, w_o, w_u, w_d, qvb, upb = mats
    gains, shifts = vecs
    x_rows, query, key, value, attended, totals, mixed, n_rows, pre, hidden, second = kept
    seqs = segs.shape[0]
    rows = grad.shape[0]
    width = query.shape[1]
    local_heads = width // HEAD

    def split(matrix):
        return matrix.reshape(seqs, seq, local_heads, HEAD)

    _, pull_second = jax.vjp(layer_norm, second, gains[1], shifts[3])
    d_second, d_gain_two, d_shift_two = pull_second(grad)
    d_down_bias = jnp.sum(d_second, axis=0)
    d_f = gather_grads(d_second.astype(jnp.bfloat16))
    grad_down = inner(hidden, d_f)
    d_hidden = times_back(d_f, w_d)
    _, pull_gelu = jax.vjp(gelu_exact, pre)
    d_pre = pull_gelu(d_hidden)[0].astype(jnp.bfloat16)
    grad_up = inner(n_rows, d_pre)
    d_up_bias = jnp.sum(d_pre.astype(jnp.float32), axis=0)

    def up_term(start, count):
        return times_back(d_pre, w_u)

    d_normed = d_second + sum_grads(up_term, rows)
    _, pull_first = jax.vjp(layer_norm, mixed, gains[0], shifts[1])
    d_mixed, d_gain_one, d_shift_one = pull_first(d_normed)
    d_out_bias = jnp.sum(d_mixed, axis=0)
    d_a = gather_grads(d_mixed.astype(jnp.bfloat16))
    grad_out = inner(attended, d_a)
    d_att = times_back(d_a, w_o).astype(jnp.bfloat16)
    d_query, d_key, d_value = lax.map(
        attend_back, (split(query), split(key), split(value), segs, totals, split(d_att))
    )
    d_query = d_query.reshape(seqs * seq, width)
    d_key = d_key.reshape(seqs * seq, width)
    d_value = d_value.reshape(seqs * seq, width)
    grad_q = inner(x_rows, d_query)
    grad_k = inner(x_rows, d_key)
    grad_v = inner(x_rows, d_value)
    d_qv = jnp.stack(
        [jnp.sum(d_query.astype(jnp.float32), axis=0), jnp.sum(d_value.astype(jnp.float32), axis=0)]
    )

    def in_term(start, count):
        part = times_back(d_query, w_q)
        part = part + times_back(d_key, w_k)
        return part + times_back(d_value, w_v)

    d_stream = d_mixed + sum_grads(in_term, rows)
    mat_grads = (grad_q, grad_k, grad_v, grad_out, grad_up, grad_down, d_qv, d_up_bias)
    vec_grads = (
        jnp.stack([d_gain_one, d_gain_two]),
        jnp.stack([d_out_bias, d_shift_one, d_down_bias, d_shift_two]),
    )
    return (d_stream, mat_grads, vec_grads)


MESH = pl.DeviceIdType.MESH
BF = jnp.bfloat16
F32 = jnp.float32
AHEAD = 6
KEPT = ("vec", "xt", "qkv", "attt", "lse", "mix", "ngt", "hidt", "gp", "sec", "out")
CH = 12


def nt(left, right):
    return lax.dot_general(left, right, (((1,), (1,)), ((), ())), preferred_element_type=F32)


def nn(left, right):
    return lax.dot_general(left, right, (((1,), (0,)), ((), ())), preferred_element_type=F32)


def tn(left, right):
    return lax.dot_general(left, right, (((0,), (0,)), ((), ())), preferred_element_type=F32)


def remote(src, dst, send_sem, recv_sem, device):
    return pltpu.make_async_remote_copy(
        src_ref=src, dst_ref=dst, send_sem=send_sem, recv_sem=recv_sem, device_id=device, device_id_type=MESH
    )


class Place:
    def __init__(self, depth):
        self.depth = depth
        self.dp = lax.axis_index("dp")
        self.x = lax.axis_index("tensor")
        self.z = self.dp // 4
        self.y = (self.dp // 2) % 2
        self.c = self.dp % 2

    def at(self, z, y, c):
        return {"dp": z * 4 + y * 2 + c, "tensor": self.x}

    def far(self, step):
        return self.at((self.z + step) % self.depth, self.y, self.c)

    def before(self, step):
        return (self.z + self.depth - step) % self.depth

    @property
    def side(self):
        return self.at(self.z, 1 - self.y, self.c)

    @property
    def twin(self):
        return self.at(self.z, self.y, 1 - self.c)

    @property
    def peer(self):
        return {"dp": self.dp, "tensor": 1 - self.x}

    def greet(self):
        barrier = pltpu.get_barrier_semaphore()
        partners = [self.far(i) for i in range(1, self.depth)] + [self.side, self.twin, self.peer]
        for device in partners:
            pl.semaphore_signal(barrier, inc=1, device_id=device, device_id_type=MESH)
        pl.semaphore_wait(barrier, len(partners))


class Gather:
    def __init__(self, place, wg, keep, send, recv, total):
        self.p, self.wg, self.keep, self.send, self.recv, self.total = place, wg, keep, send, recv, total
        self.view = wg.reshape(wg.shape[0], place.depth, 2, 2, *wg.shape[2:])
        self.time = 0
        self.have = 0

    def far(self, k, i):
        p = self.p
        return remote(self.wg.at[k, p.dp], self.wg.at[k, p.dp], self.send.at[k, i - 1], self.recv.at[k, i - 1], p.far(i))

    def far_in(self, k, i):
        p = self.p
        ref = self.wg.at[k, p.before(i) * 4 + p.y * 2 + p.c]
        return remote(ref, ref, self.send.at[k, i - 1], self.recv.at[k, i - 1], p.far(i))

    def side(self, k, y):
        p, d = self.p, self.p.depth - 1
        ref = self.view.at[k, :, y, p.c]
        return remote(ref, ref, self.send.at[k, d], self.recv.at[k, d], p.side)

    def twin(self, k, c):
        p, d = self.p, self.p.depth
        ref = self.view.at[k, :, :, c]
        return remote(ref, ref, self.send.at[k, d], self.recv.at[k, d], p.twin)

    def begin(self, ahead):
        self.ahead = ahead
        for k in range(ahead):
            for i in range(1, self.p.depth):
                self.far(k, i).start()

    def tick(self):
        t, n = self.time, self.total
        if t >= n + 3:
            return
        if t + self.ahead < n:
            for i in range(1, self.p.depth):
                self.far(t + self.ahead, i).start()
        if t < n:
            for i in range(1, self.p.depth):
                self.far_in(t, i).wait_recv()
            self.side(t, self.p.y).start()
        if 1 <= t <= n:
            self.side(t - 1, 1 - self.p.y).wait_recv()
            self.twin(t - 1, self.p.c).start()
        if t >= 2 and t - 2 < n:
            self.twin(t - 2, 1 - self.p.c).wait_recv()
            self.have = t - 1
            self.keep(t - 2)
        self.time += 1

    def until(self, count):
        while self.have < count:
            self.tick()

    def finish(self):
        self.until(self.total)
        for k in range(self.total):
            for i in range(1, self.p.depth):
                self.far(k, i).wait_send()
            self.side(k, self.p.y).wait_send()
            self.twin(k, self.p.c).wait_send()


def norm_rows(z, gain, shift):
    mean = jnp.mean(z, axis=-1, keepdims=True)
    cent = z - mean
    var = jnp.mean(cent * cent, axis=-1, keepdims=True)
    return cent * lax.rsqrt(var + EPS) * gain + shift


def fwd_kernel(depth, layers, vp, tok, segc, segr, w_query, w_key, w_value, w_out, w_up, w_down,
               wg_o, vec_o, out_o, xt_o, qkv_o, attt_o, lse_o, mix_o, nt_o, ht_o, gp_o, sec_o,
               wg, vg, vec, stream, normed, bias, work, prob, xt, qkv, attt, lse, mix, ngt, hidt, gp, sec,
               xg, ng, hid, att, sbuf, rbuf,
               w_send, w_recv, v_send, v_recv, d_send, d_recv, x_send, x_recv, o_sem, k_sem):
    p = Place(depth)
    x = p.x
    rows = tok.shape[0]
    group = 2 * rows
    heads_w = qkv.shape[-1]
    mine = pl.ds(pl.multiple_of(x * rows, rows), rows)
    theirs = pl.ds(pl.multiple_of((1 - x) * rows, rows), rows)
    n_chunks = layers * CH

    def keep_chunk(k):
        pltpu.make_async_copy(wg.at[k], wg_o.at[k], k_sem.at[k]).start()

    gat = Gather(p, wg, keep_chunk, w_send, w_recv, n_chunks)
    for l in range(layers):
        c0 = l * CH
        for m, w in enumerate((w_query, w_key, w_value)):
            wg[c0 + m, p.dp] = w[l]
        for hh in range(2):
            wg[c0 + 3, p.dp, hh * 32:(hh + 1) * 32, :] = w_out[l, :, hh * 512:(hh + 1) * 512]
        for j in range(4):
            wg[c0 + 4 + j, p.dp] = w_up[l, :, j * 512:(j + 1) * 512]
            for q in range(2):
                wg[c0 + 8 + j, p.dp, :, q * 256:(q + 1) * 256] = w_down[l, q * 64:(q + 1) * 64, j * 256:(j + 1) * 256]
    vg[x, p.z, p.y, p.c] = vp[...]
    xg[0, mine, :] = tok[...]
    p.greet()

    def give_rows(ref, index):
        return remote(ref, ref, x_send.at[index], x_recv.at[index], p.peer)

    v_far = [remote(vg.at[x, p.z, p.y, p.c], vg.at[x, p.z, p.y, p.c], v_send.at[i - 1], v_recv.at[i - 1], p.far(i))
             for i in range(1, depth)]
    for copy in v_far:
        copy.start()
    give_rows(xg.at[0, mine, :], 0).start()
    gat.begin(AHEAD)

    stream[...] = tok[...].astype(F32)
    def bias_rows(i, _):
        r = pl.ds(pl.multiple_of(i * 64, 64), 64)
        bias[r, :] = jnp.where(segc[r, :] == segr[...], 0.0, NEG)
        return _
    lax.fori_loop(0, group // 64, bias_rows, 0)

    for copy in v_far:
        copy.wait_recv()
    v_side = remote(vg.at[x, :, p.y, p.c], vg.at[x, :, p.y, p.c], v_send.at[depth - 1], v_recv.at[depth - 1], p.side)
    v_side.start()
    v_side.wait_recv()
    v_twin = remote(vg.at[x, :, :, p.c], vg.at[x, :, :, p.c], v_send.at[depth], v_recv.at[depth], p.twin)
    v_twin.start()
    v_twin.wait_recv()
    v_peer = remote(vg.at[x], vg.at[x], v_send.at[depth + 1], v_recv.at[depth + 1], p.peer)
    v_peer.start()
    gat.tick()
    v_peer.wait_recv()
    for z in range(depth):
        for y in range(2):
            b = (z * 2 + y) * 128
            vec[0:16, b:b + 128] = (vg[0, z, y, 0, 0:16] + vg[0, z, y, 1, 0:16]
                                    + vg[1, z, y, 0, 0:16] + vg[1, z, y, 1, 0:16])
    for z in range(depth):
        for_half = vg[x, z, 0, 0, 16:24] + vg[x, z, 0, 1, 16:24] + vg[x, z, 1, 0, 16:24] + vg[x, z, 1, 1, 16:24]
        vec[16:24, z * 128:(z + 1) * 128] = for_half
        for y in range(2):
            for c in range(2):
                b = (z * 4 + y * 2 + c) * 128
                vec[24:32, b:b + 128] = vg[x, z, y, c, 24:32]
    kept = {}

    def keep(name, src, dst):
        copy = pltpu.make_async_copy(src, dst, o_sem.at[KEPT.index(name)])
        copy.start()
        kept[name] = copy

    def fresh(name):
        if name in kept:
            kept.pop(name).wait()

    keep("vec", vec, vec_o)

    def give_part(l, h):
        cols = slice(h * 256, (h + 1) * 256)
        return remote(sbuf.at[:, cols], rbuf.at[l * 2 + 1, :, cols], d_send.at[l, h], d_recv.at[l, h], p.peer)

    def gain(l, i):
        r = l * 2 + i
        return vec[r:r + 1, 0:1024]

    def shift(l, i):
        r = 4 + l * 4 + i
        return vec[r:r + 1, 0:1024]

    def project(l, r):
        for m in range(3):
            w = wg[l * CH + m].reshape(-1, heads_w)
            res = nn(xg[l, r, :], w)
            if m != 1:
                b = 16 + l * 2 + (m // 2)
                res = res + vec[b:b + 1, 0:heads_w]
            qkv[m, r, :] = res.astype(BF)

    half_lane = lax.broadcasted_iota(jnp.int32, (1, 128), 1) < HEAD
    first_half = jnp.where(half_lane, 1.0, 0.0).astype(BF)
    second_half = jnp.where(half_lane, 0.0, 1.0).astype(BF)
    scale = HEAD ** -0.5

    def attend(l, first, last):
        def pair(hp, carry):
            lanes = pl.ds(pl.multiple_of(hp * 128, 128), 128)
            k128 = qkv[1, :, lanes]
            v_t = qkv[2, :, lanes].T
            for qb in range(group // 256):
                q_rows = slice(qb * 256, (qb + 1) * 256)
                q128 = qkv[0, q_rows, lanes]
                both = []
                for half in range(2):
                    k_half = k128 * ((second_half if half else first_half) * scale)
                    work[half] = nt(k_half, q128)
                    top = jnp.full((8, 256), NEG, F32)
                    for i in range(group // 64):
                        r = slice(i * 64, (i + 1) * 64)
                        s = work[half, r, :] + bias[r, q_rows]
                        work[half, r, :] = s
                        top = jnp.maximum(top, jnp.max(s.reshape(8, 8, 256), axis=0))
                    top = jnp.max(top, axis=0, keepdims=True)
                    tot = jnp.zeros((8, 256), F32)
                    for i in range(group // 64):
                        r = slice(i * 64, (i + 1) * 64)
                        e = jnp.exp(work[half, r, :] - top)
                        tot = tot + jnp.sum(e.reshape(8, 8, 256), axis=0)
                        prob[half, r, :] = e.astype(BF)
                    tot = jnp.sum(tot, axis=0, keepdims=True)
                    lse[pl.ds(hp * 2 + half, 1), q_rows] = top + jnp.log(tot)
                    res = nn(v_t[half * HEAD:(half + 1) * HEAD], prob[half])
                    both.append(res / tot)
                o_t = jnp.concatenate(both, axis=0)
                attt[lanes, q_rows] = o_t.astype(BF)
                att[q_rows, lanes] = o_t.T.astype(BF)
            return carry
        lax.fori_loop(first, last, pair, 0)

    def out_term(l, r):
        w = wg[l * CH + 3]
        w = jnp.concatenate([w[:, 0:32, :], w[:, 32:64, :]], axis=2).reshape(heads_w, -1)
        return nn(att[r, :], w)

    def flip(src, dst):
        def block(i, carry):
            c = pl.ds(pl.multiple_of(i * 256, 256), 256)
            dst[c, :] = src[:, c].T
            return carry
        lax.fori_loop(0, src.shape[1] // 256, block, 0)

    inv_sqrt2 = 2.0 ** -0.5
    inv_sqrt_2pi = (2.0 * math.pi) ** -0.5

    def up(l, j):
        b = 24 + l
        for cb in range(2):
            cols = slice(j * 512 + cb * 256, j * 512 + (cb + 1) * 256)
            w = wg[l * CH + 4 + j, :, :, cb * 256:(cb + 1) * 256].reshape(-1, 256)
            work[cb] = nn(ng[l], w) + vec[b:b + 1, cols]

            def some(i, carry):
                r = pl.ds(pl.multiple_of(i * 32, 32), 32)
                pre = work[cb, r, :]
                part = 0.5 + 0.5 * lax.erf(pre * inv_sqrt2)
                hid[r, cols] = (pre * part).astype(BF)
                gp[r, cols] = (part + pre * jnp.exp(-0.5 * pre * pre) * inv_sqrt_2pi).astype(BF)
                return carry
            lax.fori_loop(0, group // 32, some, 0)

    def down_term(l, r, h):
        w = wg[l * CH + 8 + h]
        w = jnp.stack([w[:, :, 0:256], w[:, :, 256:512]], axis=1).reshape(-1, 256)
        return nn(hid[r, :], w)

    for l in range(layers):
        c0 = l * CH
        gat.until(c0 + 3)
        fresh("qkv")
        project(l, mine)
        if l > 0:
            gat.tick()
        give_rows(xg.at[l, theirs, :], l * 4).wait_recv()
        project(l, theirs)
        keep("qkv", qkv, qkv_o.at[l])
        fresh("lse")
        fresh("attt")
        attend(l, 0, 2)
        gat.tick()
        attend(l, 2, 4)
        keep("lse", lse, lse_o.at[l])
        keep("attt", attt, attt_o.at[l])
        gat.until(c0 + 4)
        sbuf[...] = out_term(l, theirs).astype(BF)
        send = remote(sbuf, rbuf.at[l * 2], x_send.at[l * 4 + 1], x_recv.at[l * 4 + 1], p.peer)
        send.start()
        fresh("mix")
        mix[...] = stream[...] + out_term(l, mine) + shift(l, 0)
        gat.tick()
        fresh("xt")
        flip(xg.at[l], xt)
        keep("xt", xt, xt_o.at[l])
        gat.tick()
        send.wait()

        def first_norm(i, carry):
            r = pl.ds(pl.multiple_of(i * 32, 32), 32)
            mixed = mix[r, :] + rbuf[l * 2, r, :].astype(F32)
            mix[r, :] = mixed
            res = norm_rows(mixed, gain(l, 0), shift(l, 1))
            normed[r, :] = res
            ng[l, pl.ds(pl.multiple_of(x * rows + i * 32, 32), 32), :] = res.astype(BF)
            return carry
        lax.fori_loop(0, rows // 32, first_norm, 0)
        give_rows(ng.at[l, mine, :], l * 4 + 2).start()
        keep("mix", mix, mix_o.at[l])
        gat.tick()
        gat.tick()
        give_rows(ng.at[l, theirs, :], l * 4 + 2).wait_recv()
        fresh("gp")
        for j in range(4):
            gat.until(c0 + 5 + j)
            up(l, j)
            if j % 2:
                gat.tick()
        keep("gp", gp, gp_o.at[l])
        for h in range(4):
            gat.until(c0 + 9 + h)
            cols = slice(h * 256, (h + 1) * 256)
            sbuf[:, cols] = down_term(l, theirs, h).astype(BF)
            give_part(l, h).start()
            if h == 0:
                fresh("sec")
            sec[:, cols] = normed[:, cols] + down_term(l, mine, h) + shift(l, 2)[:, cols]
        fresh("ngt")
        flip(ng.at[l], ngt)
        keep("ngt", ngt, nt_o.at[l])
        fresh("hidt")
        flip(hid, hidt)
        keep("hidt", hidt, ht_o.at[l])
        for h in range(4):
            give_part(l, h).wait()

        def second_norm(i, carry):
            r = pl.ds(pl.multiple_of(i * 32, 32), 32)
            second = sec[r, :] + rbuf[l * 2 + 1, r, :].astype(F32)
            sec[r, :] = second
            res = norm_rows(second, gain(l, 1), shift(l, 3))
            stream[r, :] = res
            if l + 1 < layers:
                xg[l + 1, pl.ds(pl.multiple_of(x * rows + i * 32, 32), 32), :] = res.astype(BF)
            return carry
        lax.fori_loop(0, rows // 32, second_norm, 0)
        if l + 1 < layers:
            give_rows(xg.at[l + 1, mine, :], l * 4 + 4).start()
        keep("sec", sec, sec_o.at[l])
    keep("out", stream, out_o)
    gat.finish()
    for copy in v_far + [v_side, v_twin, v_peer]:
        copy.wait_send()
    for l in range(layers):
        give_rows(xg.at[l, mine, :], l * 4).wait_send()
        give_rows(ng.at[l, mine, :], l * 4 + 2).wait_send()
    for name in list(kept):
        fresh(name)
    for k in range(n_chunks):
        pltpu.make_async_copy(wg.at[k], wg_o.at[k], k_sem.at[k]).wait()


def forward_call(depth, layers, rows, vp, tok, segc, segr, *weights):
    group, hw, fh = 2 * rows, 512, 2048
    vm = pltpu.VMEM
    saved = [((layers, 1024, group), BF), ((layers, 3, group, hw), BF), ((layers, hw, group), BF),
             ((layers, 8, group), F32), ((layers, rows, 1024), F32), ((layers, 1024, group), BF),
             ((layers, fh, group), BF), ((layers, group, fh), BF), ((layers, rows, 1024), F32)]
    dp = depth * 4
    n = layers * CH
    out_shape = [jax.ShapeDtypeStruct((n, dp, 64, 512), BF), jax.ShapeDtypeStruct((32, 2048), F32),
                 jax.ShapeDtypeStruct((rows, 1024), F32)] + [jax.ShapeDtypeStruct(s, t) for s, t in saved]
    scratch = [vm((n, dp, 64, 512), BF), vm((2, depth, 2, 2, 32, 128), F32), vm((32, 2048), F32), vm((rows, 1024), F32), vm((rows, 1024), F32),
               vm((group, group), F32), vm((2, group, 256), F32), vm((2, group, 256), BF)]
    scratch += [vm(s[1:], t) for s, t in saved]
    scratch += [vm((layers, group, 1024), BF), vm((layers, group, 1024), BF), vm((group, fh), BF), vm((group, hw), BF)]
    scratch += [vm((rows, 1024), BF), vm((2 * layers, rows, 1024), BF)]
    dma = pltpu.SemaphoreType.DMA
    scratch += [dma((n, depth + 1)), dma((n, depth + 1)), dma((depth + 2,)), dma((depth + 2,)),
                dma((layers, 4)), dma((layers, 4)), dma((4 * layers,)), dma((4 * layers,)), dma((len(KEPT),)), dma((n,))]
    full = pl.BlockSpec(memory_space=pltpu.VMEM)
    hbm = pl.BlockSpec(memory_space=pl.ANY)
    return pl.pallas_call(
        functools.partial(fwd_kernel, depth, layers),
        out_shape=out_shape,
        in_specs=[full] * 10,
        out_specs=[hbm] * len(out_shape),
        scratch_shapes=scratch,
        compiler_params=pltpu.CompilerParams(collective_id=1, has_side_effects=True, vmem_limit_bytes=63 * 2**20),
        cost_estimate=pl.CostEstimate(flops=14 * 10**9, bytes_accessed=60 * 10**6, transcendentals=0),
    )(vp, tok, segc, segr, *weights)


class Scatter:
    def __init__(self, place, order, grads, r1, r2, r3, stage, put, send, recv, out_sem):
        self.p, self.order, self.grads, self.r1, self.r2, self.r3 = place, order, grads, r1, r2, r3
        self.stage, self.put, self.send, self.recv, self.out_sem = stage, put, send, recv, out_sem
        self.view = grads.reshape(grads.shape[0], place.depth, 2, 2, *grads.shape[2:])
        self.time = 0
        self.ready = 0
        self.total = len(order)
        self.slots = r1.shape[0]
        self.outs = {}

    def core(self, n):
        p, s, d = self.p, n % self.slots, self.p.depth - 1
        return remote(self.view.at[self.order[n] % CH, :, :, 1 - p.c], self.r1.at[s],
                      self.send.at[n, d + 1], self.recv.at[n, d + 1], p.twin)

    def side(self, n):
        p, s, d = self.p, n % self.slots, self.p.depth - 1
        return remote(self.r1.at[s, :, 1 - p.y], self.r2.at[s], self.send.at[n, d], self.recv.at[n, d], p.side)

    def far(self, n, i):
        p, s = self.p, n % self.slots
        return remote(self.r2.at[s, (p.z + i) % p.depth], self.r3.at[s, i - 1],
                      self.send.at[n, i - 1], self.recv.at[n, i - 1], p.far(i))

    def step_far(self, n):
        p, s = self.p, n % self.slots
        for i in range(1, p.depth):
            self.far(n, i).wait()
        self.side(n).wait_send()
        if n >= 2:
            for copy in self.outs[n - 2]:
                copy.wait()
        total = self.r2[s, p.z].astype(F32)
        for i in range(p.depth - 1):
            total = total + self.r3[s, i].astype(F32)
        self.stage[n % 2] = total
        self.outs[n] = self.put(self.order[n], self.stage.at[n % 2], self.out_sem.at[n % 2])
        for copy in self.outs[n]:
            copy.start()

    def step_side(self, n):
        p, s = self.p, n % self.slots
        self.side(n).wait_recv()
        self.r2[s] = self.r2[s] + self.r1[s, :, p.y]
        for i in range(1, p.depth):
            self.far(n, i).start()

    def step_core(self, n):
        p, s = self.p, n % self.slots
        self.core(n).wait()
        self.r1[s] = self.r1[s] + self.view[self.order[n] % CH, :, :, p.c]
        self.side(n).start()

    def tick(self):
        t, n = self.time, self.total
        if t >= n + 5 or (t < n and t >= self.ready):
            return
        if 5 <= t:
            self.step_far(t - 5)
        if 3 <= t < n + 3:
            self.step_side(t - 3)
        if 1 <= t < n + 1:
            self.step_core(t - 1)
        if t < n:
            self.core(t).start()
        self.time += 1

    def free(self, n):
        while self.time < n - CH + 2:
            self.tick()

    def finish(self):
        while self.time < self.total + 5:
            self.tick()
        for n in (self.total - 2, self.total - 1):
            for copy in self.outs[n]:
                copy.wait()


def bwd_kernel(depth, layers, vec, cot, segc, segr, wg, xt_i, qkv_i, attt_i, lse_i, mix_i, nt_i, ht_i, gp_i, sec_i,
               grad_o, vsum_o, gq_o, gk_o, gv_o, go_o, gu_o, gd_o,
               grads, r1, r2, r3, stage, wqkv, wo, wu, wd,
               xt, qkv, attt, lse, mix, ngt, hidt, gp, sec,
               dpre, fg, ag, rbuf, sbuf, g, dz, dqkv, datt, work, prob, bias, vacc, vx, vc, vy, vz,
               g_send, g_recv, f_send, f_recv, x_send, x_recv, v_send, v_recv, l_sem, o_sem, e_sem):
    p = Place(depth)
    x = p.x
    rows = cot.shape[0]
    group = 2 * rows
    heads_w = datt.shape[-1]
    mine = pl.ds(pl.multiple_of(x * rows, rows), rows)
    theirs = pl.ds(pl.multiple_of((1 - x) * rows, rows), rows)
    loads = {}

    def load(name, src, dst):
        copy = pltpu.make_async_copy(src, dst, l_sem.at[len(loads)])
        copy.start()
        loads[name] = copy

    def need(*names):
        for name in names:
            loads[name].wait()

    def load_down(l):
        for h in range(4):
            for q in range(2):
                load(("d", l, h, q), wg.at[l * CH + 8 + h, :, :, q * 256:(q + 1) * 256],
                     wd.at[:, q, :, h * 256:(h + 1) * 256])

    def need_down(l):
        need(*[("d", l, h, q) for h in range(4) for q in range(2)])

    def load_out(l):
        for hh in range(2):
            load(("o", l, hh), wg.at[l * CH + 3, :, hh * 32:(hh + 1) * 32, :], wo.at[:, :, hh * 512:(hh + 1) * 512])

    top = layers - 1
    load(("sec", top), sec_i.at[top], sec)
    load_down(top)
    load(("gp", top), gp_i.at[top], gp)
    load(("wu", top), wg.at[pl.ds(top * CH + 4, 4)], wu)
    load(("hidt", top), ht_i.at[top], hidt)
    load(("ngt", top), nt_i.at[top], ngt)
    load(("mix", top), mix_i.at[top], mix)
    load_out(top)
    load(("attt", top), attt_i.at[top], attt)
    load(("qkv", top), qkv_i.at[top], qkv)
    load(("lse", top), lse_i.at[top], lse)
    load(("wqkv", top), wg.at[pl.ds(top * CH, 3)], wqkv)
    load(("xt", top), xt_i.at[top], xt)

    order = []
    for l in reversed(range(layers)):
        order += [l * CH + k for k in (8, 9, 10, 11, 4, 5, 6, 7, 3, 0, 1, 2)]

    def put(k, src, sem):
        l, k = k // CH, k % CH
        if k < 3:
            pairs = [(src, (gq_o, gk_o, gv_o)[k].at[l])]
        elif k == 3:
            pairs = [(src.at[hh * 32:(hh + 1) * 32], go_o.at[l, :, hh * 512:(hh + 1) * 512]) for hh in range(2)]
        elif k < 8:
            pairs = [(src, gu_o.at[l, :, (k - 4) * 512:(k - 3) * 512])]
        else:
            h = k - 8
            pairs = [(src.at[:, q * 256:(q + 1) * 256], gd_o.at[l, q * 64:(q + 1) * 64, h * 256:(h + 1) * 256])
                     for q in range(2)]
        return [pltpu.make_async_copy(a, b, sem.at[i]) for i, (a, b) in enumerate(pairs)]

    rs = Scatter(p, order, grads, r1, r2, r3, stage, put, g_send, g_recv, o_sem)
    p.greet()
    g[...] = cot[...].astype(F32)
    vacc[...] = jnp.zeros_like(vacc)
    def bias_rows(i, carry):
        r = pl.ds(pl.multiple_of(i * 64, 64), 64)
        bias[r, :] = jnp.where(segc[r, :] == segr[...], 0.0, NEG)
        return carry
    lax.fori_loop(0, group // 64, bias_rows, 0)

    def give_rows(ref, index):
        return remote(ref, ref, x_send.at[index], x_recv.at[index], p.peer)

    def give_part(l, h, r):
        ref = fg.at[l, r, h * 256:(h + 1) * 256]
        return remote(ref, ref, f_send.at[l, h], f_recv.at[l, h], p.peer)

    ones = jnp.ones((8, group), BF)
    half_lane = lax.broadcasted_iota(jnp.int32, (1, 128), 1) < HEAD
    first_half = jnp.where(half_lane, 1.0, 0.0).astype(BF)
    second_half = jnp.where(half_lane, 0.0, 1.0).astype(BF)
    scale = HEAD ** -0.5

    def norm_back(z_ref, extra, gain_row, shift_row, out_row, dest):
        gain = vec[gain_row:gain_row + 1, 0:1024]

        def some(i, carry):
            sg, ss, so = carry
            r = pl.ds(pl.multiple_of(i * 32, 32), 32)
            zz = z_ref[r, :]
            mean = jnp.mean(zz, axis=-1, keepdims=True)
            cent = zz - mean
            var = jnp.mean(cent * cent, axis=-1, keepdims=True)
            inv = lax.rsqrt(var + EPS)
            hat = cent * inv
            up = g[r, :] if extra is None else dz[r, :] + extra[r, :].astype(F32)
            gg = up * gain
            m1 = jnp.mean(gg, axis=-1, keepdims=True)
            m2 = jnp.mean(gg * hat, axis=-1, keepdims=True)
            d = inv * (gg - m1 - hat * m2)
            dz[r, :] = d
            dest[pl.ds(pl.multiple_of(x * rows + i * 32, 32), 32), :] = d.astype(BF)
            fold = lambda v: jnp.sum(v.reshape(4, 8, 1024), axis=0)
            return sg + fold(up * hat), ss + fold(up), so + fold(d)
        zero = jnp.zeros((8, 1024), F32)
        sg, ss, so = lax.fori_loop(0, rows // 32, some, (zero, zero, zero))
        vacc[gain_row:gain_row + 1, :] = jnp.sum(sg, axis=0, keepdims=True)
        vacc[shift_row:shift_row + 1, :] = jnp.sum(ss, axis=0, keepdims=True)
        vacc[out_row:out_row + 1, :] = jnp.sum(so, axis=0, keepdims=True)

    def hidden_back(l, r):
        def block(nb, carry):
            cols = pl.ds(pl.multiple_of(nb * 256, 256), 256)
            w = wd[pl.ds(nb * 2, 2)].reshape(256, -1)
            dpre[r, cols] = (nt(fg[l, r, :], w) * gp[r, cols].astype(F32)).astype(BF)
            return carry
        lax.fori_loop(0, 8, block, 0)

    def up_back(r, nb):
        w = [wu[j, nb * 4:(nb + 1) * 4].reshape(256, 512) for j in range(4)]
        return sum(nt(dpre[r, j * 512:(j + 1) * 512], w[j]) for j in range(4))

    def in_back(r, nb):
        w = [wqkv[m, nb * 4:(nb + 1) * 4].reshape(256, 512) for m in range(3)]
        return sum(nt(dqkv[m, r, :], w[m]) for m in range(3))

    def grad_down(h):
        def block(mb, carry):
            r = pl.ds(pl.multiple_of(mb * 512, 512), 512)
            res = nn(hidt[r, :], fg[l, :, h * 256:(h + 1) * 256]).astype(BF).reshape(4, 2, 64, 256)
            for q in range(2):
                grads[8 + h, pl.ds(mb * 4, 4), :, q * 256:(q + 1) * 256] = res[:, q]
            return carry
        lax.fori_loop(0, 4, block, 0)

    def grad_cols(slot, lhs, rhs, mb):
        r = slice(mb * 256, (mb + 1) * 256)
        grads[slot, mb * 4:(mb + 1) * 4] = nn(lhs[r, :], rhs).astype(BF).reshape(4, 64, 512)

    def grad_out():
        for mb in range(2):
            res = nn(attt[mb * 256:(mb + 1) * 256, :], ag[l]).astype(BF).reshape(8, 32, 1024)
            for hh in range(2):
                grads[3, mb * 8:(mb + 1) * 8, hh * 32:(hh + 1) * 32, :] = res[:, :, hh * 512:(hh + 1) * 512]

    def attend_back(first, last):
        def pair(hp, carry):
            lanes = pl.ds(pl.multiple_of(hp * 128, 128), 128)
            q128, k128, v128 = qkv[0, :, lanes], qkv[1, :, lanes], qkv[2, :, lanes]
            o128 = datt[:, lanes]
            k_t = k128.T * scale
            d_k = d_v = None
            d_q = []
            for half in range(2):
                m = second_half if half else first_half
                work[0] = nt(k128 * (m * scale), q128)
                work[1] = nt(v128 * m, o128)
                l_row = lse[pl.ds(hp * 2 + half, 1), :]

                def some(i, dots):
                    r = pl.ds(pl.multiple_of(i * 32, 32), 32)
                    e = jnp.exp(work[0, r, :] + bias[r, :] - l_row)
                    work[0, r, :] = e
                    prob[0, r, :] = e.astype(BF)
                    return dots + jnp.sum((e * work[1, r, :]).reshape(4, 8, group), axis=0)
                dots = lax.fori_loop(0, group // 32, some, jnp.zeros((8, group), F32))
                r_row = jnp.sum(dots, axis=0, keepdims=True)

                def more(i, c):
                    r = pl.ds(pl.multiple_of(i * 32, 32), 32)
                    prob[1, r, :] = (work[0, r, :] * (work[1, r, :] - r_row)).astype(BF)
                    return c
                lax.fori_loop(0, group // 32, more, 0)
                dv_half = nn(prob[0], o128 * m)
                dk_half = nn(prob[1], q128 * m)
                d_v = dv_half if half == 0 else d_v + dv_half
                d_k = dk_half if half == 0 else d_k + dk_half
                d_q.append(nn(k_t[half * HEAD:(half + 1) * HEAD], prob[1]))
            dqkv[0, :, lanes] = jnp.concatenate(d_q, axis=0).T.astype(BF)
            dqkv[1, :, lanes] = (d_k * scale).astype(BF)
            dqkv[2, :, lanes] = d_v.astype(BF)
            return carry
        lax.fori_loop(first, last, pair, 0)

    for l in reversed(range(layers)):
        base = (layers - 1 - l) * 4
        need(("sec", l))
        norm_back(sec, None, l * 2 + 1, 4 + l * 4 + 3, 4 + l * 4 + 2, fg.at[l])
        for h in range(4):
            give_part(l, h, mine).start()
        if l > 0:
            load(("sec", l - 1), sec_i.at[l - 1], sec)
        need_down(l)
        need(("gp", l))
        hidden_back(l, mine)
        need(("hidt", l))
        for h in range(4):
            give_part(l, h, theirs).wait_recv()
            rs.free(rs.ready)
            grad_down(h)
            rs.ready += 1
            rs.tick()
        if l > 0:
            load(("hidt", l - 1), ht_i.at[l - 1], hidt)
        hidden_back(l, theirs)
        if l > 0:
            load_down(l - 1)
            load(("gp", l - 1), gp_i.at[l - 1], gp)
        need(("wu", l))
        if l < top:
            give_rows(sbuf, base - 1).wait_send()
        for nb in range(4):
            sbuf[:, nb * 256:(nb + 1) * 256] = up_back(theirs, nb).astype(BF)
        send = remote(sbuf, rbuf.at[l * 2], x_send.at[base + 1], x_recv.at[base + 1], p.peer)
        send.start()
        rs.tick()
        for nb in range(4):
            cols = slice(nb * 256, (nb + 1) * 256)
            dz[:, cols] = dz[:, cols] + up_back(mine, nb)
        if l > 0:
            load(("wu", l - 1), wg.at[pl.ds((l - 1) * CH + 4, 4)], wu)
        need(("ngt", l))
        rs.free(rs.ready + 3)
        for j in range(4):
            for mb in range(4):
                grad_cols(4 + j, ngt, dpre[:, j * 512:(j + 1) * 512], mb)
            res = nn(ones, dpre[:, j * 512:(j + 1) * 512])
            row, col = 16 + l * 2 + j // 2, (j % 2) * 512
            vacc[row:row + 1, col:col + 512] = res[0:1]
        if l > 0:
            load(("ngt", l - 1), nt_i.at[l - 1], ngt)
        rs.ready += 4
        rs.tick()
        need(("mix", l))
        send.wait()
        norm_back(mix, rbuf.at[l * 2], l * 2, 4 + l * 4 + 1, 4 + l * 4, ag.at[l])
        give_rows(ag.at[l, mine, :], base + 2).start()
        if l > 0:
            load(("mix", l - 1), mix_i.at[l - 1], mix)
        need(("o", l, 0), ("o", l, 1))
        w_o = wo[...].reshape(heads_w, -1)
        datt[mine, :] = nt(ag[l, mine, :], w_o).astype(BF)
        rs.tick()
        rs.tick()
        give_rows(ag.at[l, theirs, :], base + 2).wait_recv()
        datt[theirs, :] = nt(ag[l, theirs, :], w_o).astype(BF)
        if l > 0:
            load_out(l - 1)
        need(("attt", l))
        rs.free(rs.ready)
        grad_out()
        rs.ready += 1
        if l > 0:
            load(("attt", l - 1), attt_i.at[l - 1], attt)
        need(("qkv", l), ("lse", l))
        attend_back(0, 2)
        rs.tick()
        attend_back(2, 4)
        rs.tick()
        if l > 0:
            load(("qkv", l - 1), qkv_i.at[l - 1], qkv)
            load(("lse", l - 1), lse_i.at[l - 1], lse)
        need(("wqkv", l))
        for nb in range(4):
            sbuf[:, nb * 256:(nb + 1) * 256] = in_back(theirs, nb).astype(BF)
        send = remote(sbuf, rbuf.at[l * 2 + 1], x_send.at[base + 3], x_recv.at[base + 3], p.peer)
        send.start()
        need(("xt", l))
        rs.free(rs.ready + 2)
        for m in range(3):
            for mb in range(4):
                grad_cols(m, xt, dqkv[m], mb)
            if m != 1:
                vacc[20 + l:21 + l, (m // 2) * 512:(m // 2) * 512 + 512] = nn(ones, dqkv[m])[0:1]
        rs.ready += 3
        rs.tick()
        for nb in range(4):
            cols = slice(nb * 256, (nb + 1) * 256)
            g[:, cols] = dz[:, cols] + in_back(mine, nb)
        if l > 0:
            load(("wqkv", l - 1), wg.at[pl.ds((l - 1) * CH, 3)], wqkv)
            load(("xt", l - 1), xt_i.at[l - 1], xt)
        rs.tick()
        send.wait_recv()
        g[...] = g[...] + rbuf[l * 2 + 1].astype(F32)
    end = pltpu.make_async_copy(g, grad_o, e_sem.at[0])
    end.start()
    s_x = remote(vacc.at[0:16], vx, v_send.at[0], v_recv.at[0], p.peer)
    s_x.start()
    rs.tick()
    s_x.wait()
    vacc[0:16] = vacc[0:16] + vx[...]
    s_c = remote(vacc, vc, v_send.at[1], v_recv.at[1], p.twin)
    s_c.start()
    s_c.wait()
    vacc[...] = vacc[...] + vc[...]
    s_y = remote(vacc, vy, v_send.at[2], v_recv.at[2], p.side)
    s_y.start()
    rs.tick()
    s_y.wait()
    vacc[...] = vacc[...] + vy[...]
    s_z = [remote(vacc, vz.at[i - 1], v_send.at[2 + i], v_recv.at[2 + i], p.far(i)) for i in range(1, depth)]
    for copy in s_z:
        copy.start()
    rs.tick()
    for copy in s_z:
        copy.wait()
    total = vacc[...]
    for i in range(depth - 1):
        total = total + vz[i]
    vc[...] = total
    last = pltpu.make_async_copy(vc, vsum_o, e_sem.at[1])
    last.start()
    rs.finish()
    send.wait_send()
    for l in range(layers):
        base = (layers - 1 - l) * 4
        for h in range(4):
            give_part(l, h, mine).wait_send()
        give_rows(ag.at[l, mine, :], base + 2).wait_send()
    end.wait()
    last.wait()


def backward_call(depth, layers, rows, vec, cot, segc, segr, wg, saved):
    group, hw, fh = 2 * rows, 512, 2048
    vm = pltpu.VMEM
    dp = depth * 4
    n = layers * CH
    slots = 6
    shapes = [(rows, 1024), (24, 1024), (layers, 64, hw), (layers, 64, hw), (layers, 64, hw), (layers, 32, 1024),
              (layers, 64, fh), (layers, 128, 1024)]
    scratch = [vm((CH, dp, 64, 512), BF), vm((slots, depth, 2, 64, 512), BF), vm((slots, depth, 64, 512), BF),
               vm((slots, depth - 1, 64, 512), BF), vm((2, 64, 512), F32),
               vm((3, dp, 64, 512), BF), vm((dp, 32, 1024), BF), vm((4, dp, 64, 512), BF), vm((dp, 2, 64, 1024), BF)]
    scratch += [vm(s.shape[1:], s.dtype) for s in saved]
    scratch += [vm((group, fh), BF), vm((layers, group, 1024), BF), vm((layers, group, 1024), BF),
                vm((2 * layers, rows, 1024), BF), vm((rows, 1024), BF), vm((rows, 1024), F32), vm((rows, 1024), F32),
                vm((3, group, hw), BF), vm((group, hw), BF), vm((2, group, group), F32), vm((2, group, group), BF),
                vm((group, group), F32), vm((24, 1024), F32), vm((16, 1024), F32),
                vm((24, 1024), F32), vm((24, 1024), F32), vm((depth - 1, 24, 1024), F32)]
    dma = pltpu.SemaphoreType.DMA
    scratch += [dma((n, depth + 1)), dma((n, depth + 1)), dma((layers, 4)), dma((layers, 4)), dma((4 * layers,)), dma((4 * layers,)),
                dma((depth + 2,)), dma((depth + 2,)), dma((24 * layers,)), dma((2, 2)), dma((2,))]
    full = pl.BlockSpec(memory_space=pltpu.VMEM)
    hbm = pl.BlockSpec(memory_space=pl.ANY)
    return pl.pallas_call(
        functools.partial(bwd_kernel, depth, layers),
        out_shape=[jax.ShapeDtypeStruct(s, F32) for s in shapes],
        in_specs=[full] * 4 + [hbm] * (1 + len(saved)),
        out_specs=[hbm] * len(shapes),
        scratch_shapes=scratch,
        compiler_params=pltpu.CompilerParams(collective_id=2, has_side_effects=True, vmem_limit_bytes=63 * 2**20),
        cost_estimate=pl.CostEstimate(flops=28 * 10**9, bytes_accessed=60 * 10**6, transcendentals=0),
    )(vec, cot, segc, segr, wg, *saved)


def pack_vectors(qv_bias, up_bias, norm_gain, shift_bias):
    layers = qv_bias.shape[0]
    dp, x = lax.axis_index("dp"), lax.axis_index("tensor")

    def spread(rows32, slot):
        tiled = jnp.tile(rows32, (1, 4))
        lane = lax.broadcasted_iota(jnp.int32, tiled.shape, 1) // 32
        return jnp.where(lane == slot, tiled, 0.0)

    full = jnp.concatenate([norm_gain.reshape(layers * 2, 32), shift_bias.reshape(layers * 4, 32)])
    full = spread(full, (dp * 2 + x) % 4)
    half = spread(qv_bias.astype(F32).reshape(layers * 2, 32), dp % 4)
    out = jnp.zeros((32, 128), F32)
    out = out.at[0:layers * 6].set(full)
    out = out.at[16:16 + layers * 2].set(half)
    return out.at[24:24 + layers].set(up_bias.astype(F32))


def on_device(
    tokens,
    cotangent,
    segment_ids,
    w_query,
    w_key,
    w_value,
    w_out,
    w_up,
    w_down,
    qv_bias,
    up_bias,
    norm_gain,
    shift_bias,
):
    layers = w_query.shape[0]
    rows = tokens.shape[0]
    depth = lax.axis_size("dp") // 4
    vp = pack_vectors(qv_bias, up_bias, norm_gain, shift_bias)
    segc, segr = segment_ids[:, None], segment_ids[None, :]
    wg, vec, out, *saved = forward_call(
        depth, layers, rows, vp, tokens, segc, segr, w_query, w_key, w_value, w_out, w_up, w_down
    )
    grad, vsum, g_q, g_k, g_v, g_o, g_u, g_d = backward_call(depth, layers, rows, vec, cotangent, segc, segr, wg, saved)
    dp, x = lax.axis_index("dp"), lax.axis_index("tensor")
    gains = lax.dynamic_slice_in_dim(vsum[0:layers * 6], (dp * 2 + x) * 32, 32, 1)
    g_qv = lax.dynamic_slice_in_dim(vsum[20:20 + layers].reshape(layers, 2, 512), dp * 32, 32, 2)
    g_ub = lax.dynamic_slice_in_dim(vsum[16:16 + 2 * layers].reshape(layers, 2048), dp * 128, 128, 1)
    return (
        out,
        grad,
        g_q,
        g_k,
        g_v,
        g_o,
        g_u,
        g_d,
        g_qv,
        g_ub,
        gains[0:layers * 2].reshape(layers, 2, 32),
        gains[layers * 2:].reshape(layers, 4, 32),
    )


def on_any_mesh(
    tokens,
    cotangent,
    segment_ids,
    w_query,
    w_key,
    w_value,
    w_out,
    w_up,
    w_down,
    qv_bias,
    up_bias,
    norm_gain,
    shift_bias,
):
    layers = w_query.shape[0]
    group = segment_ids.shape[0]
    seq = min(LEN, group)
    segs = segment_ids.reshape(group // seq, seq)
    stream = tokens.astype(jnp.float32)
    kept_all = []
    mats_all = []
    vecs_all = []
    for layer in range(layers):
        mats = (
            lax.all_gather(w_query[layer], "dp", axis=0, tiled=True),
            lax.all_gather(w_key[layer], "dp", axis=0, tiled=True),
            lax.all_gather(w_value[layer], "dp", axis=0, tiled=True),
            lax.all_gather(w_out[layer], "dp", axis=0, tiled=True),
            lax.all_gather(w_up[layer], "dp", axis=0, tiled=True),
            lax.all_gather(w_down[layer], "dp", axis=0, tiled=True),
            lax.all_gather(qv_bias[layer], "dp", axis=1, tiled=True),
            lax.all_gather(up_bias[layer], "dp", axis=0, tiled=True),
        )
        vecs = (
            lax.all_gather(norm_gain[layer], ("dp", "tensor"), axis=1, tiled=True),
            lax.all_gather(shift_bias[layer], ("dp", "tensor"), axis=1, tiled=True),
        )
        stream, kept = forward_layer(stream, mats, vecs, segs, seq)
        kept_all.append(kept)
        mats_all.append(mats)
        vecs_all.append(vecs)
    grad = cotangent.astype(jnp.float32)
    mat_shards = [None] * layers
    vec_shards = [None] * layers
    for layer in reversed(range(layers)):
        mats = (
            lax.all_gather(w_query[layer], "dp", axis=0, tiled=True),
            lax.all_gather(w_key[layer], "dp", axis=0, tiled=True),
            lax.all_gather(w_value[layer], "dp", axis=0, tiled=True),
            lax.all_gather(w_out[layer], "dp", axis=0, tiled=True),
            lax.all_gather(w_up[layer], "dp", axis=0, tiled=True),
            lax.all_gather(w_down[layer], "dp", axis=0, tiled=True),
            lax.all_gather(qv_bias[layer], "dp", axis=1, tiled=True),
            lax.all_gather(up_bias[layer], "dp", axis=0, tiled=True),
        )
        grad, mat_grads, vec_grads = backward_layer(
            grad, mats, vecs_all[layer], kept_all[layer], segs, seq
        )
        g_q, g_k, g_v, g_o, g_u, g_d, g_qv, g_ub = mat_grads
        mat_shards[layer] = (
            lax.psum_scatter(
                g_q.astype(jnp.bfloat16), "dp", scatter_dimension=0, tiled=True
            ).astype(jnp.float32),
            lax.psum_scatter(
                g_k.astype(jnp.bfloat16), "dp", scatter_dimension=0, tiled=True
            ).astype(jnp.float32),
            lax.psum_scatter(
                g_v.astype(jnp.bfloat16), "dp", scatter_dimension=0, tiled=True
            ).astype(jnp.float32),
            lax.psum_scatter(
                g_o.astype(jnp.bfloat16), "dp", scatter_dimension=0, tiled=True
            ).astype(jnp.float32),
            lax.psum_scatter(
                g_u.astype(jnp.bfloat16), "dp", scatter_dimension=0, tiled=True
            ).astype(jnp.float32),
            lax.psum_scatter(
                g_d.astype(jnp.bfloat16), "dp", scatter_dimension=0, tiled=True
            ).astype(jnp.float32),
            lax.psum_scatter(
                g_qv.astype(jnp.bfloat16), "dp", scatter_dimension=1, tiled=True
            ).astype(jnp.float32),
            lax.psum_scatter(
                g_ub.astype(jnp.bfloat16), "dp", scatter_dimension=0, tiled=True
            ).astype(jnp.float32),
        )
        g_gain, g_shift = vec_grads
        vec_shards[layer] = (
            lax.psum_scatter(g_gain, ("dp", "tensor"), scatter_dimension=1, tiled=True),
            lax.psum_scatter(g_shift, ("dp", "tensor"), scatter_dimension=1, tiled=True),
        )

    def stacked(index, source):
        return jnp.stack([entry[index] for entry in source])

    return (
        stream,
        grad,
        stacked(0, mat_shards),
        stacked(1, mat_shards),
        stacked(2, mat_shards),
        stacked(3, mat_shards),
        stacked(4, mat_shards),
        stacked(5, mat_shards),
        stacked(6, mat_shards),
        stacked(7, mat_shards),
        stacked(0, vec_shards),
        stacked(1, vec_shards),
    )


def solution(mesh):
    in_specs = (
        P(("dp", "tensor"), None),
        P(("dp", "tensor"), None),
        P("dp"),
        P(None, "dp", "tensor"),
        P(None, "dp", "tensor"),
        P(None, "dp", "tensor"),
        P(None, ("tensor", "dp"), None),
        P(None, "dp", "tensor"),
        P(None, ("tensor", "dp"), None),
        P(None, None, ("tensor", "dp")),
        P(None, ("tensor", "dp")),
        P(None, None, ("dp", "tensor")),
        P(None, None, ("dp", "tensor")),
    )
    out_specs = (
        P(("dp", "tensor"), None),
        P(("dp", "tensor"), None),
        P(None, "dp", "tensor"),
        P(None, "dp", "tensor"),
        P(None, "dp", "tensor"),
        P(None, ("tensor", "dp"), None),
        P(None, "dp", "tensor"),
        P(None, ("tensor", "dp"), None),
        P(None, None, ("tensor", "dp")),
        P(None, ("tensor", "dp")),
        P(None, None, ("dp", "tensor")),
        P(None, None, ("dp", "tensor")),
    )
    small = mesh.shape["tensor"] == 2 and mesh.shape["dp"] == 16
    return jax.shard_map(
        on_device if small else on_any_mesh, mesh=mesh, in_specs=in_specs, out_specs=out_specs, check_vma=False
    )
```

```python
import functools
import math

import jax
import jax.numpy as jnp
from jax import lax
from jax.experimental import pallas as pl
from jax.experimental.pallas import tpu as pltpu
from jax.sharding import PartitionSpec as P

HEAD = 64
LEN = 512


EPS = 1e-06
NEG = -1e30


def layer_norm(z, gain, shift):
    mean = jnp.mean(z, axis=-1, keepdims=True)
    cent = z - mean
    var = jnp.mean(cent * cent, axis=-1, keepdims=True)
    return cent * lax.rsqrt(var + EPS) * gain + shift


def gelu_exact(pre):
    return jax.nn.gelu(pre, approximate=False)


def inner(left, right):
    return lax.dot_general(
        left, right, (((0,), (0,)), ((), ())), preferred_element_type=jnp.float32
    )


def times_back(left, right):
    return lax.dot_general(
        left, right, (((1,), (1,)), ((), ())), preferred_element_type=jnp.float32
    )


def gather_rows(rows):
    return lax.all_gather(rows, "tensor", axis=0, tiled=True)


def gather_grads(rows):
    return lax.all_gather(rows, "tensor", axis=0, tiled=True)


def sum_rows(term, rows):
    return lax.psum_scatter(
        term(jnp.int32(0), lax.axis_size("tensor") * rows).astype(jnp.bfloat16),
        "tensor",
        scatter_dimension=0,
        tiled=True,
    ).astype(jnp.float32)


def sum_grads(term, rows):
    return lax.psum_scatter(
        term(jnp.int32(0), lax.axis_size("tensor") * rows).astype(jnp.bfloat16),
        "tensor",
        scatter_dimension=0,
        tiled=True,
    ).astype(jnp.float32)


def allowed(segment):
    return segment[:, None] == segment[None, :]


def attend_one(args):
    query, key, value, segment = args
    scale = HEAD ** (-0.5)
    scores = jnp.einsum("qhd,khd->hqk", query, key, preferred_element_type=jnp.float32) * scale
    scores = jnp.where(allowed(segment)[None], scores, NEG)
    top = jnp.max(scores, axis=-1, keepdims=True)
    total = top + jnp.log(jnp.sum(jnp.exp(scores - top), axis=-1, keepdims=True))
    probs = jnp.exp(scores - total).astype(jnp.bfloat16)
    result = jnp.einsum("hqk,khd->qhd", probs, value, preferred_element_type=jnp.float32)
    return (result.astype(jnp.bfloat16), total[..., 0])


def attend_back(args):
    query, key, value, segment, total, d_att = args
    scale = HEAD ** (-0.5)
    scores = jnp.einsum("qhd,khd->hqk", query, key, preferred_element_type=jnp.float32) * scale
    scores = jnp.where(allowed(segment)[None], scores, NEG)
    probs = jnp.exp(scores - total[..., None])
    d_probs = jnp.einsum("qhd,khd->hqk", d_att, value, preferred_element_type=jnp.float32)
    row_dot = jnp.sum(d_probs * probs, axis=-1, keepdims=True)
    d_scores = (probs * (d_probs - row_dot)).astype(jnp.bfloat16)
    d_query = (
        jnp.einsum("hqk,khd->qhd", d_scores, key, preferred_element_type=jnp.float32) * scale
    ).astype(jnp.bfloat16)
    d_key = (
        jnp.einsum("hqk,qhd->khd", d_scores, query, preferred_element_type=jnp.float32) * scale
    ).astype(jnp.bfloat16)
    d_value = jnp.einsum(
        "hqk,qhd->khd", probs.astype(jnp.bfloat16), d_att, preferred_element_type=jnp.float32
    ).astype(jnp.bfloat16)
    return (d_query, d_key, d_value)


def forward_layer(stream, mats, vecs, segs, seq):
    w_q, w_k, w_v, w_o, w_u, w_d, qvb, upb = mats
    gains, shifts = vecs
    seqs = segs.shape[0]
    rows = stream.shape[0]
    x_rows = gather_rows(stream.astype(jnp.bfloat16))
    query = (
        jnp.dot(x_rows, w_q, preferred_element_type=jnp.float32) + qvb[0].astype(jnp.float32)
    ).astype(jnp.bfloat16)
    key = jnp.dot(x_rows, w_k, preferred_element_type=jnp.float32).astype(jnp.bfloat16)
    value = (
        jnp.dot(x_rows, w_v, preferred_element_type=jnp.float32) + qvb[1].astype(jnp.float32)
    ).astype(jnp.bfloat16)
    width = query.shape[1]
    local_heads = width // HEAD

    def split(matrix):
        return matrix.reshape(seqs, seq, local_heads, HEAD)

    attended, totals = lax.map(attend_one, (split(query), split(key), split(value), segs))
    attended = attended.reshape(seqs * seq, width)

    def out_term(start, count):
        return jnp.dot(attended, w_o, preferred_element_type=jnp.float32)

    out_sum = sum_rows(out_term, rows)
    mixed = stream + out_sum + shifts[0]
    normed = layer_norm(mixed, gains[0], shifts[1])
    n_rows = gather_rows(normed.astype(jnp.bfloat16))
    pre = jnp.dot(n_rows, w_u, preferred_element_type=jnp.float32) + upb.astype(jnp.float32)
    hidden = gelu_exact(pre).astype(jnp.bfloat16)

    def down_term(start, count):
        return jnp.dot(hidden, w_d, preferred_element_type=jnp.float32)

    down_sum = sum_rows(down_term, rows)
    second = normed + down_sum + shifts[2]
    result = layer_norm(second, gains[1], shifts[3])
    kept = (x_rows, query, key, value, attended, totals, mixed, n_rows, pre, hidden, second)
    return (result, kept)


def backward_layer(grad, mats, vecs, kept, segs, seq):
    w_q, w_k, w_v, w_o, w_u, w_d, qvb, upb = mats
    gains, shifts = vecs
    x_rows, query, key, value, attended, totals, mixed, n_rows, pre, hidden, second = kept
    seqs = segs.shape[0]
    rows = grad.shape[0]
    width = query.shape[1]
    local_heads = width // HEAD

    def split(matrix):
        return matrix.reshape(seqs, seq, local_heads, HEAD)

    _, pull_second = jax.vjp(layer_norm, second, gains[1], shifts[3])
    d_second, d_gain_two, d_shift_two = pull_second(grad)
    d_down_bias = jnp.sum(d_second, axis=0)
    d_f = gather_grads(d_second.astype(jnp.bfloat16))
    grad_down = inner(hidden, d_f)
    d_hidden = times_back(d_f, w_d)
    _, pull_gelu = jax.vjp(gelu_exact, pre)
    d_pre = pull_gelu(d_hidden)[0].astype(jnp.bfloat16)
    grad_up = inner(n_rows, d_pre)
    d_up_bias = jnp.sum(d_pre.astype(jnp.float32), axis=0)

    def up_term(start, count):
        return times_back(d_pre, w_u)

    d_normed = d_second + sum_grads(up_term, rows)
    _, pull_first = jax.vjp(layer_norm, mixed, gains[0], shifts[1])
    d_mixed, d_gain_one, d_shift_one = pull_first(d_normed)
    d_out_bias = jnp.sum(d_mixed, axis=0)
    d_a = gather_grads(d_mixed.astype(jnp.bfloat16))
    grad_out = inner(attended, d_a)
    d_att = times_back(d_a, w_o).astype(jnp.bfloat16)
    d_query, d_key, d_value = lax.map(
        attend_back, (split(query), split(key), split(value), segs, totals, split(d_att))
    )
    d_query = d_query.reshape(seqs * seq, width)
    d_key = d_key.reshape(seqs * seq, width)
    d_value = d_value.reshape(seqs * seq, width)
    grad_q = inner(x_rows, d_query)
    grad_k = inner(x_rows, d_key)
    grad_v = inner(x_rows, d_value)
    d_qv = jnp.stack(
        [jnp.sum(d_query.astype(jnp.float32), axis=0), jnp.sum(d_value.astype(jnp.float32), axis=0)]
    )

    def in_term(start, count):
        part = times_back(d_query, w_q)
        part = part + times_back(d_key, w_k)
        return part + times_back(d_value, w_v)

    d_stream = d_mixed + sum_grads(in_term, rows)
    mat_grads = (grad_q, grad_k, grad_v, grad_out, grad_up, grad_down, d_qv, d_up_bias)
    vec_grads = (
        jnp.stack([d_gain_one, d_gain_two]),
        jnp.stack([d_out_bias, d_shift_one, d_down_bias, d_shift_two]),
    )
    return (d_stream, mat_grads, vec_grads)


MESH = pl.DeviceIdType.MESH
BF = jnp.bfloat16
F32 = jnp.float32
AHEAD = 2
KEPT = ("vec", "xt", "qkv", "attt", "lse", "mix", "ngt", "hidt", "gp", "sec", "inv", "out")
CH = 12


def nt(left, right):
    return lax.dot_general(left, right, (((1,), (1,)), ((), ())), preferred_element_type=F32)


def nn(left, right):
    return lax.dot_general(left, right, (((1,), (0,)), ((), ())), preferred_element_type=F32)


def tn(left, right):
    return lax.dot_general(left, right, (((0,), (0,)), ((), ())), preferred_element_type=F32)


def remote(src, dst, send_sem, recv_sem, device):
    return pltpu.make_async_remote_copy(
        src_ref=src, dst_ref=dst, send_sem=send_sem, recv_sem=recv_sem, device_id=device, device_id_type=MESH
    )


class Place:
    def __init__(self, depth):
        self.depth = depth
        self.dp = lax.axis_index("dp")
        self.x = lax.axis_index("tensor")
        self.z = self.dp // 4
        self.y = (self.dp // 2) % 2
        self.c = self.dp % 2

    def at(self, z, y, c):
        return {"dp": z * 4 + y * 2 + c, "tensor": self.x}

    def far(self, step):
        return self.at((self.z + step) % self.depth, self.y, self.c)

    def before(self, step):
        return (self.z + self.depth - step) % self.depth

    @property
    def side(self):
        return self.at(self.z, 1 - self.y, self.c)

    @property
    def twin(self):
        return self.at(self.z, self.y, 1 - self.c)

    @property
    def peer(self):
        return {"dp": self.dp, "tensor": 1 - self.x}

    def greet(self):
        barrier = pltpu.get_barrier_semaphore()
        partners = [self.far(i) for i in range(1, self.depth)] + [self.side, self.twin, self.peer]
        for device in partners:
            pl.semaphore_signal(barrier, inc=1, device_id=device, device_id_type=MESH)
        pl.semaphore_wait(barrier, len(partners))


class Gather:
    def __init__(self, place, wg, keep, send, recv, total):
        self.p, self.wg, self.keep, self.send, self.recv, self.total = place, wg, keep, send, recv, total
        self.view = wg.reshape(wg.shape[0], place.depth, 2, 2, *wg.shape[2:])
        self.time = 0
        self.have = 0

    def far(self, k, i):
        p = self.p
        return remote(self.wg.at[k, p.dp], self.wg.at[k, p.dp], self.send.at[k, i - 1], self.recv.at[k, i - 1], p.far(i))

    def far_in(self, k, i):
        p = self.p
        ref = self.wg.at[k, p.before(i) * 4 + p.y * 2 + p.c]
        return remote(ref, ref, self.send.at[k, i - 1], self.recv.at[k, i - 1], p.far(i))

    def side(self, k, y):
        p, d = self.p, self.p.depth - 1
        ref = self.view.at[k, :, y, p.c]
        return remote(ref, ref, self.send.at[k, d], self.recv.at[k, d], p.side)

    def twin(self, k, c):
        p, d = self.p, self.p.depth
        ref = self.view.at[k, :, :, c]
        return remote(ref, ref, self.send.at[k, d], self.recv.at[k, d], p.twin)

    def begin(self, ahead):
        self.ahead = ahead
        for k in range(ahead):
            for i in range(1, self.p.depth):
                self.far(k, i).start()

    def tick(self):
        t, n = self.time, self.total
        if t >= n + 3:
            return
        if t + self.ahead < n:
            for i in range(1, self.p.depth):
                self.far(t + self.ahead, i).start()
        if t < n:
            for i in range(1, self.p.depth):
                self.far_in(t, i).wait_recv()
            self.side(t, self.p.y).start()
        if 1 <= t <= n:
            self.side(t - 1, 1 - self.p.y).wait_recv()
            self.twin(t - 1, self.p.c).start()
        if t >= 2 and t - 2 < n:
            self.twin(t - 2, 1 - self.p.c).wait_recv()
            self.have = t - 1
            self.keep(t - 2)
        self.time += 1

    def until(self, count):
        while self.have < count:
            self.tick()

    def finish(self):
        self.until(self.total)
        for k in range(self.total):
            for i in range(1, self.p.depth):
                self.far(k, i).wait_send()
            self.side(k, self.p.y).wait_send()
            self.twin(k, self.p.c).wait_send()


def norm_rows(z, gain, shift):
    mean = jnp.mean(z, axis=-1, keepdims=True)
    cent = z - mean
    inv = lax.rsqrt(jnp.mean(cent * cent, axis=-1, keepdims=True) + EPS)
    hat = cent * inv
    return hat * gain + shift, hat, jnp.broadcast_to(inv, (z.shape[0], 128))


def mask_bias(segr, bias):
    seg = segr[...].astype(F32)
    n = seg.shape[1]
    column = jnp.broadcast_to(seg, (8, n)).T
    for i in range(n // 64):
        r = slice(i * 64, (i + 1) * 64)
        bias[r, :] = jnp.where(column[r, 0:1] == seg, 0.0, NEG)


def fwd_kernel(depth, layers, gains, shifts, qvb, upb, tok, segr, w_query, w_key, w_value, w_out, w_up, w_down,
               wg_o, vec_o, out_o, xt_o, qkv_o, attt_o, lse_o, mix_o, nt_o, ht_o, gp_o, sec_o, inv_o,
               wg, vg, vec, stream, normed, bias, work, prob, xt, qkv, attt, lse, mix, ngt, hidt, gp, sec, inv,
               xg, ng, hid, att, sbuf, rbuf,
               w_send, w_recv, v_send, v_recv, d_send, d_recv, x_send, x_recv, o_sem, k_sem):
    p = Place(depth)
    x = p.x
    rows = tok.shape[0]
    group = 2 * rows
    heads_w = qkv.shape[-1]
    mine = pl.ds(pl.multiple_of(x * rows, rows), rows)
    theirs = pl.ds(pl.multiple_of((1 - x) * rows, rows), rows)
    n_chunks = layers * CH

    def keep_chunk(k):
        pltpu.make_async_copy(wg.at[k], wg_o.at[k], k_sem.at[k]).start()

    gat = Gather(p, wg, keep_chunk, w_send, w_recv, n_chunks)
    for l in range(layers):
        c0 = l * CH
        for m, w in enumerate((w_query, w_key, w_value)):
            wg[c0 + m, p.dp] = w[l]
        for hh in range(2):
            wg[c0 + 3, p.dp, hh * 32:(hh + 1) * 32, :] = w_out[l, :, hh * 512:(hh + 1) * 512]
        for j in range(4):
            wg[c0 + 4 + j, p.dp] = w_up[l, :, j * 512:(j + 1) * 512]
            for q in range(2):
                wg[c0 + 8 + j, p.dp, :, q * 256:(q + 1) * 256] = w_down[l, q * 64:(q + 1) * 64, j * 256:(j + 1) * 256]
    own = vg.at[x, p.z, p.y, p.c]
    lane = lax.broadcasted_iota(jnp.int32, (1, 128), 1)

    def spread(row, slot):
        row = jnp.concatenate([row.astype(F32)] * 4, axis=1)
        return jnp.where(jnp.logical_and(lane >= slot * 32, lane < slot * 32 + 32), row, 0.0)

    own[...] = jnp.zeros((32, 128), F32)
    for l in range(layers):
        own[l * 2:l * 2 + 2, :] = spread(gains[l], (p.c * 2 + x) % 4)
        own[2 * layers + l * 4:2 * layers + l * 4 + 4, :] = spread(shifts[l], (p.c * 2 + x) % 4)
        own[16 + l * 2:18 + l * 2, :] = spread(qvb[l], p.dp % 4)
        own[24 + l:25 + l, :] = upb[l:l + 1, :].astype(F32)
    xg[0, mine, :] = tok[...]
    p.greet()

    def give_rows(ref, index):
        return remote(ref, ref, x_send.at[index], x_recv.at[index], p.peer)

    v_far = [remote(vg.at[x, p.z, p.y, p.c], vg.at[x, p.z, p.y, p.c], v_send.at[i - 1], v_recv.at[i - 1], p.far(i))
             for i in range(1, depth)]
    for copy in v_far:
        copy.start()
    give_rows(xg.at[0, mine, :], 0).start()
    gat.begin(AHEAD)

    stream[...] = tok[...].astype(F32)
    mask_bias(segr, bias)
    for copy in v_far:
        copy.wait_recv()
    v_side = remote(vg.at[x, :, p.y, p.c], vg.at[x, :, p.y, p.c], v_send.at[depth - 1], v_recv.at[depth - 1], p.side)
    v_side.start()
    v_side.wait_recv()
    v_twin = remote(vg.at[x, :, :, p.c], vg.at[x, :, :, p.c], v_send.at[depth], v_recv.at[depth], p.twin)
    v_twin.start()
    v_twin.wait_recv()
    v_peer = remote(vg.at[x], vg.at[x], v_send.at[depth + 1], v_recv.at[depth + 1], p.peer)
    v_peer.start()
    gat.tick()
    v_peer.wait_recv()
    for z in range(depth):
        for y in range(2):
            b = (z * 2 + y) * 128
            vec[0:16, b:b + 128] = (vg[0, z, y, 0, 0:16] + vg[0, z, y, 1, 0:16]
                                    + vg[1, z, y, 0, 0:16] + vg[1, z, y, 1, 0:16])
    for z in range(depth):
        for_half = vg[x, z, 0, 0, 16:24] + vg[x, z, 0, 1, 16:24] + vg[x, z, 1, 0, 16:24] + vg[x, z, 1, 1, 16:24]
        vec[16:24, z * 128:(z + 1) * 128] = for_half
        for y in range(2):
            for c in range(2):
                b = (z * 4 + y * 2 + c) * 128
                vec[24:32, b:b + 128] = vg[x, z, y, c, 24:32]
    kept = {}

    def keep(name, src, dst):
        copy = pltpu.make_async_copy(src, dst, o_sem.at[KEPT.index(name)])
        copy.start()
        kept[name] = copy

    def fresh(name):
        if name in kept:
            kept.pop(name).wait()

    keep("vec", vec, vec_o)

    def give_half(l, hh):
        cols = slice(hh * 512, (hh + 1) * 512)
        return remote(sbuf.at[:, cols], rbuf.at[l * 2, :, cols], d_send.at[l, 4 + hh], d_recv.at[l, 4 + hh], p.peer)

    def give_part(l, h):
        cols = slice(h * 256, (h + 1) * 256)
        return remote(sbuf.at[:, cols], rbuf.at[l * 2 + 1, :, cols], d_send.at[l, h], d_recv.at[l, h], p.peer)

    def gain(l, i):
        r = l * 2 + i
        return vec[r:r + 1, 0:1024]

    def shift(l, i):
        r = 4 + l * 4 + i
        return vec[r:r + 1, 0:1024]

    def project(l, r):
        for m in range(3):
            w = wg[l * CH + m].reshape(-1, heads_w)
            res = nn(xg[l, r, :], w)
            if m != 1:
                b = 16 + l * 2 + (m // 2)
                res = res + vec[b:b + 1, 0:heads_w]
            qkv[m, r, :] = res.astype(BF)

    half_lane = lax.broadcasted_iota(jnp.int32, (1, 128), 1) < HEAD
    first_half = jnp.where(half_lane, 1.0, 0.0).astype(BF)
    second_half = jnp.where(half_lane, 0.0, 1.0).astype(BF)
    scale = HEAD ** -0.5

    def attend(q_rows):
        def pair(hp, carry):
            lanes = pl.ds(pl.multiple_of(hp * 128, 128), 128)
            k128 = qkv[1, :, lanes]
            v_t = qkv[2, :, lanes].T
            q128 = qkv[0, q_rows, lanes]
            both = []
            for half in range(2):
                k_half = k128 * ((second_half if half else first_half) * scale)
                work[half] = nt(k_half, q128)
                top = jnp.full((8, rows), NEG, F32)
                for i in range(group // 64):
                    r = slice(i * 64, (i + 1) * 64)
                    s = work[half, r, :] + bias[r, q_rows]
                    work[half, r, :] = s
                    top = jnp.maximum(top, jnp.max(s.reshape(8, 8, rows), axis=0))
                top = jnp.max(top, axis=0, keepdims=True)
                tot = jnp.zeros((8, rows), F32)
                for i in range(group // 64):
                    r = slice(i * 64, (i + 1) * 64)
                    e = jnp.exp(work[half, r, :] - top)
                    tot = tot + jnp.sum(e.reshape(8, 8, rows), axis=0)
                    prob[half, r, :] = e.astype(BF)
                tot = jnp.sum(tot, axis=0, keepdims=True)
                lse[pl.ds(hp * 2 + half, 1), q_rows] = top + jnp.log(tot)
                both.append(nn(v_t[half * HEAD:(half + 1) * HEAD], prob[half]) / tot)
            o_t = jnp.concatenate(both, axis=0)
            attt[lanes, q_rows] = o_t.astype(BF)
            att[q_rows, lanes] = o_t.T.astype(BF)
            return carry
        lax.fori_loop(0, heads_w // 128, pair, 0)

    def out_term(l, r, hh):
        return nn(att[r, :], wg[l * CH + 3, :, hh * 32:(hh + 1) * 32, :].reshape(heads_w, 512))

    def flip(src, dst):
        def block(i, carry):
            c = pl.ds(pl.multiple_of(i * 256, 256), 256)
            dst[c, :] = src[:, c].T
            return carry
        lax.fori_loop(0, src.shape[1] // 256, block, 0)

    inv_sqrt2 = 2.0 ** -0.5
    inv_sqrt_2pi = (2.0 * math.pi) ** -0.5

    def up(l, j):
        b = 24 + l
        for cb in range(2):
            cols = slice(j * 512 + cb * 256, j * 512 + (cb + 1) * 256)
            w = wg[l * CH + 4 + j, :, :, cb * 256:(cb + 1) * 256].reshape(-1, 256)
            work[cb] = nn(ng[l], w) + vec[b:b + 1, cols]

            def some(i, carry):
                r = pl.ds(pl.multiple_of(i * 32, 32), 32)
                pre = work[cb, r, :]
                part = 0.5 + 0.5 * lax.erf(pre * inv_sqrt2)
                hid[r, cols] = (pre * part).astype(BF)
                gp[r, cols] = (part + pre * jnp.exp(-0.5 * pre * pre) * inv_sqrt_2pi).astype(BF)
                return carry
            lax.fori_loop(0, group // 32, some, 0)

    def down_term(l, r, h):
        w = wg[l * CH + 8 + h]
        w = jnp.stack([w[:, :, 0:256], w[:, :, 256:512]], axis=1).reshape(-1, 256)
        return nn(hid[r, :], w)

    for l in range(layers):
        c0 = l * CH
        gat.until(c0 + 3)
        fresh("qkv")
        project(l, mine)
        if l > 0:
            gat.tick()
        give_rows(xg.at[l, theirs, :], l * 4).wait_recv()
        project(l, theirs)
        keep("qkv", qkv, qkv_o.at[l])
        fresh("lse")
        fresh("attt")
        attend(theirs)
        gat.until(c0 + 4)
        for hh in range(2):
            sbuf[:, hh * 512:(hh + 1) * 512] = out_term(l, theirs, hh).astype(BF)
            give_half(l, hh).start()
        gat.tick()
        attend(mine)
        keep("lse", lse, lse_o.at[l])
        keep("attt", attt, attt_o.at[l])
        fresh("mix")
        for hh in range(2):
            cols = slice(hh * 512, (hh + 1) * 512)
            mix[:, cols] = stream[:, cols] + out_term(l, mine, hh) + shift(l, 0)[:, cols]
        gat.tick()
        fresh("xt")
        flip(xg.at[l], xt)
        keep("xt", xt, xt_o.at[l])
        gat.tick()
        for hh in range(2):
            give_half(l, hh).wait()

        fresh("inv")

        def first_norm(i, carry):
            r = pl.ds(pl.multiple_of(i * 32, 32), 32)
            mixed = mix[r, :] + rbuf[l * 2, r, :].astype(F32)
            res, mix[r, :], inv[0, r, :] = norm_rows(mixed, gain(l, 0), shift(l, 1))
            normed[r, :] = res
            ng[l, pl.ds(pl.multiple_of(x * rows + i * 32, 32), 32), :] = res.astype(BF)
            return carry
        lax.fori_loop(0, rows // 32, first_norm, 0)
        give_rows(ng.at[l, mine, :], l * 4 + 2).start()
        keep("mix", mix, mix_o.at[l])
        gat.tick()
        gat.tick()
        give_rows(ng.at[l, theirs, :], l * 4 + 2).wait_recv()
        fresh("gp")
        for j in range(4):
            gat.until(c0 + 5 + j)
            up(l, j)
            if j % 2:
                gat.tick()
        keep("gp", gp, gp_o.at[l])
        for h in range(4):
            gat.until(c0 + 9 + h)
            cols = slice(h * 256, (h + 1) * 256)
            sbuf[:, cols] = down_term(l, theirs, h).astype(BF)
            give_part(l, h).start()
            if h == 0:
                fresh("sec")
            sec[:, cols] = normed[:, cols] + down_term(l, mine, h) + shift(l, 2)[:, cols]
        fresh("ngt")
        flip(ng.at[l], ngt)
        keep("ngt", ngt, nt_o.at[l])
        fresh("hidt")
        flip(hid, hidt)
        keep("hidt", hidt, ht_o.at[l])
        for h in range(4):
            give_part(l, h).wait()

        def second_norm(i, carry):
            r = pl.ds(pl.multiple_of(i * 32, 32), 32)
            second = sec[r, :] + rbuf[l * 2 + 1, r, :].astype(F32)
            res, sec[r, :], inv[1, r, :] = norm_rows(second, gain(l, 1), shift(l, 3))
            stream[r, :] = res
            if l + 1 < layers:
                xg[l + 1, pl.ds(pl.multiple_of(x * rows + i * 32, 32), 32), :] = res.astype(BF)
            return carry
        lax.fori_loop(0, rows // 32, second_norm, 0)
        if l + 1 < layers:
            give_rows(xg.at[l + 1, mine, :], l * 4 + 4).start()
        keep("sec", sec, sec_o.at[l])
        keep("inv", inv, inv_o.at[l])
    keep("out", stream, out_o)
    gat.finish()
    for copy in v_far + [v_side, v_twin, v_peer]:
        copy.wait_send()
    for l in range(layers):
        give_rows(xg.at[l, mine, :], l * 4).wait_send()
        give_rows(ng.at[l, mine, :], l * 4 + 2).wait_send()
    for name in list(kept):
        fresh(name)
    for k in range(n_chunks):
        pltpu.make_async_copy(wg.at[k], wg_o.at[k], k_sem.at[k]).wait()


def forward_call(depth, layers, rows, gains, shifts, qvb, upb, tok, segr, *weights):
    group, hw, fh = 2 * rows, 512, 2048
    vm = pltpu.VMEM
    saved = [((layers, 1024, group), BF), ((layers, 3, group, hw), BF), ((layers, hw, group), BF),
             ((layers, 8, group), F32), ((layers, rows, 1024), F32), ((layers, 1024, group), BF),
             ((layers, fh, group), BF), ((layers, group, fh), BF), ((layers, rows, 1024), F32),
             ((layers, 2, rows, 128), F32)]
    dp = depth * 4
    n = layers * CH
    out_shape = [jax.ShapeDtypeStruct((n, dp, 64, 512), BF), jax.ShapeDtypeStruct((32, 2048), F32),
                 jax.ShapeDtypeStruct((rows, 1024), F32)] + [jax.ShapeDtypeStruct(s, t) for s, t in saved]
    scratch = [vm((n, dp, 64, 512), BF), vm((2, depth, 2, 2, 32, 128), F32), vm((32, 2048), F32), vm((rows, 1024), F32), vm((rows, 1024), F32),
               vm((group, group), F32), vm((2, group, 256), F32), vm((2, group, 256), BF)]
    scratch += [vm(s[1:], t) for s, t in saved]
    scratch += [vm((layers, group, 1024), BF), vm((layers, group, 1024), BF), vm((group, fh), BF), vm((group, hw), BF)]
    scratch += [vm((rows, 1024), BF), vm((2 * layers, rows, 1024), BF)]
    dma = pltpu.SemaphoreType.DMA
    scratch += [dma((n, depth + 1)), dma((n, depth + 1)), dma((depth + 2,)), dma((depth + 2,)),
                dma((layers, 6)), dma((layers, 6)), dma((4 * layers,)), dma((4 * layers,)), dma((len(KEPT),)), dma((n,))]
    full = pl.BlockSpec(memory_space=pltpu.VMEM)
    hbm = pl.BlockSpec(memory_space=pl.ANY)
    return pl.pallas_call(
        functools.partial(fwd_kernel, depth, layers),
        out_shape=out_shape,
        in_specs=[full] * 12,
        out_specs=[hbm] * len(out_shape),
        scratch_shapes=scratch,
        compiler_params=pltpu.CompilerParams(collective_id=1, has_side_effects=True, vmem_limit_bytes=63 * 2**20),
        cost_estimate=pl.CostEstimate(flops=14 * 10**9, bytes_accessed=60 * 10**6, transcendentals=0),
    )(gains, shifts, qvb, upb, tok, segr, *weights)


class Scatter:
    def __init__(self, place, order, grads, r1, r2, r3, stage, put, send, recv, out_sem):
        self.p, self.order, self.grads, self.r1, self.r2, self.r3 = place, order, grads, r1, r2, r3
        self.stage, self.put, self.send, self.recv, self.out_sem = stage, put, send, recv, out_sem
        self.view = grads.reshape(grads.shape[0], place.depth, 2, 2, *grads.shape[2:])
        self.time = 0
        self.ready = 0
        self.total = len(order)
        self.slots = r1.shape[0]
        self.outs = {}

    def core(self, n):
        p, s, d = self.p, n % self.slots, self.p.depth - 1
        return remote(self.view.at[self.order[n] % CH, :, :, 1 - p.c], self.r1.at[s],
                      self.send.at[n, d + 1], self.recv.at[n, d + 1], p.twin)

    def side(self, n):
        p, s, d = self.p, n % self.slots, self.p.depth - 1
        return remote(self.r1.at[s, :, 1 - p.y], self.r2.at[s], self.send.at[n, d], self.recv.at[n, d], p.side)

    def far(self, n, i):
        p, s = self.p, n % self.slots
        return remote(self.r2.at[s, (p.z + i) % p.depth], self.r3.at[s, i - 1],
                      self.send.at[n, i - 1], self.recv.at[n, i - 1], p.far(i))

    def step_far(self, n):
        p, s = self.p, n % self.slots
        for i in range(1, p.depth):
            self.far(n, i).wait()
        self.side(n).wait_send()
        if n >= 2:
            for copy in self.outs[n - 2]:
                copy.wait()
        total = self.r2[s, p.z].astype(F32)
        for i in range(p.depth - 1):
            total = total + self.r3[s, i].astype(F32)
        self.stage[n % 2] = total
        self.outs[n] = self.put(self.order[n], self.stage.at[n % 2], self.out_sem.at[n % 2])
        for copy in self.outs[n]:
            copy.start()

    def step_side(self, n):
        p, s = self.p, n % self.slots
        self.side(n).wait_recv()
        self.r2[s] = self.r2[s] + self.r1[s, :, p.y]
        for i in range(1, p.depth):
            self.far(n, i).start()

    def step_core(self, n):
        p, s = self.p, n % self.slots
        self.core(n).wait()
        self.r1[s] = self.r1[s] + self.view[self.order[n] % CH, :, :, p.c]
        self.side(n).start()

    def tick(self):
        t, n = self.time, self.total
        if t >= n + 5 or (t < n and t >= self.ready):
            return
        if 5 <= t:
            self.step_far(t - 5)
        if 3 <= t < n + 3:
            self.step_side(t - 3)
        if 1 <= t < n + 1:
            self.step_core(t - 1)
        if t < n:
            self.core(t).start()
        self.time += 1

    def free(self, n):
        while self.time < n - CH + 2:
            self.tick()

    def finish(self):
        while self.time < self.total + 5:
            self.tick()
        for n in (self.total - 2, self.total - 1):
            for copy in self.outs[n]:
                copy.wait()


def bwd_kernel(depth, layers, vec, cot, segr, wg, xt_i, qkv_i, attt_i, lse_i, mix_i, nt_i, ht_i, gp_i, sec_i, inv_i,
               grad_o, vsum_o, gq_o, gk_o, gv_o, go_o, gu_o, gd_o,
               grads, r1, r2, r3, stage, wqkv, wo, wu, wd,
               xt, qkv, attt, lse, mix, ngt, hidt, gp, sec, inv,
               dpre, fg, ag, rbuf, sbuf, g, dz, dqkv, datt, work, prob, bias, vacc, vx, vc, vy, vz,
               g_send, g_recv, f_send, f_recv, x_send, x_recv, v_send, v_recv, l_sem, o_sem, e_sem):
    p = Place(depth)
    x = p.x
    rows = cot.shape[0]
    group = 2 * rows
    heads_w = datt.shape[-1]
    mine = pl.ds(pl.multiple_of(x * rows, rows), rows)
    theirs = pl.ds(pl.multiple_of((1 - x) * rows, rows), rows)
    loads = {}

    def load(name, src, dst):
        copy = pltpu.make_async_copy(src, dst, l_sem.at[len(loads)])
        copy.start()
        loads[name] = copy

    def need(*names):
        for name in names:
            loads[name].wait()

    def load_down(l):
        for h in range(4):
            for q in range(2):
                load(("d", l, h, q), wg.at[l * CH + 8 + h, :, :, q * 256:(q + 1) * 256],
                     wd.at[:, q, :, h * 256:(h + 1) * 256])

    def need_down(l):
        need(*[("d", l, h, q) for h in range(4) for q in range(2)])

    def load_out(l):
        for hh in range(2):
            load(("o", l, hh), wg.at[l * CH + 3, :, hh * 32:(hh + 1) * 32, :], wo.at[:, :, hh * 512:(hh + 1) * 512])

    top = layers - 1
    load(("inv", top), inv_i.at[top], inv)
    load(("sec", top), sec_i.at[top], sec)
    load_down(top)
    load(("gp", top), gp_i.at[top], gp)
    load(("wu", top), wg.at[pl.ds(top * CH + 4, 4)], wu)
    load(("hidt", top), ht_i.at[top], hidt)
    load(("ngt", top), nt_i.at[top], ngt)
    load(("mix", top), mix_i.at[top], mix)
    load_out(top)
    load(("attt", top), attt_i.at[top], attt)
    load(("qkv", top), qkv_i.at[top], qkv)
    load(("lse", top), lse_i.at[top], lse)
    load(("wqkv", top), wg.at[pl.ds(top * CH, 3)], wqkv)
    load(("xt", top), xt_i.at[top], xt)

    order = []
    for l in reversed(range(layers)):
        order += [l * CH + k for k in (8, 9, 10, 11, 4, 5, 6, 7, 3, 0, 1, 2)]

    def put(k, src, sem):
        l, k = k // CH, k % CH
        if k < 3:
            pairs = [(src, (gq_o, gk_o, gv_o)[k].at[l])]
        elif k == 3:
            pairs = [(src.at[hh * 32:(hh + 1) * 32], go_o.at[l, :, hh * 512:(hh + 1) * 512]) for hh in range(2)]
        elif k < 8:
            pairs = [(src, gu_o.at[l, :, (k - 4) * 512:(k - 3) * 512])]
        else:
            h = k - 8
            pairs = [(src.at[:, q * 256:(q + 1) * 256], gd_o.at[l, q * 64:(q + 1) * 64, h * 256:(h + 1) * 256])
                     for q in range(2)]
        return [pltpu.make_async_copy(a, b, sem.at[i]) for i, (a, b) in enumerate(pairs)]

    rs = Scatter(p, order, grads, r1, r2, r3, stage, put, g_send, g_recv, o_sem)
    p.greet()
    g[...] = cot[...].astype(F32)
    vacc[...] = jnp.zeros_like(vacc)
    mask_bias(segr, bias)

    def give_rows(ref, index):
        return remote(ref, ref, x_send.at[index], x_recv.at[index], p.peer)

    def give_part(l, h, r):
        ref = fg.at[l, r, h * 256:(h + 1) * 256]
        return remote(ref, ref, f_send.at[l, h], f_recv.at[l, h], p.peer)

    def give_cols(l, which, nb):
        cols, i = slice(nb * 256, (nb + 1) * 256), 4 + which * 4 + nb
        return remote(sbuf.at[:, cols], rbuf.at[l * 2 + which, :, cols], f_send.at[l, i], f_recv.at[l, i], p.peer)

    ones = jnp.ones((8, group), BF)
    half_lane = lax.broadcasted_iota(jnp.int32, (1, 128), 1) < HEAD
    first_half = jnp.where(half_lane, 1.0, 0.0).astype(BF)
    second_half = jnp.where(half_lane, 0.0, 1.0).astype(BF)
    scale = HEAD ** -0.5

    def norm_back(hat_ref, inv_ref, extra, gain_row, shift_row, out_row, dest):
        gain = vec[gain_row:gain_row + 1, 0:1024]

        def some(i, carry):
            sg, ss, so = carry
            r = pl.ds(pl.multiple_of(i * 32, 32), 32)
            hat = hat_ref[r, :]
            up = g[r, :] if extra is None else dz[r, :] + extra[r, :].astype(F32)
            gg = up * gain
            m1 = jnp.mean(gg, axis=-1, keepdims=True)
            m2 = jnp.mean(gg * hat, axis=-1, keepdims=True)
            d = inv_ref[r, 0:1] * (gg - m1 - hat * m2)
            dz[r, :] = d
            dest[pl.ds(pl.multiple_of(x * rows + i * 32, 32), 32), :] = d.astype(BF)
            fold = lambda v: jnp.sum(v.reshape(4, 8, 1024), axis=0)
            return sg + fold(up * hat), ss + fold(up), so + fold(d)
        zero = jnp.zeros((8, 1024), F32)
        sg, ss, so = lax.fori_loop(0, rows // 32, some, (zero, zero, zero))
        vacc[gain_row:gain_row + 1, :] = jnp.sum(sg, axis=0, keepdims=True)
        vacc[shift_row:shift_row + 1, :] = jnp.sum(ss, axis=0, keepdims=True)
        vacc[out_row:out_row + 1, :] = jnp.sum(so, axis=0, keepdims=True)

    def hidden_back(l, r):
        def block(nb, carry):
            cols = pl.ds(pl.multiple_of(nb * 512, 512), 512)
            w = wd[pl.ds(nb * 4, 4)].reshape(512, -1)
            dpre[r, cols] = (nt(fg[l, r, :], w) * gp[r, cols].astype(F32)).astype(BF)
            return carry
        lax.fori_loop(0, 4, block, 0, unroll=2)

    def up_back(r, nb):
        w = [wu[j, nb * 4:(nb + 1) * 4].reshape(256, 512) for j in range(4)]
        return sum(nt(dpre[r, j * 512:(j + 1) * 512], w[j]) for j in range(4))

    def in_back(r, nb):
        w = [wqkv[m, nb * 4:(nb + 1) * 4].reshape(256, 512) for m in range(3)]
        return sum(nt(dqkv[m, r, :], w[m]) for m in range(3))

    def grad_down(h):
        def block(mb, carry):
            r = pl.ds(pl.multiple_of(mb * 512, 512), 512)
            res = nn(hidt[r, :], fg[l, :, h * 256:(h + 1) * 256]).astype(BF).reshape(4, 2, 64, 256)
            for q in range(2):
                grads[8 + h, pl.ds(mb * 4, 4), :, q * 256:(q + 1) * 256] = res[:, q]
            return carry
        lax.fori_loop(0, 4, block, 0)

    def grad_cols(slot, lhs, rhs, mb):
        r = slice(mb * 256, (mb + 1) * 256)
        grads[slot, mb * 4:(mb + 1) * 4] = nn(lhs[r, :], rhs).astype(BF).reshape(4, 64, 512)

    def grad_out():
        for mb in range(2):
            res = nn(attt[mb * 256:(mb + 1) * 256, :], ag[l]).astype(BF).reshape(8, 32, 1024)
            for hh in range(2):
                grads[3, mb * 8:(mb + 1) * 8, hh * 32:(hh + 1) * 32, :] = res[:, :, hh * 512:(hh + 1) * 512]

    def attend_back(first, last):
        def pair(hp, carry):
            lanes = pl.ds(pl.multiple_of(hp * 128, 128), 128)
            q128, k128, v128 = qkv[0, :, lanes], qkv[1, :, lanes], qkv[2, :, lanes]
            o128 = datt[:, lanes]
            k_t = k128.T * scale
            d_k = d_v = None
            d_q = []
            for half in range(2):
                m = second_half if half else first_half
                work[0] = nt(k128 * (m * scale), q128)
                work[1] = nt(v128 * m, o128)
                l_row = lse[pl.ds(hp * 2 + half, 1), :]

                def some(i, dots):
                    r = pl.ds(pl.multiple_of(i * 32, 32), 32)
                    e = jnp.exp(work[0, r, :] + bias[r, :] - l_row)
                    work[0, r, :] = e
                    prob[0, r, :] = e.astype(BF)
                    return dots + jnp.sum((e * work[1, r, :]).reshape(4, 8, group), axis=0)
                dots = lax.fori_loop(0, group // 32, some, jnp.zeros((8, group), F32), unroll=True)
                r_row = jnp.sum(dots, axis=0, keepdims=True)

                def more(i, c):
                    r = pl.ds(pl.multiple_of(i * 32, 32), 32)
                    prob[1, r, :] = (work[0, r, :] * (work[1, r, :] - r_row)).astype(BF)
                    return c
                lax.fori_loop(0, group // 32, more, 0, unroll=True)
                dv_half = nn(prob[0], o128 * m)
                dk_half = nn(prob[1], q128 * m)
                d_v = dv_half if half == 0 else d_v + dv_half
                d_k = dk_half if half == 0 else d_k + dk_half
                d_q.append(nn(k_t[half * HEAD:(half + 1) * HEAD], prob[1]))
            dqkv[0, :, lanes] = jnp.concatenate(d_q, axis=0).T.astype(BF)
            dqkv[1, :, lanes] = (d_k * scale).astype(BF)
            dqkv[2, :, lanes] = d_v.astype(BF)
            return carry
        lax.fori_loop(first, last, pair, 0)

    for l in reversed(range(layers)):
        base = (layers - 1 - l) * 4
        need(("sec", l), ("inv", l))
        norm_back(sec, inv.at[1], None, l * 2 + 1, 4 + l * 4 + 3, 4 + l * 4 + 2, fg.at[l])
        for h in range(4):
            give_part(l, h, mine).start()
        if l > 0:
            load(("sec", l - 1), sec_i.at[l - 1], sec)
        need_down(l)
        need(("gp", l))
        hidden_back(l, mine)
        need(("hidt", l))
        for h in range(4):
            give_part(l, h, theirs).wait_recv()
            rs.free(rs.ready)
            grad_down(h)
            rs.ready += 1
            rs.tick()
        if l > 0:
            load(("hidt", l - 1), ht_i.at[l - 1], hidt)
        hidden_back(l, theirs)
        if l > 0:
            load_down(l - 1)
            load(("gp", l - 1), gp_i.at[l - 1], gp)
        need(("wu", l))
        if l < top:
            for nb in range(4):
                give_cols(l + 1, 1, nb).wait_send()
        for nb in range(4):
            sbuf[:, nb * 256:(nb + 1) * 256] = up_back(theirs, nb).astype(BF)
            give_cols(l, 0, nb).start()
        rs.tick()
        for nb in range(4):
            cols = slice(nb * 256, (nb + 1) * 256)
            dz[:, cols] = dz[:, cols] + up_back(mine, nb)
        if l > 0:
            load(("wu", l - 1), wg.at[pl.ds((l - 1) * CH + 4, 4)], wu)
        need(("ngt", l))
        rs.free(rs.ready + 3)
        for j in range(4):
            for mb in range(4):
                grad_cols(4 + j, ngt, dpre[:, j * 512:(j + 1) * 512], mb)
            res = nn(ones, dpre[:, j * 512:(j + 1) * 512])
            row, col = 16 + l * 2 + j // 2, (j % 2) * 512
            vacc[row:row + 1, col:col + 512] = res[0:1]
        if l > 0:
            load(("ngt", l - 1), nt_i.at[l - 1], ngt)
        rs.ready += 4
        rs.tick()
        need(("mix", l))
        for nb in range(4):
            give_cols(l, 0, nb).wait()
        norm_back(mix, inv.at[0], rbuf.at[l * 2], l * 2, 4 + l * 4 + 1, 4 + l * 4, ag.at[l])
        give_rows(ag.at[l, mine, :], base + 2).start()
        if l > 0:
            load(("mix", l - 1), mix_i.at[l - 1], mix)
            load(("inv", l - 1), inv_i.at[l - 1], inv)
        need(("o", l, 0), ("o", l, 1))
        w_o = wo[...].reshape(heads_w, -1)
        datt[mine, :] = nt(ag[l, mine, :], w_o).astype(BF)
        rs.tick()
        rs.tick()
        give_rows(ag.at[l, theirs, :], base + 2).wait_recv()
        datt[theirs, :] = nt(ag[l, theirs, :], w_o).astype(BF)
        if l > 0:
            load_out(l - 1)
        need(("attt", l))
        rs.free(rs.ready)
        grad_out()
        rs.ready += 1
        if l > 0:
            load(("attt", l - 1), attt_i.at[l - 1], attt)
        need(("qkv", l), ("lse", l))
        attend_back(0, 2)
        rs.tick()
        attend_back(2, 4)
        rs.tick()
        if l > 0:
            load(("qkv", l - 1), qkv_i.at[l - 1], qkv)
            load(("lse", l - 1), lse_i.at[l - 1], lse)
        need(("wqkv", l))
        for nb in range(4):
            sbuf[:, nb * 256:(nb + 1) * 256] = in_back(theirs, nb).astype(BF)
            give_cols(l, 1, nb).start()
        need(("xt", l))
        rs.free(rs.ready + 2)
        for m in range(3):
            for mb in range(4):
                grad_cols(m, xt, dqkv[m], mb)
            if m != 1:
                vacc[20 + l:21 + l, (m // 2) * 512:(m // 2) * 512 + 512] = nn(ones, dqkv[m])[0:1]
        rs.ready += 3
        rs.tick()
        for nb in range(4):
            cols = slice(nb * 256, (nb + 1) * 256)
            g[:, cols] = dz[:, cols] + in_back(mine, nb)
        if l > 0:
            load(("wqkv", l - 1), wg.at[pl.ds((l - 1) * CH, 3)], wqkv)
            load(("xt", l - 1), xt_i.at[l - 1], xt)
        rs.tick()
        for nb in range(4):
            give_cols(l, 1, nb).wait_recv()
        g[...] = g[...] + rbuf[l * 2 + 1].astype(F32)
    end = pltpu.make_async_copy(g, grad_o, e_sem.at[0])
    end.start()
    s_x = remote(vacc.at[0:16], vx, v_send.at[0], v_recv.at[0], p.peer)
    s_x.start()
    rs.tick()
    s_x.wait()
    vacc[0:16] = vacc[0:16] + vx[...]
    s_c = remote(vacc, vc, v_send.at[1], v_recv.at[1], p.twin)
    s_c.start()
    rs.tick()
    s_c.wait()
    vacc[...] = vacc[...] + vc[...]
    s_y = remote(vacc, vy, v_send.at[2], v_recv.at[2], p.side)
    s_y.start()
    rs.tick()
    s_y.wait()
    vacc[...] = vacc[...] + vy[...]
    s_z = [remote(vacc, vz.at[i - 1], v_send.at[2 + i], v_recv.at[2 + i], p.far(i)) for i in range(1, depth)]
    for copy in s_z:
        copy.start()
    rs.tick()
    for copy in s_z:
        copy.wait()
    total = vacc[...]
    for i in range(depth - 1):
        total = total + vz[i]
    vc[...] = total
    last = pltpu.make_async_copy(vc, vsum_o, e_sem.at[1])
    last.start()
    rs.finish()
    for nb in range(4):
        give_cols(0, 1, nb).wait_send()
    for l in range(layers):
        base = (layers - 1 - l) * 4
        for h in range(4):
            give_part(l, h, mine).wait_send()
        give_rows(ag.at[l, mine, :], base + 2).wait_send()
    end.wait()
    last.wait()


def backward_call(depth, layers, rows, vec, cot, segr, wg, saved):
    group, hw, fh = 2 * rows, 512, 2048
    vm = pltpu.VMEM
    dp = depth * 4
    n = layers * CH
    slots = 6
    shapes = [(rows, 1024), (24, 1024), (layers, 64, hw), (layers, 64, hw), (layers, 64, hw), (layers, 32, 1024),
              (layers, 64, fh), (layers, 128, 1024)]
    scratch = [vm((CH, dp, 64, 512), BF), vm((slots, depth, 2, 64, 512), BF), vm((slots, depth, 64, 512), BF),
               vm((slots, depth - 1, 64, 512), BF), vm((2, 64, 512), F32),
               vm((3, dp, 64, 512), BF), vm((dp, 32, 1024), BF), vm((4, dp, 64, 512), BF), vm((dp, 2, 64, 1024), BF)]
    scratch += [vm(s.shape[1:], s.dtype) for s in saved]
    scratch += [vm((group, fh), BF), vm((layers, group, 1024), BF), vm((layers, group, 1024), BF),
                vm((2 * layers, rows, 1024), BF), vm((rows, 1024), BF), vm((rows, 1024), F32), vm((rows, 1024), F32),
                vm((3, group, hw), BF), vm((group, hw), BF), vm((2, group, group), F32), vm((2, group, group), BF),
                vm((group, group), F32), vm((24, 1024), F32), vm((16, 1024), F32),
                vm((24, 1024), F32), vm((24, 1024), F32), vm((depth - 1, 24, 1024), F32)]
    dma = pltpu.SemaphoreType.DMA
    scratch += [dma((n, depth + 1)), dma((n, depth + 1)), dma((layers, 12)), dma((layers, 12)), dma((4 * layers,)), dma((4 * layers,)),
                dma((depth + 2,)), dma((depth + 2,)), dma((24 * layers,)), dma((2, 2)), dma((2,))]
    full = pl.BlockSpec(memory_space=pltpu.VMEM)
    hbm = pl.BlockSpec(memory_space=pl.ANY)
    return pl.pallas_call(
        functools.partial(bwd_kernel, depth, layers),
        out_shape=[jax.ShapeDtypeStruct(s, F32) for s in shapes],
        in_specs=[full] * 3 + [hbm] * (1 + len(saved)),
        out_specs=[hbm] * len(shapes),
        scratch_shapes=scratch,
        compiler_params=pltpu.CompilerParams(collective_id=2, has_side_effects=True, vmem_limit_bytes=63 * 2**20),
        cost_estimate=pl.CostEstimate(flops=28 * 10**9, bytes_accessed=60 * 10**6, transcendentals=0),
    )(vec, cot, segr, wg, *saved)


def finish_kernel(layers, vsum, *refs):
    n = 8
    srcs, dsts, qv, ub, gain, shift = refs[:n], refs[n:2 * n], *refs[2 * n:2 * n + 4]
    bufs, sem = refs[2 * n + 4:3 * n + 4], refs[-1]
    into = [pltpu.make_async_copy(s, b, sem.at[0, i]) for i, (s, b) in enumerate(zip(srcs, bufs))]
    away = [pltpu.make_async_copy(b, d, sem.at[1, i]) for i, (b, d) in enumerate(zip(bufs, dsts))]
    for copy in into:
        copy.start()
    dp, x = lax.axis_index("dp"), lax.axis_index("tensor")

    def part(row, count, block, slot):
        whole = vsum[row:row + count, pl.ds(pl.multiple_of(block * 128, 128), 128)]
        res = jnp.zeros((count, 32), F32)
        for i in range(4):
            res = jnp.where(slot == i, whole[:, i * 32:(i + 1) * 32], res)
        return res
    for l in range(layers):
        gain[l] = part(l * 2, 2, dp // 2, (dp % 2) * 2 + x)
        shift[l] = part(2 * layers + l * 4, 4, dp // 2, (dp % 2) * 2 + x)
        for i in range(2):
            qv[l, i:i + 1, :] = part(20 + l, 1, i * 4 + dp // 4, dp % 4)
        row = jnp.where(dp // 8 == 0, vsum[16 + l * 2:17 + l * 2, :], vsum[17 + l * 2:18 + l * 2, :])
        block = jnp.zeros((1, 128), F32)
        for i in range(8):
            block = jnp.where(dp % 8 == i, row[:, i * 128:(i + 1) * 128], block)
        ub[l:l + 1, :] = block
    for i in range(n):
        into[i].wait()
        away[i].start()
    for copy in away:
        copy.wait()


def finish_call(layers, vsum, *arrays):
    vm = pltpu.VMEM
    full = pl.BlockSpec(memory_space=pltpu.VMEM)
    hbm = pl.BlockSpec(memory_space=pl.ANY)
    small = [(layers, 2, 32), (layers, 128), (layers, 2, 32), (layers, 4, 32)]
    return pl.pallas_call(
        functools.partial(finish_kernel, layers),
        out_shape=[jax.ShapeDtypeStruct(a.shape, F32) for a in arrays] + [jax.ShapeDtypeStruct(s, F32) for s in small],
        in_specs=[full] + [hbm] * len(arrays),
        out_specs=[hbm] * len(arrays) + [full] * 4,
        scratch_shapes=[vm(a.shape, F32) for a in arrays] + [pltpu.SemaphoreType.DMA((2, len(arrays)))],
        compiler_params=pltpu.CompilerParams(vmem_limit_bytes=60 * 2**20),
    )(vsum, *arrays)


def on_device(
    tokens,
    cotangent,
    segment_ids,
    w_query,
    w_key,
    w_value,
    w_out,
    w_up,
    w_down,
    qv_bias,
    up_bias,
    norm_gain,
    shift_bias,
):
    layers = w_query.shape[0]
    rows = tokens.shape[0]
    depth = lax.axis_size("dp") // 4
    segr = segment_ids[None, :]
    wg, vec, out, *saved = forward_call(
        depth, layers, rows, norm_gain, shift_bias, qv_bias, up_bias, tokens, segr,
        w_query, w_key, w_value, w_out, w_up, w_down
    )
    grad, vsum, *grads = backward_call(depth, layers, rows, vec, cotangent, segr, wg, saved)
    return finish_call(layers, vsum, out, grad, *grads)


def on_any_mesh(
    tokens,
    cotangent,
    segment_ids,
    w_query,
    w_key,
    w_value,
    w_out,
    w_up,
    w_down,
    qv_bias,
    up_bias,
    norm_gain,
    shift_bias,
):
    layers = w_query.shape[0]
    group = segment_ids.shape[0]
    seq = min(LEN, group)
    segs = segment_ids.reshape(group // seq, seq)
    stream = tokens.astype(jnp.float32)
    kept_all = []
    mats_all = []
    vecs_all = []
    for layer in range(layers):
        mats = (
            lax.all_gather(w_query[layer], "dp", axis=0, tiled=True),
            lax.all_gather(w_key[layer], "dp", axis=0, tiled=True),
            lax.all_gather(w_value[layer], "dp", axis=0, tiled=True),
            lax.all_gather(w_out[layer], "dp", axis=0, tiled=True),
            lax.all_gather(w_up[layer], "dp", axis=0, tiled=True),
            lax.all_gather(w_down[layer], "dp", axis=0, tiled=True),
            lax.all_gather(qv_bias[layer], "dp", axis=1, tiled=True),
            lax.all_gather(up_bias[layer], "dp", axis=0, tiled=True),
        )
        vecs = (
            lax.all_gather(norm_gain[layer], ("dp", "tensor"), axis=1, tiled=True),
            lax.all_gather(shift_bias[layer], ("dp", "tensor"), axis=1, tiled=True),
        )
        stream, kept = forward_layer(stream, mats, vecs, segs, seq)
        kept_all.append(kept)
        mats_all.append(mats)
        vecs_all.append(vecs)
    grad = cotangent.astype(jnp.float32)
    mat_shards = [None] * layers
    vec_shards = [None] * layers
    for layer in reversed(range(layers)):
        mats = (
            lax.all_gather(w_query[layer], "dp", axis=0, tiled=True),
            lax.all_gather(w_key[layer], "dp", axis=0, tiled=True),
            lax.all_gather(w_value[layer], "dp", axis=0, tiled=True),
            lax.all_gather(w_out[layer], "dp", axis=0, tiled=True),
            lax.all_gather(w_up[layer], "dp", axis=0, tiled=True),
            lax.all_gather(w_down[layer], "dp", axis=0, tiled=True),
            lax.all_gather(qv_bias[layer], "dp", axis=1, tiled=True),
            lax.all_gather(up_bias[layer], "dp", axis=0, tiled=True),
        )
        grad, mat_grads, vec_grads = backward_layer(
            grad, mats, vecs_all[layer], kept_all[layer], segs, seq
        )
        g_q, g_k, g_v, g_o, g_u, g_d, g_qv, g_ub = mat_grads
        mat_shards[layer] = (
            lax.psum_scatter(
                g_q.astype(jnp.bfloat16), "dp", scatter_dimension=0, tiled=True
            ).astype(jnp.float32),
            lax.psum_scatter(
                g_k.astype(jnp.bfloat16), "dp", scatter_dimension=0, tiled=True
            ).astype(jnp.float32),
            lax.psum_scatter(
                g_v.astype(jnp.bfloat16), "dp", scatter_dimension=0, tiled=True
            ).astype(jnp.float32),
            lax.psum_scatter(
                g_o.astype(jnp.bfloat16), "dp", scatter_dimension=0, tiled=True
            ).astype(jnp.float32),
            lax.psum_scatter(
                g_u.astype(jnp.bfloat16), "dp", scatter_dimension=0, tiled=True
            ).astype(jnp.float32),
            lax.psum_scatter(
                g_d.astype(jnp.bfloat16), "dp", scatter_dimension=0, tiled=True
            ).astype(jnp.float32),
            lax.psum_scatter(
                g_qv.astype(jnp.bfloat16), "dp", scatter_dimension=1, tiled=True
            ).astype(jnp.float32),
            lax.psum_scatter(
                g_ub.astype(jnp.bfloat16), "dp", scatter_dimension=0, tiled=True
            ).astype(jnp.float32),
        )
        g_gain, g_shift = vec_grads
        vec_shards[layer] = (
            lax.psum_scatter(g_gain, ("dp", "tensor"), scatter_dimension=1, tiled=True),
            lax.psum_scatter(g_shift, ("dp", "tensor"), scatter_dimension=1, tiled=True),
        )

    def stacked(index, source):
        return jnp.stack([entry[index] for entry in source])

    return (
        stream,
        grad,
        stacked(0, mat_shards),
        stacked(1, mat_shards),
        stacked(2, mat_shards),
        stacked(3, mat_shards),
        stacked(4, mat_shards),
        stacked(5, mat_shards),
        stacked(6, mat_shards),
        stacked(7, mat_shards),
        stacked(0, vec_shards),
        stacked(1, vec_shards),
    )


def solution(mesh):
    in_specs = (
        P(("dp", "tensor"), None),
        P(("dp", "tensor"), None),
        P("dp"),
        P(None, "dp", "tensor"),
        P(None, "dp", "tensor"),
        P(None, "dp", "tensor"),
        P(None, ("tensor", "dp"), None),
        P(None, "dp", "tensor"),
        P(None, ("tensor", "dp"), None),
        P(None, None, ("tensor", "dp")),
        P(None, ("tensor", "dp")),
        P(None, None, ("dp", "tensor")),
        P(None, None, ("dp", "tensor")),
    )
    out_specs = (
        P(("dp", "tensor"), None),
        P(("dp", "tensor"), None),
        P(None, "dp", "tensor"),
        P(None, "dp", "tensor"),
        P(None, "dp", "tensor"),
        P(None, ("tensor", "dp"), None),
        P(None, "dp", "tensor"),
        P(None, ("tensor", "dp"), None),
        P(None, None, ("tensor", "dp")),
        P(None, ("tensor", "dp")),
        P(None, None, ("dp", "tensor")),
        P(None, None, ("dp", "tensor")),
    )
    small = mesh.shape["tensor"] == 2 and mesh.shape["dp"] == 16
    return jax.shard_map(
        on_device if small else on_any_mesh, mesh=mesh, in_specs=in_specs, out_specs=out_specs, check_vma=False
    )
```

```python
import functools
import math

import jax
import jax.numpy as jnp
from jax import lax
from jax.experimental import pallas as pl
from jax.experimental.pallas import tpu as pltpu
from jax.sharding import PartitionSpec as P

HEAD = 64
LEN = 512


EPS = 1e-06
NEG = -1e30


def layer_norm(z, gain, shift):
    mean = jnp.mean(z, axis=-1, keepdims=True)
    cent = z - mean
    var = jnp.mean(cent * cent, axis=-1, keepdims=True)
    return cent * lax.rsqrt(var + EPS) * gain + shift


def gelu_exact(pre):
    return jax.nn.gelu(pre, approximate=False)


def inner(left, right):
    return lax.dot_general(
        left, right, (((0,), (0,)), ((), ())), preferred_element_type=jnp.float32
    )


def times_back(left, right):
    return lax.dot_general(
        left, right, (((1,), (1,)), ((), ())), preferred_element_type=jnp.float32
    )


def gather_rows(rows):
    return lax.all_gather(rows, "tensor", axis=0, tiled=True)


def gather_grads(rows):
    return lax.all_gather(rows, "tensor", axis=0, tiled=True)


def sum_rows(term, rows):
    return lax.psum_scatter(
        term(jnp.int32(0), lax.axis_size("tensor") * rows).astype(jnp.bfloat16),
        "tensor",
        scatter_dimension=0,
        tiled=True,
    ).astype(jnp.float32)


def sum_grads(term, rows):
    return lax.psum_scatter(
        term(jnp.int32(0), lax.axis_size("tensor") * rows).astype(jnp.bfloat16),
        "tensor",
        scatter_dimension=0,
        tiled=True,
    ).astype(jnp.float32)


def allowed(segment):
    return segment[:, None] == segment[None, :]


def attend_one(args):
    query, key, value, segment = args
    scale = HEAD ** (-0.5)
    scores = jnp.einsum("qhd,khd->hqk", query, key, preferred_element_type=jnp.float32) * scale
    scores = jnp.where(allowed(segment)[None], scores, NEG)
    top = jnp.max(scores, axis=-1, keepdims=True)
    total = top + jnp.log(jnp.sum(jnp.exp(scores - top), axis=-1, keepdims=True))
    probs = jnp.exp(scores - total).astype(jnp.bfloat16)
    result = jnp.einsum("hqk,khd->qhd", probs, value, preferred_element_type=jnp.float32)
    return (result.astype(jnp.bfloat16), total[..., 0])


def attend_back(args):
    query, key, value, segment, total, d_att = args
    scale = HEAD ** (-0.5)
    scores = jnp.einsum("qhd,khd->hqk", query, key, preferred_element_type=jnp.float32) * scale
    scores = jnp.where(allowed(segment)[None], scores, NEG)
    probs = jnp.exp(scores - total[..., None])
    d_probs = jnp.einsum("qhd,khd->hqk", d_att, value, preferred_element_type=jnp.float32)
    row_dot = jnp.sum(d_probs * probs, axis=-1, keepdims=True)
    d_scores = (probs * (d_probs - row_dot)).astype(jnp.bfloat16)
    d_query = (
        jnp.einsum("hqk,khd->qhd", d_scores, key, preferred_element_type=jnp.float32) * scale
    ).astype(jnp.bfloat16)
    d_key = (
        jnp.einsum("hqk,qhd->khd", d_scores, query, preferred_element_type=jnp.float32) * scale
    ).astype(jnp.bfloat16)
    d_value = jnp.einsum(
        "hqk,qhd->khd", probs.astype(jnp.bfloat16), d_att, preferred_element_type=jnp.float32
    ).astype(jnp.bfloat16)
    return (d_query, d_key, d_value)


def forward_layer(stream, mats, vecs, segs, seq):
    w_q, w_k, w_v, w_o, w_u, w_d, qvb, upb = mats
    gains, shifts = vecs
    seqs = segs.shape[0]
    rows = stream.shape[0]
    x_rows = gather_rows(stream.astype(jnp.bfloat16))
    query = (
        jnp.dot(x_rows, w_q, preferred_element_type=jnp.float32) + qvb[0].astype(jnp.float32)
    ).astype(jnp.bfloat16)
    key = jnp.dot(x_rows, w_k, preferred_element_type=jnp.float32).astype(jnp.bfloat16)
    value = (
        jnp.dot(x_rows, w_v, preferred_element_type=jnp.float32) + qvb[1].astype(jnp.float32)
    ).astype(jnp.bfloat16)
    width = query.shape[1]
    local_heads = width // HEAD

    def split(matrix):
        return matrix.reshape(seqs, seq, local_heads, HEAD)

    attended, totals = lax.map(attend_one, (split(query), split(key), split(value), segs))
    attended = attended.reshape(seqs * seq, width)

    def out_term(start, count):
        return jnp.dot(attended, w_o, preferred_element_type=jnp.float32)

    out_sum = sum_rows(out_term, rows)
    mixed = stream + out_sum + shifts[0]
    normed = layer_norm(mixed, gains[0], shifts[1])
    n_rows = gather_rows(normed.astype(jnp.bfloat16))
    pre = jnp.dot(n_rows, w_u, preferred_element_type=jnp.float32) + upb.astype(jnp.float32)
    hidden = gelu_exact(pre).astype(jnp.bfloat16)

    def down_term(start, count):
        return jnp.dot(hidden, w_d, preferred_element_type=jnp.float32)

    down_sum = sum_rows(down_term, rows)
    second = normed + down_sum + shifts[2]
    result = layer_norm(second, gains[1], shifts[3])
    kept = (x_rows, query, key, value, attended, totals, mixed, n_rows, pre, hidden, second)
    return (result, kept)


def backward_layer(grad, mats, vecs, kept, segs, seq):
    w_q, w_k, w_v, w_o, w_u, w_d, qvb, upb = mats
    gains, shifts = vecs
    x_rows, query, key, value, attended, totals, mixed, n_rows, pre, hidden, second = kept
    seqs = segs.shape[0]
    rows = grad.shape[0]
    width = query.shape[1]
    local_heads = width // HEAD

    def split(matrix):
        return matrix.reshape(seqs, seq, local_heads, HEAD)

    _, pull_second = jax.vjp(layer_norm, second, gains[1], shifts[3])
    d_second, d_gain_two, d_shift_two = pull_second(grad)
    d_down_bias = jnp.sum(d_second, axis=0)
    d_f = gather_grads(d_second.astype(jnp.bfloat16))
    grad_down = inner(hidden, d_f)
    d_hidden = times_back(d_f, w_d)
    _, pull_gelu = jax.vjp(gelu_exact, pre)
    d_pre = pull_gelu(d_hidden)[0].astype(jnp.bfloat16)
    grad_up = inner(n_rows, d_pre)
    d_up_bias = jnp.sum(d_pre.astype(jnp.float32), axis=0)

    def up_term(start, count):
        return times_back(d_pre, w_u)

    d_normed = d_second + sum_grads(up_term, rows)
    _, pull_first = jax.vjp(layer_norm, mixed, gains[0], shifts[1])
    d_mixed, d_gain_one, d_shift_one = pull_first(d_normed)
    d_out_bias = jnp.sum(d_mixed, axis=0)
    d_a = gather_grads(d_mixed.astype(jnp.bfloat16))
    grad_out = inner(attended, d_a)
    d_att = times_back(d_a, w_o).astype(jnp.bfloat16)
    d_query, d_key, d_value = lax.map(
        attend_back, (split(query), split(key), split(value), segs, totals, split(d_att))
    )
    d_query = d_query.reshape(seqs * seq, width)
    d_key = d_key.reshape(seqs * seq, width)
    d_value = d_value.reshape(seqs * seq, width)
    grad_q = inner(x_rows, d_query)
    grad_k = inner(x_rows, d_key)
    grad_v = inner(x_rows, d_value)
    d_qv = jnp.stack(
        [jnp.sum(d_query.astype(jnp.float32), axis=0), jnp.sum(d_value.astype(jnp.float32), axis=0)]
    )

    def in_term(start, count):
        part = times_back(d_query, w_q)
        part = part + times_back(d_key, w_k)
        return part + times_back(d_value, w_v)

    d_stream = d_mixed + sum_grads(in_term, rows)
    mat_grads = (grad_q, grad_k, grad_v, grad_out, grad_up, grad_down, d_qv, d_up_bias)
    vec_grads = (
        jnp.stack([d_gain_one, d_gain_two]),
        jnp.stack([d_out_bias, d_shift_one, d_down_bias, d_shift_two]),
    )
    return (d_stream, mat_grads, vec_grads)


MESH = pl.DeviceIdType.MESH
BF = jnp.bfloat16
F32 = jnp.float32
AHEAD = 2
EARLY = 2
LATER, MORE, SIDE = 8, 2, 1
KEPT = ("vec", "xt", "qkv", "attt", "lse", "mix", "ngt", "hidt", "gp", "sec", "inv", "out")
CH = 12


def nt(left, right):
    return lax.dot_general(left, right, (((1,), (1,)), ((), ())), preferred_element_type=F32)


def nn(left, right):
    return lax.dot_general(left, right, (((1,), (0,)), ((), ())), preferred_element_type=F32)


def tn(left, right):
    return lax.dot_general(left, right, (((0,), (0,)), ((), ())), preferred_element_type=F32)


def remote(src, dst, send_sem, recv_sem, device):
    return pltpu.make_async_remote_copy(
        src_ref=src, dst_ref=dst, send_sem=send_sem, recv_sem=recv_sem, device_id=device, device_id_type=MESH
    )


class Place:
    def __init__(self, depth):
        self.depth = depth
        self.dp = lax.axis_index("dp")
        self.x = lax.axis_index("tensor")
        self.z = self.dp // 4
        self.y = (self.dp // 2) % 2
        self.c = self.dp % 2

    def at(self, z, y, c):
        return {"dp": z * 4 + y * 2 + c, "tensor": self.x}

    def far(self, step):
        return self.at((self.z + step) % self.depth, self.y, self.c)

    def before(self, step):
        return (self.z + self.depth - step) % self.depth

    @property
    def side(self):
        return self.at(self.z, 1 - self.y, self.c)

    @property
    def twin(self):
        return self.at(self.z, self.y, 1 - self.c)

    @property
    def peer(self):
        return {"dp": self.dp, "tensor": 1 - self.x}

    def greet(self):
        partners = [self.far(i) for i in range(1, self.depth)] + [self.side, self.twin, self.peer]
        for device in partners:
            pl.semaphore_signal(pltpu.get_barrier_semaphore(), inc=1, device_id=device, device_id_type=MESH)

    def met(self):
        pl.semaphore_wait(pltpu.get_barrier_semaphore(), self.depth + 2)


class Gather:
    def __init__(self, place, wg, own, keep, send, recv, total):
        self.p, self.wg, self.own, self.keep, self.send, self.recv, self.total = place, wg, own, keep, send, recv, total
        self.view = wg.reshape(wg.shape[0], place.depth, 2, 2, *wg.shape[2:])
        self.time = 0
        self.have = self.given = 0

    def far(self, k, i):
        p = self.p
        return remote(self.wg.at[k, p.dp], self.wg.at[k, p.dp], self.send.at[k, i - 1], self.recv.at[k, i - 1], p.far(i))

    def far_in(self, k, i):
        p = self.p
        ref = self.wg.at[k, p.before(i) * 4 + p.y * 2 + p.c]
        return remote(ref, ref, self.send.at[k, i - 1], self.recv.at[k, i - 1], p.far(i))

    def side(self, k, y):
        p, d = self.p, self.p.depth - 1
        ref = self.view.at[k, :, y, p.c]
        return remote(ref, ref, self.send.at[k, d], self.recv.at[k, d], p.side)

    def side_part(self, k, i, y):
        p, d = self.p, self.p.depth + 1 + i
        ref = self.view.at[k, (p.z + i) % p.depth, y, p.c]
        return remote(ref, ref, self.send.at[k, d], self.recv.at[k, d], p.side)

    def sides(self, k, y):
        if k < EARLY:
            return [self.side_part(k, i, y) for i in range(self.p.depth)]
        return [self.side(k, y)]

    def twin(self, k, c):
        p, d = self.p, self.p.depth
        ref = self.view.at[k, :, :, c]
        return remote(ref, ref, self.send.at[k, d], self.recv.at[k, d], p.twin)

    def launch(self, k):
        for copy in self.own[k]:
            copy.wait()
        for i in range(1, self.p.depth):
            self.far(k, i).start()

    def begin(self, ahead):
        self.ahead = self.sent = ahead
        for k in range(ahead):
            self.launch(k)
            if k < EARLY:
                self.side_part(k, 0, self.p.y).start()

    def tick(self):
        t, n = self.time, self.total
        lag = SIDE if t >= LATER else 1
        if self.have == n:
            return
        while self.sent < min(n, t + 1 + (MORE if t >= LATER else self.ahead)):
            self.launch(self.sent)
            self.sent += 1
        if t < n:
            for i in range(1, self.p.depth):
                self.far_in(t, i).wait_recv()
                if t < EARLY:
                    self.side_part(t, self.p.depth - i, self.p.y).start()
            if t >= EARLY:
                self.side(t, self.p.y).start()
        while self.given <= min(t - lag, n - 1):
            for copy in self.sides(self.given, 1 - self.p.y):
                copy.wait_recv()
            self.twin(self.given, self.p.c).start()
            self.given += 1
        while self.have <= min(t - lag - 1, n - 1):
            self.twin(self.have, 1 - self.p.c).wait_recv()
            self.keep(self.have)
            self.have += 1
        self.time += 1

    def until(self, count):
        while self.have < count:
            self.tick()

    def finish(self):
        self.until(self.total)
        for k in range(self.total):
            for i in range(1, self.p.depth):
                self.far(k, i).wait_send()
            for copy in self.sides(k, self.p.y):
                copy.wait_send()
            self.twin(k, self.p.c).wait_send()


def norm_rows(z, gain, shift):
    mean = jnp.mean(z, axis=-1, keepdims=True)
    cent = z - mean
    inv = lax.rsqrt(jnp.mean(cent * cent, axis=-1, keepdims=True) + EPS)
    hat = cent * inv
    return hat * gain + shift, hat, jnp.broadcast_to(inv, (z.shape[0], 128))


def mask_bias(segr, bias):
    seg = segr[...].astype(F32)
    n = seg.shape[1]
    column = jnp.broadcast_to(seg, (8, n)).T
    for i in range(n // 64):
        r = slice(i * 64, (i + 1) * 64)
        bias[r, :] = jnp.where(column[r, 0:1] == seg, 0.0, NEG)


def fwd_kernel(depth, layers, gains, shifts, qvb, upb, tok, segr, w_query, w_key, w_value, w_out, w_up, w_down,
               wg_o, vec_o, out_o, xt_o, qkv_o, attt_o, lse_o, mix_o, nt_o, ht_o, gp_o, sec_o, inv_o,
               wg, vg, vec, stream, normed, bias, work, prob, xt, qkv, attt, lse, mix, ngt, hidt, gp, sec, inv,
               xg, ng, hid, att, sbuf, rbuf,
               w_send, w_recv, v_send, v_recv, d_send, d_recv, x_send, x_recv, o_sem, k_sem, own_sem):
    p = Place(depth)
    x = p.x
    rows = tok.shape[0]
    group = 2 * rows
    heads_w = qkv.shape[-1]
    mine = pl.ds(pl.multiple_of(x * rows, rows), rows)
    theirs = pl.ds(pl.multiple_of((1 - x) * rows, rows), rows)
    n_chunks = layers * CH

    def keep_chunk(k):
        pltpu.make_async_copy(wg.at[k], wg_o.at[k], k_sem.at[k]).start()

    shards = []
    for l in range(layers):
        c0 = l * CH
        pairs = [[(w.at[l], wg.at[c0 + m, p.dp])] for m, w in enumerate((w_query, w_key, w_value))]
        pairs.append([(w_out.at[l, :, hh * 512:(hh + 1) * 512], wg.at[c0 + 3, p.dp, hh * 32:(hh + 1) * 32, :])
                      for hh in range(2)])
        for j in range(4):
            pairs.append([(w_up.at[l, :, j * 512:(j + 1) * 512], wg.at[c0 + 4 + j, p.dp])])
        for j in range(4):
            pairs.append([(w_down.at[l, q * 64:(q + 1) * 64, j * 256:(j + 1) * 256],
                           wg.at[c0 + 8 + j, p.dp, :, q * 256:(q + 1) * 256]) for q in range(2)])
        for k, chunk in enumerate(pairs):
            shards.append([pltpu.make_async_copy(a, b, own_sem.at[c0 + k, i]) for i, (a, b) in enumerate(chunk)])
    p.greet()
    for chunk in shards[:4]:
        for copy in chunk:
            copy.start()
    gat = Gather(p, wg, shards, keep_chunk, w_send, w_recv, n_chunks)
    own = vg.at[x, p.z, p.y, p.c]
    lane = lax.broadcasted_iota(jnp.int32, (1, 128), 1)

    def spread(row, slot):
        row = jnp.concatenate([row.astype(F32)] * 4, axis=1)
        return jnp.where(jnp.logical_and(lane >= slot * 32, lane < slot * 32 + 32), row, 0.0)

    own[...] = jnp.zeros((32, 128), F32)
    for l in range(layers):
        own[l * 2:l * 2 + 2, :] = spread(gains[l], (p.c * 2 + x) % 4)
        own[2 * layers + l * 4:2 * layers + l * 4 + 4, :] = spread(shifts[l], (p.c * 2 + x) % 4)
        own[16 + l * 2:18 + l * 2, :] = spread(qvb[l], p.dp % 4)
        own[24 + l:25 + l, :] = upb[l:l + 1, :].astype(F32)
    xg[0, mine, :] = tok[...]
    p.met()

    def give_block(ref, l, side, which, i):
        r = pl.ds(pl.multiple_of(side * rows + i * (rows // 2), rows // 2), rows // 2)
        n = l * 4 + which + i
        return remote(ref.at[l, r, :], ref.at[l, r, :], x_send.at[n], x_recv.at[n], p.peer)

    v_far = [remote(vg.at[x, p.z, p.y, p.c], vg.at[x, p.z, p.y, p.c], v_send.at[i - 1], v_recv.at[i - 1], p.far(i))
             for i in range(1, depth)]
    for copy in v_far:
        copy.start()
    for i in range(2):
        give_block(xg, 0, x, 0, i).start()
    gat.begin(AHEAD)
    for chunk in shards[4:]:
        for copy in chunk:
            copy.start()

    stream[...] = tok[...].astype(F32)
    mask_bias(segr, bias)
    for copy in v_far:
        copy.wait_recv()
    v_side = remote(vg.at[x, :, p.y, p.c], vg.at[x, :, p.y, p.c], v_send.at[depth - 1], v_recv.at[depth - 1], p.side)
    v_side.start()
    v_side.wait_recv()
    v_twin = remote(vg.at[x, :, :, p.c], vg.at[x, :, :, p.c], v_send.at[depth], v_recv.at[depth], p.twin)
    v_twin.start()
    v_twin.wait_recv()
    v_peer = remote(vg.at[x], vg.at[x], v_send.at[depth + 1], v_recv.at[depth + 1], p.peer)
    v_peer.start()
    gat.tick()
    v_peer.wait_recv()
    for z in range(depth):
        for y in range(2):
            b = (z * 2 + y) * 128
            vec[0:16, b:b + 128] = (vg[0, z, y, 0, 0:16] + vg[0, z, y, 1, 0:16]
                                    + vg[1, z, y, 0, 0:16] + vg[1, z, y, 1, 0:16])
    for z in range(depth):
        for_half = vg[x, z, 0, 0, 16:24] + vg[x, z, 0, 1, 16:24] + vg[x, z, 1, 0, 16:24] + vg[x, z, 1, 1, 16:24]
        vec[16:24, z * 128:(z + 1) * 128] = for_half
        for y in range(2):
            for c in range(2):
                b = (z * 4 + y * 2 + c) * 128
                vec[24:32, b:b + 128] = vg[x, z, y, c, 24:32]
    kept = {}

    def keep(name, src, dst):
        copy = pltpu.make_async_copy(src, dst, o_sem.at[KEPT.index(name)])
        copy.start()
        kept[name] = copy

    def fresh(name):
        if name in kept:
            kept.pop(name).wait()

    keep("vec", vec, vec_o)

    def give_half(l, hh):
        cols = slice(hh * 512, (hh + 1) * 512)
        return remote(sbuf.at[:, cols], rbuf.at[l * 2, :, cols], d_send.at[l, 4 + hh], d_recv.at[l, 4 + hh], p.peer)

    def give_part(l, h):
        cols = slice(h * 256, (h + 1) * 256)
        return remote(sbuf.at[:, cols], rbuf.at[l * 2 + 1, :, cols], d_send.at[l, h], d_recv.at[l, h], p.peer)

    def gain(l, i):
        r = l * 2 + i
        return vec[r:r + 1, 0:1024]

    def shift(l, i):
        r = 4 + l * 4 + i
        return vec[r:r + 1, 0:1024]

    def project(l, r):
        for m in range(3):
            w = wg[l * CH + m].reshape(-1, heads_w)
            res = nn(xg[l, r, :], w)
            if m != 1:
                b = 16 + l * 2 + (m // 2)
                res = res + vec[b:b + 1, 0:heads_w]
            qkv[m, r, :] = res.astype(BF)

    half_lane = lax.broadcasted_iota(jnp.int32, (1, 128), 1) < HEAD
    first_half = jnp.where(half_lane, 1.0, 0.0).astype(BF)
    second_half = jnp.where(half_lane, 0.0, 1.0).astype(BF)
    scale = HEAD ** -0.5

    def attend(q_rows):
        def pair(hp, carry):
            lanes = pl.ds(pl.multiple_of(hp * 128, 128), 128)
            k128 = qkv[1, :, lanes]
            v_t = qkv[2, :, lanes].T
            q128 = qkv[0, q_rows, lanes]
            both = []
            for half in range(2):
                k_half = k128 * ((second_half if half else first_half) * scale)
                work[half] = nt(k_half, q128)
                top = jnp.full((8, rows), NEG, F32)
                for i in range(group // 64):
                    r = slice(i * 64, (i + 1) * 64)
                    s = work[half, r, :] + bias[r, q_rows]
                    work[half, r, :] = s
                    top = jnp.maximum(top, jnp.max(s.reshape(8, 8, rows), axis=0))
                top = jnp.max(top, axis=0, keepdims=True)
                tot = jnp.zeros((8, rows), F32)
                for i in range(group // 64):
                    r = slice(i * 64, (i + 1) * 64)
                    e = jnp.exp(work[half, r, :] - top)
                    tot = tot + jnp.sum(e.reshape(8, 8, rows), axis=0)
                    prob[half, r, :] = e.astype(BF)
                tot = jnp.sum(tot, axis=0, keepdims=True)
                lse[pl.ds(hp * 2 + half, 1), q_rows] = top + jnp.log(tot)
                both.append(nn(v_t[half * HEAD:(half + 1) * HEAD], prob[half]) / tot)
            o_t = jnp.concatenate(both, axis=0)
            attt[lanes, q_rows] = o_t.astype(BF)
            att[q_rows, lanes] = o_t.T.astype(BF)
            return carry
        lax.fori_loop(0, heads_w // 128, pair, 0)

    def out_term(l, r, hh):
        return nn(att[r, :], wg[l * CH + 3, :, hh * 32:(hh + 1) * 32, :].reshape(heads_w, 512))

    def flip(src, dst):
        def block(i, carry):
            c = pl.ds(pl.multiple_of(i * 256, 256), 256)
            dst[c, :] = src[:, c].T
            return carry
        lax.fori_loop(0, src.shape[1] // 256, block, 0)

    inv_sqrt2 = 2.0 ** -0.5
    inv_sqrt_2pi = (2.0 * math.pi) ** -0.5

    def up(l, j):
        b = 24 + l
        for cb in range(2):
            cols = slice(j * 512 + cb * 256, j * 512 + (cb + 1) * 256)
            w = wg[l * CH + 4 + j, :, :, cb * 256:(cb + 1) * 256].reshape(-1, 256)
            work[cb] = nn(ng[l], w) + vec[b:b + 1, cols]

            def some(i, carry):
                r = pl.ds(pl.multiple_of(i * 32, 32), 32)
                pre = work[cb, r, :]
                part = 0.5 + 0.5 * lax.erf(pre * inv_sqrt2)
                hid[r, cols] = (pre * part).astype(BF)
                gp[r, cols] = (part + pre * jnp.exp(-0.5 * pre * pre) * inv_sqrt_2pi).astype(BF)
                return carry
            lax.fori_loop(0, group // 32, some, 0)

    def down_term(l, r, h):
        w = wg[l * CH + 8 + h]
        w = jnp.stack([w[:, :, 0:256], w[:, :, 256:512]], axis=1).reshape(-1, 256)
        return nn(hid[r, :], w)

    for l in range(layers):
        c0 = l * CH
        gat.until(c0 + 3)
        fresh("qkv")
        project(l, mine)
        if l > 0:
            gat.tick()
        for i in range(2):
            give_block(xg, l, 1 - x, 0, i).wait_recv()
        project(l, theirs)
        keep("qkv", qkv, qkv_o.at[l])
        fresh("lse")
        fresh("attt")
        attend(theirs)
        gat.until(c0 + 4)
        for hh in range(2):
            sbuf[:, hh * 512:(hh + 1) * 512] = out_term(l, theirs, hh).astype(BF)
            give_half(l, hh).start()
        gat.tick()
        attend(mine)
        keep("lse", lse, lse_o.at[l])
        keep("attt", attt, attt_o.at[l])
        fresh("mix")
        for hh in range(2):
            cols = slice(hh * 512, (hh + 1) * 512)
            mix[:, cols] = stream[:, cols] + out_term(l, mine, hh) + shift(l, 0)[:, cols]
        gat.tick()
        fresh("xt")
        flip(xg.at[l], xt)
        keep("xt", xt, xt_o.at[l])
        gat.tick()
        for hh in range(2):
            give_half(l, hh).wait()

        fresh("inv")

        def first_norm(i, carry):
            r = pl.ds(pl.multiple_of(i * 32, 32), 32)
            mixed = mix[r, :] + rbuf[l * 2, r, :].astype(F32)
            res, mix[r, :], inv[0, r, :] = norm_rows(mixed, gain(l, 0), shift(l, 1))
            normed[r, :] = res
            ng[l, pl.ds(pl.multiple_of(x * rows + i * 32, 32), 32), :] = res.astype(BF)
            return carry
        for i in range(2):
            lax.fori_loop(i * rows // 64, (i + 1) * rows // 64, first_norm, 0)
            give_block(ng, l, x, 2, i).start()
        keep("mix", mix, mix_o.at[l])
        gat.tick()
        gat.tick()
        for i in range(2):
            give_block(ng, l, 1 - x, 2, i).wait_recv()
        fresh("gp")
        for j in range(4):
            gat.until(c0 + 5 + j)
            up(l, j)
            if j % 2:
                gat.tick()
        keep("gp", gp, gp_o.at[l])
        for h in range(4):
            gat.until(c0 + 9 + h)
            cols = slice(h * 256, (h + 1) * 256)
            sbuf[:, cols] = down_term(l, theirs, h).astype(BF)
            give_part(l, h).start()
            if h == 0:
                fresh("sec")
            sec[:, cols] = normed[:, cols] + down_term(l, mine, h) + shift(l, 2)[:, cols]
        fresh("ngt")
        flip(ng.at[l], ngt)
        keep("ngt", ngt, nt_o.at[l])
        fresh("hidt")
        flip(hid, hidt)
        keep("hidt", hidt, ht_o.at[l])
        for h in range(4):
            give_part(l, h).wait()

        def second_norm(i, carry):
            r = pl.ds(pl.multiple_of(i * 32, 32), 32)
            second = sec[r, :] + rbuf[l * 2 + 1, r, :].astype(F32)
            res, sec[r, :], inv[1, r, :] = norm_rows(second, gain(l, 1), shift(l, 3))
            stream[r, :] = res
            if l + 1 < layers:
                xg[l + 1, pl.ds(pl.multiple_of(x * rows + i * 32, 32), 32), :] = res.astype(BF)
            return carry
        for i in range(2):
            lax.fori_loop(i * rows // 64, (i + 1) * rows // 64, second_norm, 0)
            if l + 1 < layers:
                give_block(xg, l + 1, x, 0, i).start()
        keep("sec", sec, sec_o.at[l])
        keep("inv", inv, inv_o.at[l])
    keep("out", stream, out_o)
    gat.finish()
    for copy in v_far + [v_side, v_twin, v_peer]:
        copy.wait_send()
    for l in range(layers):
        for i in range(2):
            give_block(xg, l, x, 0, i).wait_send()
            give_block(ng, l, x, 2, i).wait_send()
    for name in list(kept):
        fresh(name)
    for k in range(n_chunks):
        pltpu.make_async_copy(wg.at[k], wg_o.at[k], k_sem.at[k]).wait()


def forward_call(depth, layers, rows, gains, shifts, qvb, upb, tok, segr, *weights):
    group, hw, fh = 2 * rows, 512, 2048
    vm = pltpu.VMEM
    saved = [((layers, 1024, group), BF), ((layers, 3, group, hw), BF), ((layers, hw, group), BF),
             ((layers, 8, group), F32), ((layers, rows, 1024), F32), ((layers, 1024, group), BF),
             ((layers, fh, group), BF), ((layers, group, fh), BF), ((layers, rows, 1024), F32),
             ((layers, 2, rows, 128), F32)]
    dp = depth * 4
    n = layers * CH
    out_shape = [jax.ShapeDtypeStruct((n, dp, 64, 512), BF), jax.ShapeDtypeStruct((32, 2048), F32),
                 jax.ShapeDtypeStruct((rows, 1024), F32)] + [jax.ShapeDtypeStruct(s, t) for s, t in saved]
    scratch = [vm((n, dp, 64, 512), BF), vm((2, depth, 2, 2, 32, 128), F32), vm((32, 2048), F32), vm((rows, 1024), F32), vm((rows, 1024), F32),
               vm((group, group), F32), vm((2, group, 256), F32), vm((2, group, 256), BF)]
    scratch += [vm(s[1:], t) for s, t in saved]
    scratch += [vm((layers, group, 1024), BF), vm((layers, group, 1024), BF), vm((group, fh), BF), vm((group, hw), BF)]
    scratch += [vm((rows, 1024), BF), vm((2 * layers, rows, 1024), BF)]
    dma = pltpu.SemaphoreType.DMA
    scratch += [dma((n, 2 * depth + 1)), dma((n, 2 * depth + 1)), dma((depth + 2,)), dma((depth + 2,)),
                dma((layers, 6)), dma((layers, 6)), dma((4 * layers,)), dma((4 * layers,)), dma((len(KEPT),)), dma((n,)), dma((n, 2))]
    full = pl.BlockSpec(memory_space=pltpu.VMEM)
    hbm = pl.BlockSpec(memory_space=pl.ANY)
    return pl.pallas_call(
        functools.partial(fwd_kernel, depth, layers),
        out_shape=out_shape,
        in_specs=[full] * 6 + [hbm] * 6,
        out_specs=[hbm] * len(out_shape),
        scratch_shapes=scratch,
        compiler_params=pltpu.CompilerParams(collective_id=1, has_side_effects=True, vmem_limit_bytes=63 * 2**20),
        cost_estimate=pl.CostEstimate(flops=14 * 10**9, bytes_accessed=60 * 10**6, transcendentals=0),
    )(gains, shifts, qvb, upb, tok, segr, *weights)


LAG_Y, LAG_Z = 2, 2


class Scatter:
    def __init__(self, place, order, grads, r1, r2, r3, stage, put, send, recv, out_sem):
        self.p, self.order, self.grads, self.r1, self.r2, self.r3 = place, order, grads, r1, r2, r3
        self.stage, self.put, self.send, self.recv, self.out_sem = stage, put, send, recv, out_sem
        self.view = grads.reshape(grads.shape[0], place.depth, 2, 2, *grads.shape[2:])
        self.time = 0
        self.ready = 0
        self.total = len(order)
        self.slots = r1.shape[0]
        self.outs = {}

    def core(self, n):
        p, s, d = self.p, n % self.slots, self.p.depth - 1
        return remote(self.view.at[self.order[n] % CH, :, :, 1 - p.c], self.r1.at[s],
                      self.send.at[n, d + 1], self.recv.at[n, d + 1], p.twin)

    def side(self, n):
        p, s, d = self.p, n % self.slots, self.p.depth - 1
        return remote(self.r1.at[s, :, 1 - p.y], self.r2.at[s], self.send.at[n, d], self.recv.at[n, d], p.side)

    def far(self, n, i):
        p, s = self.p, n % self.slots
        return remote(self.r2.at[s, (p.z + i) % p.depth], self.r3.at[s, i - 1],
                      self.send.at[n, i - 1], self.recv.at[n, i - 1], p.far(i))

    def step_far(self, n):
        p, s = self.p, n % self.slots
        for i in range(1, p.depth):
            self.far(n, i).wait()
        self.side(n).wait_send()
        if n >= 2:
            for copy in self.outs[n - 2]:
                copy.wait()
        total = self.r2[s, p.z].astype(F32)
        for i in range(p.depth - 1):
            total = total + self.r3[s, i].astype(F32)
        self.stage[n % 2] = total
        self.outs[n] = self.put(self.order[n], self.stage.at[n % 2], self.out_sem.at[n % 2])
        for copy in self.outs[n]:
            copy.start()

    def step_side(self, n):
        p, s = self.p, n % self.slots
        self.side(n).wait_recv()
        self.r2[s] = self.r2[s] + self.r1[s, :, p.y]
        for i in range(1, p.depth):
            self.far(n, i).start()

    def step_core(self, n):
        p, s = self.p, n % self.slots
        self.core(n).wait()
        self.r1[s] = self.r1[s] + self.view[self.order[n] % CH, :, :, p.c]
        self.side(n).start()

    def tick(self):
        t, n = self.time, self.total
        far, side = 1 + LAG_Y + LAG_Z, 1 + LAG_Y
        if t >= n + far or (t < n and t >= self.ready):
            return
        if far <= t:
            self.step_far(t - far)
        if side <= t < n + side:
            self.step_side(t - side)
        if 1 <= t < n + 1:
            self.step_core(t - 1)
        if t < n:
            self.core(t).start()
        self.time += 1

    def free(self, n):
        while self.time < n - CH + 2:
            self.tick()

    def finish(self):
        while self.time < self.total + 1 + LAG_Y + LAG_Z:
            self.tick()
        for n in (self.total - 2, self.total - 1):
            for copy in self.outs[n]:
                copy.wait()


def bwd_kernel(depth, layers, vec, cot, segr, wg, xt_i, qkv_i, attt_i, lse_i, mix_i, nt_i, ht_i, gp_i, sec_i, inv_i,
               grad_o, vsum_o, gq_o, gk_o, gv_o, go_o, gu_o, gd_o,
               grads, r1, r2, r3, stage, wqkv, wo, wu, wd,
               xt, qkv, attt, lse, mix, ngt, hidt, gp, sec, inv,
               dpre, fg, ag, rbuf, sbuf, g, dz, dqkv, datt, work, prob, bias, vacc, vx, vc, vy, vz,
               g_send, g_recv, f_send, f_recv, x_send, x_recv, v_send, v_recv, l_sem, o_sem, e_sem):
    p = Place(depth)
    x = p.x
    rows = cot.shape[0]
    group = 2 * rows
    heads_w = datt.shape[-1]
    mine = pl.ds(pl.multiple_of(x * rows, rows), rows)
    theirs = pl.ds(pl.multiple_of((1 - x) * rows, rows), rows)
    p.greet()
    loads = {}

    def load(name, src, dst):
        copy = pltpu.make_async_copy(src, dst, l_sem.at[len(loads)])
        copy.start()
        loads[name] = copy

    def need(*names):
        for name in names:
            loads[name].wait()

    def load_down(l):
        for h in range(4):
            for q in range(2):
                load(("d", l, h, q), wg.at[l * CH + 8 + h, :, :, q * 256:(q + 1) * 256],
                     wd.at[:, q, :, h * 256:(h + 1) * 256])

    def need_down(l):
        need(*[("d", l, h, q) for h in range(4) for q in range(2)])

    def load_out(l):
        for hh in range(2):
            load(("o", l, hh), wg.at[l * CH + 3, :, hh * 32:(hh + 1) * 32, :], wo.at[:, :, hh * 512:(hh + 1) * 512])

    top = layers - 1
    load(("inv", top), inv_i.at[top], inv)
    load(("sec", top), sec_i.at[top], sec)

    def load_first():
        load(("hidt", top), ht_i.at[top], hidt)
        load_down(top)
        load(("gp", top), gp_i.at[top], gp)

    def load_rest():
        load(("wu", top), wg.at[pl.ds(top * CH + 4, 4)], wu)
        load(("ngt", top), nt_i.at[top], ngt)
        load(("mix", top), mix_i.at[top], mix)
        load_out(top)
        load(("attt", top), attt_i.at[top], attt)
        load(("qkv", top), qkv_i.at[top], qkv)
        load(("lse", top), lse_i.at[top], lse)
        load(("wqkv", top), wg.at[pl.ds(top * CH, 3)], wqkv)
        load(("xt", top), xt_i.at[top], xt)

    order = []
    for l in reversed(range(layers)):
        order += [l * CH + k for k in (8, 9, 10, 11, 4, 5, 6, 7, 3, 0, 1, 2)]

    def put(k, src, sem):
        l, k = k // CH, k % CH
        if k < 3:
            pairs = [(src, (gq_o, gk_o, gv_o)[k].at[l])]
        elif k == 3:
            pairs = [(src.at[hh * 32:(hh + 1) * 32], go_o.at[l, :, hh * 512:(hh + 1) * 512]) for hh in range(2)]
        elif k < 8:
            pairs = [(src, gu_o.at[l, :, (k - 4) * 512:(k - 3) * 512])]
        else:
            h = k - 8
            pairs = [(src.at[:, q * 256:(q + 1) * 256], gd_o.at[l, q * 64:(q + 1) * 64, h * 256:(h + 1) * 256])
                     for q in range(2)]
        return [pltpu.make_async_copy(a, b, sem.at[i]) for i, (a, b) in enumerate(pairs)]

    rs = Scatter(p, order, grads, r1, r2, r3, stage, put, g_send, g_recv, o_sem)
    g[...] = cot[...].astype(F32)
    vacc[...] = jnp.zeros_like(vacc)
    mask_bias(segr, bias)

    def give_block(l, side, i):
        r = pl.ds(pl.multiple_of(side * rows + i * (rows // 2), rows // 2), rows // 2)
        n = l * 2 + i
        return remote(ag.at[l, r, :], ag.at[l, r, :], x_send.at[n], x_recv.at[n], p.peer)

    def give_part(l, h, r):
        ref = fg.at[l, r, h * 256:(h + 1) * 256]
        return remote(ref, ref, f_send.at[l, h], f_recv.at[l, h], p.peer)

    def give_cols(l, which, nb):
        cols, i = slice(nb * 256, (nb + 1) * 256), 4 + which * 4 + nb
        return remote(sbuf.at[:, cols], rbuf.at[l * 2 + which, :, cols], f_send.at[l, i], f_recv.at[l, i], p.peer)

    ones = jnp.ones((8, group), BF)
    half_lane = lax.broadcasted_iota(jnp.int32, (1, 128), 1) < HEAD
    first_half = jnp.where(half_lane, 1.0, 0.0).astype(BF)
    second_half = jnp.where(half_lane, 0.0, 1.0).astype(BF)
    scale = HEAD ** -0.5

    def norm_back(hat_ref, inv_ref, extra, gain_row, shift_row, out_row, dest, after=None):
        gain = vec[gain_row:gain_row + 1, 0:1024]

        def some(i, carry):
            sg, ss, so = carry
            r = pl.ds(pl.multiple_of(i * 32, 32), 32)
            hat = hat_ref[r, :]
            up = g[r, :] if extra is None else dz[r, :] + extra[r, :].astype(F32)
            gg = up * gain
            m1 = jnp.mean(gg, axis=-1, keepdims=True)
            m2 = jnp.mean(gg * hat, axis=-1, keepdims=True)
            d = inv_ref[r, 0:1] * (gg - m1 - hat * m2)
            dz[r, :] = d
            dest[pl.ds(pl.multiple_of(x * rows + i * 32, 32), 32), :] = d.astype(BF)
            fold = lambda v: jnp.sum(v.reshape(4, 8, 1024), axis=0)
            return sg + fold(up * hat), ss + fold(up), so + fold(d)
        zero = jnp.zeros((8, 1024), F32)
        sums = (zero, zero, zero)
        for i in range(2):
            sums = lax.fori_loop(i * rows // 64, (i + 1) * rows // 64, some, sums)
            if after is not None:
                after(i)
        sg, ss, so = sums
        vacc[gain_row:gain_row + 1, :] = jnp.sum(sg, axis=0, keepdims=True)
        vacc[shift_row:shift_row + 1, :] = jnp.sum(ss, axis=0, keepdims=True)
        vacc[out_row:out_row + 1, :] = jnp.sum(so, axis=0, keepdims=True)

    def hidden_back(l, r):
        def block(nb, carry):
            cols = pl.ds(pl.multiple_of(nb * 512, 512), 512)
            w = wd[pl.ds(nb * 4, 4)].reshape(512, -1)
            dpre[r, cols] = (nt(fg[l, r, :], w) * gp[r, cols].astype(F32)).astype(BF)
            return carry
        lax.fori_loop(0, 4, block, 0, unroll=2)

    def up_back(r, nb):
        w = [wu[j, nb * 4:(nb + 1) * 4].reshape(256, 512) for j in range(4)]
        return sum(nt(dpre[r, j * 512:(j + 1) * 512], w[j]) for j in range(4))

    def in_back(r, nb):
        w = [wqkv[m, nb * 4:(nb + 1) * 4].reshape(256, 512) for m in range(3)]
        return sum(nt(dqkv[m, r, :], w[m]) for m in range(3))

    def grad_down(h):
        def block(mb, carry):
            r = pl.ds(pl.multiple_of(mb * 512, 512), 512)
            res = nn(hidt[r, :], fg[l, :, h * 256:(h + 1) * 256]).astype(BF).reshape(4, 2, 64, 256)
            for q in range(2):
                grads[8 + h, pl.ds(mb * 4, 4), :, q * 256:(q + 1) * 256] = res[:, q]
            return carry
        lax.fori_loop(0, 4, block, 0)

    def grad_cols(slot, lhs, rhs, mb):
        r = slice(mb * 256, (mb + 1) * 256)
        grads[slot, mb * 4:(mb + 1) * 4] = nn(lhs[r, :], rhs).astype(BF).reshape(4, 64, 512)

    def grad_out():
        for mb in range(2):
            res = nn(attt[mb * 256:(mb + 1) * 256, :], ag[l]).astype(BF).reshape(8, 32, 1024)
            for hh in range(2):
                grads[3, mb * 8:(mb + 1) * 8, hh * 32:(hh + 1) * 32, :] = res[:, :, hh * 512:(hh + 1) * 512]

    def attend_back(first, last):
        def pair(hp, carry):
            lanes = pl.ds(pl.multiple_of(hp * 128, 128), 128)
            q128, k128, v128 = qkv[0, :, lanes], qkv[1, :, lanes], qkv[2, :, lanes]
            o128 = datt[:, lanes]
            k_t = k128.T * scale
            d_k = d_v = None
            d_q = []
            for half in range(2):
                m = second_half if half else first_half
                work[0] = nt(k128 * (m * scale), q128)
                work[1] = nt(v128 * m, o128)
                l_row = lse[pl.ds(hp * 2 + half, 1), :]

                def some(i, dots):
                    r = pl.ds(pl.multiple_of(i * 32, 32), 32)
                    e = jnp.exp(work[0, r, :] + bias[r, :] - l_row)
                    work[0, r, :] = e
                    prob[0, r, :] = e.astype(BF)
                    return dots + jnp.sum((e * work[1, r, :]).reshape(4, 8, group), axis=0)
                dots = lax.fori_loop(0, group // 32, some, jnp.zeros((8, group), F32), unroll=True)
                r_row = jnp.sum(dots, axis=0, keepdims=True)

                def more(i, c):
                    r = pl.ds(pl.multiple_of(i * 32, 32), 32)
                    prob[1, r, :] = (work[0, r, :] * (work[1, r, :] - r_row)).astype(BF)
                    return c
                lax.fori_loop(0, group // 32, more, 0, unroll=True)
                dv_half = nn(prob[0], o128 * m)
                dk_half = nn(prob[1], q128 * m)
                d_v = dv_half if half == 0 else d_v + dv_half
                d_k = dk_half if half == 0 else d_k + dk_half
                d_q.append(nn(k_t[half * HEAD:(half + 1) * HEAD], prob[1]))
            dqkv[0, :, lanes] = jnp.concatenate(d_q, axis=0).T.astype(BF)
            dqkv[1, :, lanes] = (d_k * scale).astype(BF)
            dqkv[2, :, lanes] = d_v.astype(BF)
            return carry
        lax.fori_loop(first, last, pair, 0)

    for l in reversed(range(layers)):
        need(("sec", l), ("inv", l))
        if l == top:
            load_first()
        norm_back(sec, inv.at[1], None, l * 2 + 1, 4 + l * 4 + 3, 4 + l * 4 + 2, fg.at[l])
        if l == top:
            p.met()
        for h in range(4):
            give_part(l, h, mine).start()
        if l > 0:
            load(("sec", l - 1), sec_i.at[l - 1], sec)
        need_down(l)
        need(("gp", l))
        hidden_back(l, mine)
        if l == top:
            load_rest()
        need(("hidt", l))
        for h in range(4):
            give_part(l, h, theirs).wait_recv()
            rs.free(rs.ready)
            grad_down(h)
            rs.ready += 1
            rs.tick()
        if l > 0:
            load(("hidt", l - 1), ht_i.at[l - 1], hidt)
        hidden_back(l, theirs)
        if l > 0:
            load_down(l - 1)
            load(("gp", l - 1), gp_i.at[l - 1], gp)
        need(("wu", l))
        if l < top:
            for nb in range(4):
                give_cols(l + 1, 1, nb).wait_send()
        for nb in range(4):
            sbuf[:, nb * 256:(nb + 1) * 256] = up_back(theirs, nb).astype(BF)
            give_cols(l, 0, nb).start()
        rs.tick()
        for nb in range(4):
            cols = slice(nb * 256, (nb + 1) * 256)
            dz[:, cols] = dz[:, cols] + up_back(mine, nb)
        if l > 0:
            load(("wu", l - 1), wg.at[pl.ds((l - 1) * CH + 4, 4)], wu)
        need(("ngt", l))
        rs.free(rs.ready + 3)
        for j in range(4):
            for mb in range(4):
                grad_cols(4 + j, ngt, dpre[:, j * 512:(j + 1) * 512], mb)
            res = nn(ones, dpre[:, j * 512:(j + 1) * 512])
            row, col = 16 + l * 2 + j // 2, (j % 2) * 512
            vacc[row:row + 1, col:col + 512] = res[0:1]
        if l > 0:
            load(("ngt", l - 1), nt_i.at[l - 1], ngt)
        rs.ready += 4
        rs.tick()
        need(("mix", l))
        for nb in range(4):
            give_cols(l, 0, nb).wait()
        norm_back(mix, inv.at[0], rbuf.at[l * 2], l * 2, 4 + l * 4 + 1, 4 + l * 4, ag.at[l],
                  lambda i: give_block(l, x, i).start())
        if l > 0:
            load(("mix", l - 1), mix_i.at[l - 1], mix)
            load(("inv", l - 1), inv_i.at[l - 1], inv)
        need(("o", l, 0), ("o", l, 1))
        w_o = wo[...].reshape(heads_w, -1)
        datt[mine, :] = nt(ag[l, mine, :], w_o).astype(BF)
        rs.tick()
        for i in range(2):
            give_block(l, 1 - x, i).wait_recv()
        datt[theirs, :] = nt(ag[l, theirs, :], w_o).astype(BF)
        if l > 0:
            load_out(l - 1)
        need(("attt", l))
        rs.free(rs.ready)
        grad_out()
        rs.ready += 1
        if l > 0:
            load(("attt", l - 1), attt_i.at[l - 1], attt)
        need(("qkv", l), ("lse", l))
        attend_back(0, 2)
        rs.tick()
        attend_back(2, 4)
        rs.tick()
        if l > 0:
            load(("qkv", l - 1), qkv_i.at[l - 1], qkv)
            load(("lse", l - 1), lse_i.at[l - 1], lse)
        need(("wqkv", l))
        for nb in range(4):
            sbuf[:, nb * 256:(nb + 1) * 256] = in_back(theirs, nb).astype(BF)
            give_cols(l, 1, nb).start()
        need(("xt", l))
        rs.free(rs.ready + 2)
        for m in range(3):
            for mb in range(4):
                grad_cols(m, xt, dqkv[m], mb)
            if m != 1:
                vacc[20 + l:21 + l, (m // 2) * 512:(m // 2) * 512 + 512] = nn(ones, dqkv[m])[0:1]
        rs.ready += 3
        rs.tick()
        for nb in range(4):
            cols = slice(nb * 256, (nb + 1) * 256)
            g[:, cols] = dz[:, cols] + in_back(mine, nb)
        if l > 0:
            load(("wqkv", l - 1), wg.at[pl.ds((l - 1) * CH, 3)], wqkv)
            load(("xt", l - 1), xt_i.at[l - 1], xt)
        rs.tick()
        for nb in range(4):
            give_cols(l, 1, nb).wait_recv()
        g[...] = g[...] + rbuf[l * 2 + 1].astype(F32)
    end = pltpu.make_async_copy(g, grad_o, e_sem.at[0])
    end.start()
    s_x = remote(vacc.at[0:16], vx, v_send.at[0], v_recv.at[0], p.peer)
    s_x.start()
    rs.tick()
    s_x.wait()
    vacc[0:16] = vacc[0:16] + vx[...]
    s_c = remote(vacc, vc, v_send.at[1], v_recv.at[1], p.twin)
    s_c.start()
    rs.tick()
    s_c.wait()
    vacc[...] = vacc[...] + vc[...]
    s_y = remote(vacc, vy, v_send.at[2], v_recv.at[2], p.side)
    s_y.start()
    rs.tick()
    s_y.wait()
    vacc[...] = vacc[...] + vy[...]
    s_z = [remote(vacc, vz.at[i - 1], v_send.at[2 + i], v_recv.at[2 + i], p.far(i)) for i in range(1, depth)]
    for copy in s_z:
        copy.start()
    rs.tick()
    for copy in s_z:
        copy.wait()
    total = vacc[...]
    for i in range(depth - 1):
        total = total + vz[i]
    vc[...] = total
    last = pltpu.make_async_copy(vc, vsum_o, e_sem.at[1])
    last.start()
    rs.finish()
    for nb in range(4):
        give_cols(0, 1, nb).wait_send()
    for l in range(layers):
        for h in range(4):
            give_part(l, h, mine).wait_send()
        for i in range(2):
            give_block(l, x, i).wait_send()
    end.wait()
    last.wait()


def backward_call(depth, layers, rows, vec, cot, segr, wg, saved):
    group, hw, fh = 2 * rows, 512, 2048
    vm = pltpu.VMEM
    dp = depth * 4
    n = layers * CH
    slots = LAG_Y + LAG_Z + 2
    shapes = [(rows, 1024), (24, 1024), (layers, 64, hw), (layers, 64, hw), (layers, 64, hw), (layers, 32, 1024),
              (layers, 64, fh), (layers, 128, 1024)]
    scratch = [vm((CH, dp, 64, 512), BF), vm((slots, depth, 2, 64, 512), BF), vm((slots, depth, 64, 512), BF),
               vm((slots, depth - 1, 64, 512), BF), vm((2, 64, 512), F32),
               vm((3, dp, 64, 512), BF), vm((dp, 32, 1024), BF), vm((4, dp, 64, 512), BF), vm((dp, 2, 64, 1024), BF)]
    scratch += [vm(s.shape[1:], s.dtype) for s in saved]
    scratch += [vm((group, fh), BF), vm((layers, group, 1024), BF), vm((layers, group, 1024), BF),
                vm((2 * layers, rows, 1024), BF), vm((rows, 1024), BF), vm((rows, 1024), F32), vm((rows, 1024), F32),
                vm((3, group, hw), BF), vm((group, hw), BF), vm((2, group, group), F32), vm((2, group, group), BF),
                vm((group, group), F32), vm((24, 1024), F32), vm((16, 1024), F32),
                vm((24, 1024), F32), vm((24, 1024), F32), vm((depth - 1, 24, 1024), F32)]
    dma = pltpu.SemaphoreType.DMA
    scratch += [dma((n, depth + 1)), dma((n, depth + 1)), dma((layers, 12)), dma((layers, 12)), dma((4 * layers,)), dma((4 * layers,)),
                dma((depth + 2,)), dma((depth + 2,)), dma((24 * layers,)), dma((2, 2)), dma((2,))]
    full = pl.BlockSpec(memory_space=pltpu.VMEM)
    hbm = pl.BlockSpec(memory_space=pl.ANY)
    return pl.pallas_call(
        functools.partial(bwd_kernel, depth, layers),
        out_shape=[jax.ShapeDtypeStruct(s, F32) for s in shapes],
        in_specs=[full] * 3 + [hbm] * (1 + len(saved)),
        out_specs=[hbm] * len(shapes),
        scratch_shapes=scratch,
        compiler_params=pltpu.CompilerParams(collective_id=2, has_side_effects=True, vmem_limit_bytes=63 * 2**20),
        cost_estimate=pl.CostEstimate(flops=28 * 10**9, bytes_accessed=60 * 10**6, transcendentals=0),
    )(vec, cot, segr, wg, *saved)


def finish_kernel(layers, vsum, *refs):
    n = 8
    srcs, dsts, qv, ub, gain, shift = refs[:n], refs[n:2 * n], *refs[2 * n:2 * n + 4]
    bufs, sem = refs[2 * n + 4:3 * n + 4], refs[-1]
    into = [pltpu.make_async_copy(s, b, sem.at[0, i]) for i, (s, b) in enumerate(zip(srcs, bufs))]
    away = [pltpu.make_async_copy(b, d, sem.at[1, i]) for i, (b, d) in enumerate(zip(bufs, dsts))]
    for copy in into:
        copy.start()
    dp, x = lax.axis_index("dp"), lax.axis_index("tensor")

    def part(row, count, block, slot):
        whole = vsum[row:row + count, pl.ds(pl.multiple_of(block * 128, 128), 128)]
        res = jnp.zeros((count, 32), F32)
        for i in range(4):
            res = jnp.where(slot == i, whole[:, i * 32:(i + 1) * 32], res)
        return res
    for l in range(layers):
        gain[l] = part(l * 2, 2, dp // 2, (dp % 2) * 2 + x)
        shift[l] = part(2 * layers + l * 4, 4, dp // 2, (dp % 2) * 2 + x)
        for i in range(2):
            qv[l, i:i + 1, :] = part(20 + l, 1, i * 4 + dp // 4, dp % 4)
        row = jnp.where(dp // 8 == 0, vsum[16 + l * 2:17 + l * 2, :], vsum[17 + l * 2:18 + l * 2, :])
        block = jnp.zeros((1, 128), F32)
        for i in range(8):
            block = jnp.where(dp % 8 == i, row[:, i * 128:(i + 1) * 128], block)
        ub[l:l + 1, :] = block
    for i in range(n):
        into[i].wait()
        away[i].start()
    for copy in away:
        copy.wait()


def finish_call(layers, vsum, *arrays):
    vm = pltpu.VMEM
    full = pl.BlockSpec(memory_space=pltpu.VMEM)
    hbm = pl.BlockSpec(memory_space=pl.ANY)
    small = [(layers, 2, 32), (layers, 128), (layers, 2, 32), (layers, 4, 32)]
    return pl.pallas_call(
        functools.partial(finish_kernel, layers),
        out_shape=[jax.ShapeDtypeStruct(a.shape, F32) for a in arrays] + [jax.ShapeDtypeStruct(s, F32) for s in small],
        in_specs=[full] + [hbm] * len(arrays),
        out_specs=[hbm] * len(arrays) + [full] * 4,
        scratch_shapes=[vm(a.shape, F32) for a in arrays] + [pltpu.SemaphoreType.DMA((2, len(arrays)))],
        compiler_params=pltpu.CompilerParams(vmem_limit_bytes=60 * 2**20),
    )(vsum, *arrays)


def on_device(
    tokens,
    cotangent,
    segment_ids,
    w_query,
    w_key,
    w_value,
    w_out,
    w_up,
    w_down,
    qv_bias,
    up_bias,
    norm_gain,
    shift_bias,
):
    layers = w_query.shape[0]
    rows = tokens.shape[0]
    depth = lax.axis_size("dp") // 4
    segr = segment_ids[None, :]
    wg, vec, out, *saved = forward_call(
        depth, layers, rows, norm_gain, shift_bias, qv_bias, up_bias, tokens, segr,
        w_query, w_key, w_value, w_out, w_up, w_down
    )
    grad, vsum, *grads = backward_call(depth, layers, rows, vec, cotangent, segr, wg, saved)
    return finish_call(layers, vsum, out, grad, *grads)


def on_any_mesh(
    tokens,
    cotangent,
    segment_ids,
    w_query,
    w_key,
    w_value,
    w_out,
    w_up,
    w_down,
    qv_bias,
    up_bias,
    norm_gain,
    shift_bias,
):
    layers = w_query.shape[0]
    group = segment_ids.shape[0]
    seq = min(LEN, group)
    segs = segment_ids.reshape(group // seq, seq)
    stream = tokens.astype(jnp.float32)
    kept_all = []
    mats_all = []
    vecs_all = []
    for layer in range(layers):
        mats = (
            lax.all_gather(w_query[layer], "dp", axis=0, tiled=True),
            lax.all_gather(w_key[layer], "dp", axis=0, tiled=True),
            lax.all_gather(w_value[layer], "dp", axis=0, tiled=True),
            lax.all_gather(w_out[layer], "dp", axis=0, tiled=True),
            lax.all_gather(w_up[layer], "dp", axis=0, tiled=True),
            lax.all_gather(w_down[layer], "dp", axis=0, tiled=True),
            lax.all_gather(qv_bias[layer], "dp", axis=1, tiled=True),
            lax.all_gather(up_bias[layer], "dp", axis=0, tiled=True),
        )
        vecs = (
            lax.all_gather(norm_gain[layer], ("dp", "tensor"), axis=1, tiled=True),
            lax.all_gather(shift_bias[layer], ("dp", "tensor"), axis=1, tiled=True),
        )
        stream, kept = forward_layer(stream, mats, vecs, segs, seq)
        kept_all.append(kept)
        mats_all.append(mats)
        vecs_all.append(vecs)
    grad = cotangent.astype(jnp.float32)
    mat_shards = [None] * layers
    vec_shards = [None] * layers
    for layer in reversed(range(layers)):
        mats = (
            lax.all_gather(w_query[layer], "dp", axis=0, tiled=True),
            lax.all_gather(w_key[layer], "dp", axis=0, tiled=True),
            lax.all_gather(w_value[layer], "dp", axis=0, tiled=True),
            lax.all_gather(w_out[layer], "dp", axis=0, tiled=True),
            lax.all_gather(w_up[layer], "dp", axis=0, tiled=True),
            lax.all_gather(w_down[layer], "dp", axis=0, tiled=True),
            lax.all_gather(qv_bias[layer], "dp", axis=1, tiled=True),
            lax.all_gather(up_bias[layer], "dp", axis=0, tiled=True),
        )
        grad, mat_grads, vec_grads = backward_layer(
            grad, mats, vecs_all[layer], kept_all[layer], segs, seq
        )
        g_q, g_k, g_v, g_o, g_u, g_d, g_qv, g_ub = mat_grads
        mat_shards[layer] = (
            lax.psum_scatter(
                g_q.astype(jnp.bfloat16), "dp", scatter_dimension=0, tiled=True
            ).astype(jnp.float32),
            lax.psum_scatter(
                g_k.astype(jnp.bfloat16), "dp", scatter_dimension=0, tiled=True
            ).astype(jnp.float32),
            lax.psum_scatter(
                g_v.astype(jnp.bfloat16), "dp", scatter_dimension=0, tiled=True
            ).astype(jnp.float32),
            lax.psum_scatter(
                g_o.astype(jnp.bfloat16), "dp", scatter_dimension=0, tiled=True
            ).astype(jnp.float32),
            lax.psum_scatter(
                g_u.astype(jnp.bfloat16), "dp", scatter_dimension=0, tiled=True
            ).astype(jnp.float32),
            lax.psum_scatter(
                g_d.astype(jnp.bfloat16), "dp", scatter_dimension=0, tiled=True
            ).astype(jnp.float32),
            lax.psum_scatter(
                g_qv.astype(jnp.bfloat16), "dp", scatter_dimension=1, tiled=True
            ).astype(jnp.float32),
            lax.psum_scatter(
                g_ub.astype(jnp.bfloat16), "dp", scatter_dimension=0, tiled=True
            ).astype(jnp.float32),
        )
        g_gain, g_shift = vec_grads
        vec_shards[layer] = (
            lax.psum_scatter(g_gain, ("dp", "tensor"), scatter_dimension=1, tiled=True),
            lax.psum_scatter(g_shift, ("dp", "tensor"), scatter_dimension=1, tiled=True),
        )

    def stacked(index, source):
        return jnp.stack([entry[index] for entry in source])

    return (
        stream,
        grad,
        stacked(0, mat_shards),
        stacked(1, mat_shards),
        stacked(2, mat_shards),
        stacked(3, mat_shards),
        stacked(4, mat_shards),
        stacked(5, mat_shards),
        stacked(6, mat_shards),
        stacked(7, mat_shards),
        stacked(0, vec_shards),
        stacked(1, vec_shards),
    )


def solution(mesh):
    in_specs = (
        P(("dp", "tensor"), None),
        P(("dp", "tensor"), None),
        P("dp"),
        P(None, "dp", "tensor"),
        P(None, "dp", "tensor"),
        P(None, "dp", "tensor"),
        P(None, ("tensor", "dp"), None),
        P(None, "dp", "tensor"),
        P(None, ("tensor", "dp"), None),
        P(None, None, ("tensor", "dp")),
        P(None, ("tensor", "dp")),
        P(None, None, ("dp", "tensor")),
        P(None, None, ("dp", "tensor")),
    )
    out_specs = (
        P(("dp", "tensor"), None),
        P(("dp", "tensor"), None),
        P(None, "dp", "tensor"),
        P(None, "dp", "tensor"),
        P(None, "dp", "tensor"),
        P(None, ("tensor", "dp"), None),
        P(None, "dp", "tensor"),
        P(None, ("tensor", "dp"), None),
        P(None, None, ("tensor", "dp")),
        P(None, ("tensor", "dp")),
        P(None, None, ("dp", "tensor")),
        P(None, None, ("dp", "tensor")),
    )
    small = mesh.shape["tensor"] == 2 and mesh.shape["dp"] == 16
    return jax.shard_map(
        on_device if small else on_any_mesh, mesh=mesh, in_specs=in_specs, out_specs=out_specs, check_vma=False
    )
```
